32 devices in a mesh: sub: 32 (over z, y, x, core).
Axes of the slice: x: 2, y: 2, z: 4, core: 2. Of those that a mesh axis runs over, the one named last changes fastest.
Arguments:
- stiffness: float32 [32, 1024, 1024], P('sub'), as said below
- neumann_inv: float32 [32, 1024, 1024], P('sub'), as said below
- coarse_basis: float32 [32, 16, 1024], P('sub'), may hold values from -0.375 to 0.375
- coarse_inv: float32 [512, 512], P('sub'), as said below
- loads: float32 [32, 64, 1024], P('sub'), may hold values from -6 to 6
- face_index: int32 [32, 4, 128], P('sub'), may hold values from 0 to 1023, as said below
- face_len: int32 [32, 4], P('sub'), may hold values from 0 to 128, as said below
Outputs:
- solution: float32 [32, 64, 1024], P('sub')
- residual: float32 [32, 64, 1024], P('sub')
The draws below stay inside these ranges and needn't reach their ends.
Inputs may be any that keep to these rules, and one draw needn't show every extreme that they name: `face_index`: within one subdomain all 512 entries are distinct. `face_len`: A block without a neighbour has length 0; paired blocks of two neighbours have equal length; some block has length 128. `stiffness`: each matrix is exactly symmetric and positive definite. `neumann_inv`: each matrix is exactly symmetric and positive definite. `coarse_inv`: the matrix is exactly symmetric and positive definite.
All inputs are finite; a program needn't handle non-finite values.
Results may differ from the reference program's by a relative error of at most 0.00022.
Values sent between devices are 32-bit elements; how exact they have to be, the bound alone decides.
No kernel may reach another device: no remote copies, remote signals or barrier semaphores. Data moves between devices by JAX's collectives and lax.ppermute only.
A program may use at most 64 MiB of HBM per device.

```python
import jax
import jax.numpy as jnp
from jax import lax

NDOF = 1024
CASES = 64
FACE = 128
CYCLE = 16
PRIMAL = 16
ITERS = 4
SUBS = 32
COARSE = 512


def spd_draw(key, count, order):
    noise = jax.random.normal(key, (count, order, order), jnp.float32)
    sym = (noise + jnp.swapaxes(noise, 1, 2)) / (2.0 * jnp.sqrt(jnp.float32(order)))
    return sym + 2.0 * jnp.eye(order, dtype=jnp.float32)[None]


def draw_stiffness(key, part):
    return spd_draw(jax.random.fold_in(key, 11), SUBS, NDOF)


def draw_neumann_inv(key, part):
    return spd_draw(jax.random.fold_in(key, 12), SUBS, NDOF)


def draw_coarse_inv(key, part):
    return spd_draw(jax.random.fold_in(key, 13), 1, COARSE)[0]


def draw_face_index(key, part):
    keys = jax.random.split(jax.random.fold_in(key, 14), SUBS)
    picks = jax.vmap(lambda one: jax.random.permutation(one, NDOF)[:4 * FACE])(keys)
    return picks.reshape(SUBS, 4, FACE).astype(jnp.int32)


def draw_face_len(key, part):
    key_h = jax.random.fold_in(key, 15)
    key_v = jax.random.fold_in(key, 16)
    across = jax.random.randint(key_h, (SUBS,), FACE // 3, FACE + 1).astype(jnp.int32)
    across = across.at[0].set(FACE)
    along = jax.random.randint(key_v, (SUBS,), FACE // 3, FACE + 1).astype(jnp.int32)
    position = jnp.arange(SUBS, dtype=jnp.int32)
    rowpos = position // CYCLE
    east = jnp.where(position == SUBS - 1, 0, across)
    north = jnp.where(rowpos == SUBS // CYCLE - 1, 0, along)
    west = jnp.roll(east, 1)
    south = jnp.roll(north, CYCLE)
    return jnp.stack([west, east, south, north], axis=1).astype(jnp.int32)


def block_scale(own_key, extent, cuts, smallest, high):
    loudness = 1.0
    for axis_at, blocks in cuts:
        heights = jax.random.uniform(jax.random.fold_in(jax.random.fold_in(own_key, 6), axis_at), (blocks,), jnp.float32, smallest / len(cuts), high / len(cuts))
        loudness = loudness * jnp.repeat(jnp.exp(heights), extent[axis_at] // blocks).reshape((-1,) + (1,) * (len(extent) - 1 - axis_at))
    return loudness


def normal_values(key, dims, scale, most, cuts=(), kind=jnp.bfloat16):
    result = jax.random.normal(key, dims, jnp.float32) * scale
    if len(cuts) > 0:
        result = block_scale(key, dims, cuts, -0.22, 0.18) * result
    return jnp.clip(result, min=-most, max=most).astype(kind)


def setup_inputs(seed: int = 0) -> dict:
    splits = jax.random.split(jax.random.key(seed), 8)
    return {
        "stiffness": draw_stiffness(jax.random.fold_in(splits[7], 71), 0),
        "neumann_inv": draw_neumann_inv(jax.random.fold_in(splits[7], 71), 0),
        "coarse_basis": normal_values(splits[2], (SUBS, PRIMAL, NDOF), (2.0 / NDOF ** 0.5), 0.375, ((0, 32),), jnp.float32),
        "coarse_inv": draw_coarse_inv(jax.random.fold_in(splits[7], 71), 0),
        "loads": normal_values(splits[4], (SUBS, CASES, NDOF), 1.0, 6.0, ((0, 32),), jnp.float32),
        "face_index": draw_face_index(jax.random.fold_in(splits[7], 71), 0),
        "face_len": draw_face_len(jax.random.fold_in(splits[7], 71), 0),
    }


HIGH = lax.Precision.HIGHEST


def assemble(local_vals, face_slots, live_slots):
    face_vals = jax.vmap(lambda loc, slot: jnp.take(loc, slot, axis=1))(local_vals, face_slots)
    face_vals = face_vals * live_slots[:, None, :]
    subs, cases = face_vals.shape[0], face_vals.shape[1]
    blocks = face_vals.reshape(subs, cases, 4, -1)
    west_in = jnp.roll(blocks[:, :, 1], 1, axis=0)
    east_in = jnp.roll(blocks[:, :, 0], -1, axis=0)
    south_in = jnp.roll(blocks[:, :, 3], CYCLE, axis=0)
    north_in = jnp.roll(blocks[:, :, 2], -CYCLE, axis=0)
    incoming = jnp.stack([west_in, east_in, south_in, north_in], axis=2).reshape(subs, cases, -1)
    incoming = incoming * live_slots[:, None, :]
    return jax.vmap(lambda loc, slot, extra: loc.at[:, slot].add(extra))(local_vals, face_slots, incoming)


def reference(stiffness, neumann_inv, coarse_basis, coarse_inv, loads, face_index, face_len):
    subs = stiffness.shape[0]
    width = face_index.shape[2]
    face_slots = face_index.reshape(subs, -1).astype(jnp.int32)
    slot_pos = jnp.arange(width, dtype=jnp.int32)
    live_slots = (slot_pos[None, None, :] < face_len[:, :, None]).astype(jnp.float32).reshape(subs, -1)
    counts = jax.vmap(lambda slot, live: jnp.ones((NDOF,), jnp.float32).at[slot].add(live))(face_slots, live_slots)
    weight = 1.0 / counts

    def inner(left, right):
        return jnp.sum(left * right * weight[:, None, :], axis=(0, 2))

    def apply_op(field):
        return assemble(jnp.einsum("skn,snm->skm", field, stiffness, precision=HIGH), face_slots, live_slots)

    def precond(resid):
        scaled = weight[:, None, :] * resid
        local_sol = jnp.einsum("skn,snm->skm", scaled, neumann_inv, precision=HIGH)
        coarse_res = jnp.einsum("scn,skn->sck", coarse_basis, scaled, precision=HIGH)
        coarse_sol = jnp.dot(coarse_inv, coarse_res.reshape(-1, coarse_res.shape[2]), precision=HIGH)
        coarse_sol = coarse_sol.reshape(coarse_res.shape)
        local_sol = local_sol + jnp.einsum("sck,scn->skn", coarse_sol, coarse_basis, precision=HIGH)
        return assemble(weight[:, None, :] * local_sol, face_slots, live_slots)

    residual = assemble(loads, face_slots, live_slots)
    solution = jnp.zeros_like(residual)
    precond_res = precond(residual)
    direction = precond_res
    rz_now = inner(residual, precond_res)
    for step in range(ITERS):
        image = apply_op(direction)
        alpha = rz_now / inner(direction, image)
        solution = solution + alpha[None, :, None] * direction
        residual = residual - alpha[None, :, None] * image
        if step + 1 < ITERS:
            precond_res = precond(residual)
            rz_next = inner(residual, precond_res)
            direction = precond_res + (rz_next / rz_now)[None, :, None] * direction
            rz_now = rz_next
    return solution, residual
```

```python
import jax
import jax.numpy as jnp
from jax import lax
from jax.sharding import PartitionSpec as P

CYCLE = 16
ITERS = 4

BF = jnp.bfloat16
F32 = jnp.float32


def split(value):
    high = lax.reduce_precision(value, 8, 7)
    return high.astype(BF), (value - high).astype(BF)


def contract(left, right, dims=((1,), (0,))):
    return lax.dot_general(left, right, (dims, ((), ())), preferred_element_type=F32)


def stacked(value):
    high, low = split(value)
    return jnp.concatenate([high, low], axis=0)


def times(value, parts, dims=((1,), (0,))):
    rows = value.shape[0]
    both = stacked(value)
    first = contract(both, parts[0], dims)
    second = contract(both[:rows], parts[1], dims)
    return first[:rows] + first[rows:] + second


def pick(value, onehot, dims=((1,), (0,))):
    rows = value.shape[0]
    both = contract(stacked(value), onehot, dims)
    return both[:rows] + both[rows:]


def swaps(total):
    sets = []
    for by in (1, CYCLE):
        for parity in (0, 1):
            ahead = [i for i in range(total - by) if (i // by) % 2 == parity]
            sets.append((by, parity, [(i, i + by) for i in ahead] + [(i + by, i) for i in ahead]))
    return sets


def local(stiffness, neumann_inv, coarse_basis, coarse_inv, loads, face_index, face_len):
    total = lax.axis_size("sub")
    me = lax.axis_index("sub")
    basis = coarse_basis[0]
    load = loads[0]
    cases, ndof = load.shape
    primal = basis.shape[0]
    width = face_index.shape[2]

    chosen = []
    for at, (by, parity, pairs) in enumerate(swaps(total)):
        if pairs:
            behind, ahead = (0, 1) if by == 1 else (2, 3)
            forward = (me // by) % 2 == parity
            chosen.append((pairs, behind, ahead, forward))
    blocks = len(chosen)
    index = jnp.concatenate([jnp.where(f, face_index[0, a], face_index[0, b]) for _, b, a, f in chosen])
    length = jnp.stack([jnp.where(f, face_len[0, a], face_len[0, b]) for _, b, a, f in chosen])
    slot = jnp.arange(width, dtype=jnp.int32)
    live = (slot[None, :] < length[:, None]).reshape(-1)
    onehot = ((index[:, None] == jnp.arange(ndof, dtype=jnp.int32)[None, :]) & live[:, None]).astype(BF)
    shared = jnp.sum(onehot.astype(F32), axis=0)
    weight = 1.0 / (1.0 + shared)

    def exchange(faces):
        order = [2, 0, 1, 3][:blocks] if blocks > 2 else list(range(blocks))
        got = [None] * blocks
        for at in order:
            piece = faces[:, at * width:(at + 1) * width]
            got[at] = lax.ppermute(piece, "sub", chosen[at][0])
        return jnp.concatenate(got, axis=1)

    def spread(value):
        flat = value.reshape(1, -1)
        got = lax.all_to_all(jnp.broadcast_to(flat, (total, flat.shape[1])), "sub", 0, 0, tiled=True)
        return got.reshape((total,) + value.shape)

    weighted_basis = basis * weight[None, :]
    basis_faces = pick(weighted_basis, onehot, ((1,), (1,)))
    load_faces = pick(load, onehot, ((1,), (1,)))
    coarse_rows = coarse_inv.shape[1]
    reps = -(-coarse_rows // width)
    inv_packed = jnp.concatenate([coarse_inv[:, i * width:(i + 1) * width] for i in range(reps)], axis=0)
    outgoing = jnp.concatenate([load_faces, basis_faces], axis=0)
    packed = []
    for at in range(blocks):
        packed.append(jnp.concatenate([outgoing[:, at * width:(at + 1) * width], inv_packed], axis=0))
    incoming = exchange(jnp.concatenate(packed, axis=1))

    functions = [weighted_basis]
    rows = [coarse_inv]
    for at in range(blocks):
        part = incoming[:, at * width:(at + 1) * width]
        functions.append(pick(part[cases:cases + primal], onehot[at * width:(at + 1) * width]))
        inv_part = part[cases + primal:]
        rows.append(jnp.concatenate([inv_part[i * primal:(i + 1) * primal] for i in range(reps)], axis=1))
    functions = jnp.concatenate(functions, axis=0)
    rows = split(jnp.concatenate(rows, axis=0))

    def widen(matrix, scale):
        high, low = split(matrix)
        if scale is not None:
            factor = (scale[:, None] * scale[None, :]).astype(BF)
            high, low = high * factor, low * factor
        return [
            jnp.concatenate([part, contract(part, onehot, ((1,), (1,))).astype(BF)], axis=1)
            for part in (high, low)
        ]

    inv_wide = widen(neumann_inv[0], weight)
    stiff_wide = widen(stiffness[0], None)
    function_image = times(functions, stiff_wide)
    function_all = jnp.concatenate([functions, function_image], axis=1)
    function_all = split(function_all)

    def dot(left, right):
        return jnp.sum(left * right, axis=1)


    def apply_both(value, coarse, sums):
        lines = coarse if sums is None else jnp.concatenate([coarse, sums], axis=0)
        everyone = spread(lines)
        wide = times(value, inv_wide)
        inside = wide[:, :ndof] + pick(exchange(wide[:, ndof:]), onehot)
        image = times(inside, stiff_wide)
        gathered = everyone[:, :primal].reshape(total * primal, cases)
        factors = times(gathered.T, rows, ((1,), (1,)))
        extra = times(factors, function_all)
        inside = inside + extra[:, :ndof]
        image = image + extra[:, ndof:]
        summed = None if sums is None else jnp.sum(everyone[:, primal:], axis=0)
        return inside, image, summed

    basis_parts = split(weighted_basis)
    basis_face_parts = split(basis_faces)

    def coarse_of(value):
        return times(value, basis_parts, ((1,), (1,))).T

    load_in = incoming[:cases]
    load_in = jnp.concatenate([load_in[:, at * width:(at + 1) * width] for at in range(blocks)], axis=1)
    residual = load + pick(load_in, onehot)
    u, image, _ = apply_both(residual, coarse_of(residual), None)
    gamma = dot(weight[None, :] * residual, u)
    delta = dot(image[:, :ndof], u)
    w = image[:, :ndof] + pick(exchange(image[:, ndof:]), onehot)
    z = q = s = p = None
    solution = None
    alpha_old = gamma_old = None
    for step in range(ITERS):
        sums = jnp.stack([gamma, delta], axis=0)
        last = step + 1 == ITERS
        if last:
            gamma, delta = jnp.sum(spread(sums), axis=0)
        else:
            m, image, summed = apply_both(w, coarse_of(w), sums)
            gamma, delta = summed
        if step == 0:
            alpha = gamma / delta
            p, s = u, w
            solution = alpha[:, None] * p
            if not last:
                q = m
        else:
            beta = gamma / gamma_old
            alpha = gamma / (delta - beta * gamma / alpha_old)
            p = u + beta[:, None] * p
            s = w + beta[:, None] * s
            solution = solution + alpha[:, None] * p
            if not last:
                q = m + beta[:, None] * q
        residual = residual - alpha[:, None] * s
        if not last:
            u = u - alpha[:, None] * q
            gamma_old, alpha_old = gamma, alpha
            gamma = dot(weight[None, :] * residual, u)
            own = image[:, :ndof]
            n = own + pick(exchange(image[:, ndof:]), onehot)
            before = weight[None, :] * w - alpha[:, None] * own
            if step == 0:
                z = n
            else:
                before = before - (alpha * beta)[:, None] * (weight[None, :] * z)
                z = n + beta[:, None] * z
            delta = dot(before, u)
            w = w - alpha[:, None] * z
    return (solution[None], residual[None])


def solution(mesh):
    placed = (
        P("sub", None, None),
        P("sub", None, None),
        P("sub", None, None),
        P("sub", None),
        P("sub", None, None),
        P("sub", None, None),
        P("sub", None),
    )
    return jax.shard_map(
        local,
        mesh=mesh,
        in_specs=placed,
        out_specs=(P("sub", None, None), P("sub", None, None)),
        check_vma=False,
    )
```

```python
import functools

import jax
import jax.numpy as jnp
from jax import lax
from jax.experimental import pallas as pl
from jax.experimental.pallas import tpu as pltpu
from jax.sharding import PartitionSpec as P

CYCLE = 16
ITERS = 4

BF = jnp.bfloat16
F32 = jnp.float32
NN = ((1,), (0,))
NT = ((1,), (1,))
TN = ((0,), (0,))
VMEM_BYTES = 40 * 1024 * 1024


def contract(left, right, dims=NN):
    return lax.dot_general(left, right, (dims, ((), ())), preferred_element_type=F32)


def split(value):
    high = value.astype(BF)
    return high, (value - high.astype(F32)).astype(BF)


def times(value, high, low, dims=NN):
    rows = value.shape[0]
    top, rest = split(value)
    both = contract(jnp.concatenate([top, rest], axis=0), high, dims)
    return both[:rows] + both[rows:] + contract(top, low, dims)


def pick(value, onehot, dims=NN):
    rows = value.shape[0]
    top, rest = split(value)
    last = (value - top.astype(F32) - rest.astype(F32)).astype(BF)
    all_three = contract(jnp.concatenate([top, rest, last], axis=0), onehot, dims)
    return all_three[:rows] + (all_three[rows:2 * rows] + all_three[2 * rows:])


def diagonal(count):
    first = lax.broadcasted_iota(jnp.int32, (count, count), 0)
    return first == lax.broadcasted_iota(jnp.int32, (count, count), 1)


def to_column(row):
    count = row.shape[1]
    return jnp.sum(jnp.where(diagonal(count), jnp.broadcast_to(row, (count, count)), 0.0), axis=1, keepdims=True)


def to_row(column):
    count = column.shape[0]
    return jnp.sum(jnp.where(diagonal(count), jnp.broadcast_to(column, (count, count)), 0.0), axis=0, keepdims=True)


def dot(left, right):
    return jnp.sum(left * right, axis=1, keepdims=True)


def stage(name, function, outs, *args):
    def kernel(*refs):
        values = function(*[ref[...] for ref in refs[:len(args)]])
        for ref, value in zip(refs[len(args):], values):
            ref[...] = value

    whole = pl.BlockSpec(memory_space=pltpu.VMEM)
    return pl.pallas_call(
        kernel,
        name=name,
        out_shape=[jax.ShapeDtypeStruct(shape, kind) for shape, kind in outs],
        in_specs=[whole] * len(args),
        out_specs=[whole] * len(outs),
        compiler_params=pltpu.CompilerParams(vmem_limit_bytes=VMEM_BYTES),
    )(*args)


def prepare(name, matrix, picker, tiles=4):
    order, slots = picker.shape
    rows = order // tiles

    def kernel(matrix_ref, picker_ref, high_ref, low_ref, fhigh_ref, flow_ref, block_high_ref, block_low_ref, total_high, total_low):
        at = pl.program_id(0)
        high, low = split(matrix_ref[...])
        high_ref[...] = high
        low_ref[...] = low
        onehot = picker_ref[...]
        mine = picker_ref[pl.ds(pl.multiple_of(at * rows, rows), rows), :]
        for part, face_ref, total in ((high, fhigh_ref, total_high), (low, flow_ref, total_low)):
            face = contract(part, onehot).astype(BF)
            face_ref[...] = face
            block = contract(mine, face, TN)

            @pl.when(at == 0)
            def _():
                total[...] = block

            @pl.when(at > 0)
            def _():
                total[...] += block

        @pl.when(at == tiles - 1)
        def _():
            block_high_ref[...] = total_high[...].astype(BF)
            block_low_ref[...] = total_low[...].astype(BF)

    shape = jax.ShapeDtypeStruct
    return pl.pallas_call(
        kernel,
        name=name,
        grid=(tiles,),
        in_specs=[
            pl.BlockSpec((rows, order), lambda i: (i, 0)),
            pl.BlockSpec((order, slots), lambda i: (0, 0)),
        ],
        out_specs=[
            pl.BlockSpec((rows, order), lambda i: (i, 0)),
            pl.BlockSpec((rows, order), lambda i: (i, 0)),
            pl.BlockSpec((rows, slots), lambda i: (i, 0)),
            pl.BlockSpec((rows, slots), lambda i: (i, 0)),
            pl.BlockSpec((slots, slots), lambda i: (0, 0)),
            pl.BlockSpec((slots, slots), lambda i: (0, 0)),
        ],
        out_shape=[shape((order, order), BF)] * 2 + [shape((order, slots), BF)] * 2 + [shape((slots, slots), BF)] * 2,
        scratch_shapes=[pltpu.VMEM((slots, slots), F32)] * 2,
        compiler_params=pltpu.CompilerParams(vmem_limit_bytes=VMEM_BYTES),
        cost_estimate=pl.CostEstimate(flops=8 * order * order * slots, bytes_accessed=10 * order * order, transcendentals=0),
    )(matrix, picker)


def swaps(total):
    sets = []
    for by in (1, CYCLE):
        for parity in (0, 1):
            ahead = [i for i in range(total - by) if (i // by) % 2 == parity]
            sets.append((by, parity, [(i, i + by) for i in ahead] + [(i + by, i) for i in ahead]))
    return sets


def local(stiffness, neumann_inv, coarse_basis, coarse_inv, loads, face_index, face_len):
    total = lax.axis_size("sub")
    me = lax.axis_index("sub")
    basis = coarse_basis[0]
    load = loads[0]
    cases, ndof = load.shape
    primal = basis.shape[0]
    width = face_index.shape[2]

    chosen = []
    for by, parity, pairs in swaps(total):
        if pairs:
            behind, ahead = (0, 1) if by == 1 else (2, 3)
            chosen.append((pairs, behind, ahead, (me // by) % 2 == parity))
    blocks = len(chosen)
    slots = blocks * width
    own_rows = (blocks + 1) * primal
    index = jnp.concatenate([jnp.where(f, face_index[0, a], face_index[0, b]) for _, b, a, f in chosen])
    length = jnp.stack([jnp.where(f, face_len[0, a], face_len[0, b]) for _, b, a, f in chosen])
    place = jnp.arange(width, dtype=jnp.int32)
    index = jnp.where(place[None, :] < length[:, None], index.reshape(blocks, width), -1).reshape(1, slots)

    vec = ((cases, ndof), F32)
    face = [((cases, width), F32)] * blocks
    column = ((cases, 1), F32)
    lines = ((primal, cases), F32)

    def cut(value):
        return [value[:, i * width:(i + 1) * width] for i in range(blocks)]

    def exchange(pieces):
        return [lax.ppermute(piece, "sub", chosen[at][0]) for at, piece in enumerate(pieces)]

    def spread(payload):
        return lax.all_to_all(payload, "sub", 0, 0, tiled=True)

    def payload_of(rows):
        return jnp.broadcast_to(rows[None], (total,) + rows.shape)

    reps = coarse_inv.shape[1] // width

    def first(index, load, basis, inv):
        picker = (lax.broadcasted_iota(jnp.int32, (ndof, slots), 0) == index).astype(F32).astype(BF)
        shared = contract(jnp.ones((8, slots), BF), picker, NT)[:1]
        weight = 1.0 / (1.0 + shared)
        weighted = basis * weight
        at_slots = pick(jnp.concatenate([load, weighted], axis=0), picker)
        inv_packed = jnp.concatenate([inv[:, i * width:(i + 1) * width] for i in range(reps)], axis=0)
        out = [jnp.concatenate([part, inv_packed], axis=0) for part in cut(at_slots)]
        return [picker, weight, weighted, at_slots[cases:]] + out

    packed = ((cases + primal + reps * primal, width), F32)
    picker, weight, weighted, basis_slots, *sent = stage(
        "first", first,
        [((ndof, slots), BF), ((1, ndof), F32), ((primal, ndof), F32), ((primal, slots), F32)] + [packed] * blocks,
        index, load, basis, coarse_inv)
    came = exchange(sent)

    inv_parts = prepare("prepare_inv", neumann_inv[0], picker)
    stiff_parts = prepare("prepare_stiff", stiffness[0], picker)

    def reach(weighted, inv, picker, high, low, fhigh, flow, *came):
        functions = [weighted]
        rows = [inv]
        for at, part in enumerate(came):
            functions.append(pick(part[cases:cases + primal], picker[:, at * width:(at + 1) * width], NT))
            rest = part[cases + primal:]
            rows.append(jnp.concatenate([rest[i * primal:(i + 1) * primal] for i in range(reps)], axis=1))
        functions = jnp.concatenate(functions, axis=0)
        rows = jnp.concatenate(rows, axis=0)
        image = times(functions, high, low)
        everything = jnp.concatenate([functions, image, times(functions, fhigh, flow)], axis=1)
        return [*split(rows), *split(everything)]

    wide = 2 * ndof + slots
    coarse = stage(
        "reach", reach,
        [((own_rows, total * primal), BF)] * 2 + [((own_rows, wide), BF)] * 2,
        weighted, coarse_inv, picker, *stiff_parts[:4], *came)

    def solve_own(part, weight, weighted, high, low, fhigh, flow):
        scaled = part * weight
        top, rest = split(scaled)
        return [times(scaled, high, low), times(scaled, fhigh, flow), times(weighted, *split(part), NT)]

    solve_outs = [vec, ((cases, slots), F32), lines]

    def solve_rest(scale, inner, inner_faces, lines, sums, weight, basis_slots, fhigh, flow, block_high, block_low, *came):
        came = scale * jnp.concatenate(came, axis=1)
        lines = lines + times(basis_slots, *split(came), NT)
        came = 0.5 * came
        inner = weight * (inner + times(came, fhigh, flow, NT))
        inner_faces = 0.5 * (inner_faces + times(came, block_high, block_low))
        return [payload_of(jnp.concatenate([lines, sums], axis=0)), inner] + cut(inner_faces)

    rest_outs = [((total, primal + 2, cases), F32), vec] + face

    def apply_own(inner, high, low, fhigh, flow):
        return [times(inner, high, low), times(inner, fhigh, flow)]

    def apply_rest(inner, image, image_faces, picker, fhigh, flow, block_high, block_low, *came):
        came = jnp.concatenate(came, axis=1)
        inner = inner + pick(came, picker, NT)
        image = image + times(came, fhigh, flow, NT)
        image_faces = image_faces + times(came, block_high, block_low)
        return [inner, image, image_faces]

    def correct(everyone, inner, image, image_faces, rows_high, rows_low, all_high, all_low):
        gathered = everyone[:, :primal].reshape(total * primal, cases)
        top, rest = split(gathered)
        factors = contract(rows_high, top) + contract(rows_high, rest) + contract(rows_low, top)
        extra = times(factors.T, all_high, all_low)
        sums = jnp.sum(everyone[:, primal:], axis=0)
        return [
            inner + extra[:, :ndof],
            image + extra[:, ndof:2 * ndof],
            to_column(sums[:1]), to_column(sums[1:2]),
        ] + cut(image_faces + extra[:, 2 * ndof:])

    def precondition(part, scale, sums, exchanged):
        inner, inner_faces, lines = stage("solve_own", solve_own, solve_outs, part, weight, weighted, *inv_parts[:4])
        payload, inner, *sent = stage(
            "solve_rest", solve_rest, rest_outs,
            scale, inner, inner_faces, lines, sums, weight, basis_slots, *inv_parts[2:], *exchanged)
        everyone = spread(payload)
        came = exchange(sent)
        image, image_faces = stage("apply_own", apply_own, [vec, ((cases, slots), F32)], inner, *stiff_parts[:4])
        inner, image, image_faces = stage(
            "apply_rest", apply_rest, [vec, vec, ((cases, slots), F32)],
            inner, image, image_faces, picker, *stiff_parts[2:], *came)
        inner, image, gamma, delta, *sent = stage(
            "correct", correct, [vec, vec, column, column] + face, everyone, inner, image, image_faces, *coarse)
        return inner, image, gamma, delta, sent

    def scatter(picker, *came):
        return pick(jnp.concatenate(came, axis=1), picker, NT)

    one = jnp.ones((cases, 1), F32)
    load_in = [part[:cases] for part in came]
    none = jnp.zeros((2, cases), F32)
    u, image, _, _, sent = precondition(load, one, none, load_in)
    came = exchange(sent)

    def begin(load, u, image, weight, picker, *load_in):
        residual = load + scatter(picker, *load_in)
        gamma = dot(residual * weight, u)
        delta = dot(image, u)
        return [residual, jnp.concatenate([to_row(gamma), to_row(delta)], axis=0)]

    pair = ((2, cases), F32)
    residual, sums = stage("begin", begin, [vec, pair], load, u, image, weight, picker, *load_in)
    part, scale = image, one
    w_from = (part, scale, came)
    state = None

    def assembled(part, scale, picker, *came):
        return [part + scale * scatter(picker, *came)]

    for step in range(ITERS - 1):
        m, image, gamma, delta, sent = precondition(part, scale, sums, came)
        (w,) = stage("assembled", assembled, [vec], part, scale, picker, *came)
        if step > 0:
            (z,) = stage("assembled", assembled, [vec], z_part, one, picker, *came)
        came_next = exchange(sent)
        if step == 0:
            def update(gamma, delta, u, w, m, image, residual, weight):
                alpha = gamma / delta
                q, s, p = m, w, u
                x = alpha * p
                residual = residual - alpha * s
                u = u - alpha * q
                part = w - alpha * image
                sums = jnp.concatenate([to_row(dot(weight * residual, u)), to_row(dot(weight * w - alpha * image, u))], axis=0)
                return [alpha, -alpha, q, s, p, x, residual, u, image, part, sums]

            alpha, scale, q, s, p, x, residual, u, z_part, part, sums = stage(
                "update", update, [column] * 2 + [vec] * 8 + [pair], gamma, delta, u, w, m, image, residual, weight)
        else:
            def update(gamma, delta, gamma_old, alpha_old, u, w, m, image, residual, x, p, s, q, z, weight):
                beta = gamma / gamma_old
                alpha = gamma / (delta - beta * gamma / alpha_old)
                q = m + beta * q
                s = w + beta * s
                p = u + beta * p
                x = x + alpha * p
                residual = residual - alpha * s
                u = u - alpha * q
                before = w - (alpha * beta) * z
                part = before - alpha * image
                sums = jnp.concatenate([to_row(dot(weight * residual, u)), to_row(dot(weight * before - alpha * image, u))], axis=0)
                return [alpha, -alpha, q, s, p, x, residual, u, image + beta * z, part, sums]

            alpha, scale, q, s, p, x, residual, u, z_part, part, sums = stage(
                "update", update, [column] * 2 + [vec] * 8 + [pair],
                gamma, delta, gamma_old, alpha_old, u, w, m, image, residual, x, p, s, q, z, weight)
        gamma_old, alpha_old = gamma, alpha
        came = came_next

    everyone = spread(payload_of(sums))

    def finish(everyone, gamma_old, alpha_old, part, scale, u, residual, x, p, s, picker, *came):
        w = part + scale * scatter(picker, *came)
        sums = jnp.sum(everyone, axis=0)
        gamma, delta = to_column(sums[:1]), to_column(sums[1:2])
        beta = gamma / gamma_old
        alpha = gamma / (delta - beta * gamma / alpha_old)
        return [x + alpha * (u + beta * p), residual - alpha * (w + beta * s)]

    x, residual = stage(
        "finish", finish, [vec, vec],
        everyone, gamma_old, alpha_old, part, scale, u, residual, x, p, s, picker, *came)
    return (x[None], residual[None])


def solution(mesh):
    placed = (
        P("sub", None, None),
        P("sub", None, None),
        P("sub", None, None),
        P("sub", None),
        P("sub", None, None),
        P("sub", None, None),
        P("sub", None),
    )
    return jax.shard_map(
        local,
        mesh=mesh,
        in_specs=placed,
        out_specs=(P("sub", None, None), P("sub", None, None)),
        check_vma=False,
    )
```

```python
import functools

import jax
import jax.numpy as jnp
from jax import lax
from jax.experimental import pallas as pl
from jax.experimental.pallas import tpu as pltpu
from jax.sharding import PartitionSpec as P

CYCLE = 16
ITERS = 4

BF = jnp.bfloat16
F32 = jnp.float32
NN = ((1,), (0,))
NT = ((1,), (1,))
TN = ((0,), (0,))
STAGE_BYTES = 8 * 1024 * 1024
PREPARE_BYTES = 16 * 1024 * 1024


def contract(left, right, dims=NN):
    return lax.dot_general(left, right, (dims, ((), ())), preferred_element_type=F32)


def split(value):
    high = value.astype(BF)
    return high, (value - high.astype(F32)).astype(BF)


def times(value, high, low, dims=NN):
    rows = value.shape[0]
    top, rest = split(value)
    both = contract(jnp.concatenate([top, rest], axis=0), high, dims)
    return both[:rows] + both[rows:] + contract(top, low, dims)


def pick(value, onehot, dims=NN):
    rows = value.shape[0]
    top, rest = split(value)
    last = (value - top.astype(F32) - rest.astype(F32)).astype(BF)
    all_three = contract(jnp.concatenate([top, rest, last], axis=0), onehot, dims)
    return all_three[:rows] + (all_three[rows:2 * rows] + all_three[2 * rows:])


def diagonal(count):
    first = lax.broadcasted_iota(jnp.int32, (count, count), 0)
    return first == lax.broadcasted_iota(jnp.int32, (count, count), 1)


def to_column(row):
    count = row.shape[1]
    return jnp.sum(jnp.where(diagonal(count), jnp.broadcast_to(row, (count, count)), 0.0), axis=1, keepdims=True)


def to_row(column):
    count = column.shape[0]
    return jnp.sum(jnp.where(diagonal(count), jnp.broadcast_to(column, (count, count)), 0.0), axis=0, keepdims=True)


def dot(left, right):
    return jnp.sum(left * right, axis=1, keepdims=True)


def stage(name, function, outs, *args, scalars=0):
    def kernel(*refs):
        values = function(*refs[:scalars], *[ref[...] for ref in refs[scalars:len(args)]])
        for ref, value in zip(refs[len(args):], values):
            ref[...] = value

    whole = pl.BlockSpec(memory_space=pltpu.VMEM)
    return pl.pallas_call(
        kernel,
        name=name,
        out_shape=[jax.ShapeDtypeStruct(shape, kind) for shape, kind in outs],
        in_specs=[pl.BlockSpec(memory_space=pltpu.SMEM)] * scalars + [whole] * (len(args) - scalars),
        out_specs=[whole] * len(outs),
        compiler_params=pltpu.CompilerParams(vmem_limit_bytes=STAGE_BYTES),
    )(*args)


def prepare(name, matrix, picker, unpicker, tiles=4):
    slots, order = picker.shape
    columns = order // tiles

    def kernel(matrix_ref, picker_ref, unpicker_ref, high_ref, low_ref, fhigh_ref, flow_ref, block_high_ref, block_low_ref, total_high, total_low):
        at = pl.program_id(0)
        high, low = split(matrix_ref[0])
        high_ref[...] = high
        low_ref[...] = low
        onehot = picker_ref[...]
        mine = unpicker_ref[...]
        for part, face_ref, total in ((high, fhigh_ref, total_high), (low, flow_ref, total_low)):
            face = contract(onehot, part).astype(BF)
            face_ref[...] = face
            block = contract(face, mine)

            @pl.when(at == 0)
            def _():
                total[...] = block

            @pl.when(at > 0)
            def _():
                total[...] += block

        @pl.when(at == tiles - 1)
        def _():
            block_high_ref[...] = total_high[...].astype(BF)
            block_low_ref[...] = total_low[...].astype(BF)

    shape = jax.ShapeDtypeStruct
    return pl.pallas_call(
        kernel,
        name=name,
        grid=(tiles,),
        in_specs=[
            pl.BlockSpec((1, order, columns), lambda i: (0, 0, i)),
            pl.BlockSpec((slots, order), lambda i: (0, 0)),
            pl.BlockSpec((columns, slots), lambda i: (i, 0)),
        ],
        out_specs=[
            pl.BlockSpec((order, columns), lambda i: (0, i)),
            pl.BlockSpec((order, columns), lambda i: (0, i)),
            pl.BlockSpec((slots, columns), lambda i: (0, i)),
            pl.BlockSpec((slots, columns), lambda i: (0, i)),
            pl.BlockSpec((slots, slots), lambda i: (0, 0)),
            pl.BlockSpec((slots, slots), lambda i: (0, 0)),
        ],
        out_shape=[shape((order, order), BF)] * 2 + [shape((slots, order), BF)] * 2 + [shape((slots, slots), BF)] * 2,
        scratch_shapes=[pltpu.VMEM((slots, slots), F32)] * 2,
        compiler_params=pltpu.CompilerParams(vmem_limit_bytes=PREPARE_BYTES),
        cost_estimate=pl.CostEstimate(flops=8 * order * order * slots, bytes_accessed=10 * order * order, transcendentals=0),
    )(matrix, picker, unpicker)


def swaps(total):
    sets = []
    for by in (1, CYCLE):
        for parity in (0, 1):
            ahead = [i for i in range(total - by) if (i // by) % 2 == parity]
            sets.append((by, parity, [(i, i + by) for i in ahead] + [(i + by, i) for i in ahead]))
    return sets


def local(stiffness, neumann_inv, coarse_basis, coarse_inv, loads, face_index, face_len):
    total = lax.axis_size("sub")
    load = loads[0]
    cases, ndof = load.shape
    primal = coarse_basis.shape[1]
    width = face_index.shape[2]

    chosen = []
    for by, parity, pairs in swaps(total):
        if pairs:
            behind, ahead = (0, 1) if by == 1 else (2, 3)
            chosen.append((pairs, behind, ahead, by, parity))
    blocks = len(chosen)
    slots = blocks * width
    own_rows = (blocks + 1) * primal
    vec = ((cases, ndof), F32)
    face = [((cases, width), F32)] * blocks
    column = ((cases, 1), F32)
    lines = ((primal, cases), F32)

    def cut(value):
        return [value[:, i * width:(i + 1) * width] for i in range(blocks)]

    def exchange(pieces):
        return [lax.ppermute(piece, "sub", chosen[at][0]) for at, piece in enumerate(pieces)]

    def spread(payload):
        return lax.all_to_all(payload, "sub", 0, 0, tiled=True)

    half = primal // 2

    def payload_of(lines, sums):
        pieces = []
        if lines is not None:
            pairs = jnp.concatenate([lines[:half], lines[half:]], axis=1)
            pieces = [pairs[i:i + 1] for i in range(half)]
        row = jnp.concatenate(pieces + [sums], axis=1)
        return jnp.broadcast_to(row, (total, row.shape[1]))

    def both_sums(everyone):
        row = jnp.sum(everyone[:, -2 * cases:], axis=0, keepdims=True)
        return to_column(row[:, :cases]), to_column(row[:, cases:])

    reps = coarse_inv.shape[1] // width

    def first(lengths, index, load, basis, inv):
        me = lax.axis_index("sub")
        load, basis = load[0], basis[0]
        rows = []
        lane = lax.broadcasted_iota(jnp.int32, (1, width), 1)
        for _, behind, ahead, by, parity in chosen:
            forward = (me // by) % 2 == parity
            row = jnp.where(forward, index[0, ahead:ahead + 1], index[0, behind:behind + 1])
            length = jnp.where(forward, lengths[0, ahead], lengths[0, behind])
            rows.append(jnp.where(lane < length, row, -1))
        row = jnp.concatenate(rows, axis=1)
        unpicker = (lax.broadcasted_iota(jnp.int32, (ndof, slots), 0) == row).astype(F32).astype(BF)
        spot = jnp.sum(jnp.where(diagonal(slots), jnp.broadcast_to(row, (slots, slots)), 0), axis=1, keepdims=True)
        picker = (lax.broadcasted_iota(jnp.int32, (slots, ndof), 1) == spot).astype(F32)
        weight = 1.0 / (1.0 + jnp.sum(picker, axis=0, keepdims=True))
        weighted = basis * weight
        at_slots = pick(jnp.concatenate([load, weighted], axis=0), unpicker)
        inv_packed = jnp.concatenate([inv[:, i * width:(i + 1) * width] for i in range(reps)], axis=0)
        out = [jnp.concatenate([part, inv_packed], axis=0) for part in cut(at_slots)]
        return [picker.astype(BF), unpicker, weight, weighted, at_slots[cases:]] + out

    packed = ((cases + primal + reps * primal, width), F32)
    picker, unpicker, weight, weighted, basis_slots, *sent = stage(
        "first", first,
        [((slots, ndof), BF), ((ndof, slots), BF), ((1, ndof), F32), ((primal, ndof), F32), ((primal, slots), F32)] + [packed] * blocks,
        face_len, face_index, loads, coarse_basis, coarse_inv, scalars=1)
    came = exchange(sent)

    inv_parts = prepare("prepare_inv", neumann_inv, picker, unpicker)
    stiff_parts = prepare("prepare_stiff", stiffness, picker, unpicker)

    def reach(weighted, inv, picker, high, low, fhigh, flow, *came):
        functions = [weighted]
        rows = [inv]
        for at, part in enumerate(came):
            functions.append(pick(part[cases:cases + primal], picker[at * width:(at + 1) * width]))
            rest = part[cases + primal:]
            rows.append(jnp.concatenate([rest[i * primal:(i + 1) * primal] for i in range(reps)], axis=1))
        functions = jnp.concatenate(functions, axis=0)
        rows = jnp.concatenate(rows, axis=0)
        image = times(functions, high, low)
        everything = jnp.concatenate([functions, image, times(functions, fhigh, flow, NT)], axis=1)
        return [rows, *split(everything)]

    wide = 2 * ndof + slots
    rows, *function_parts = stage(
        "reach", reach,
        [((own_rows, total * primal), F32)] + [((own_rows, wide), BF)] * 2,
        weighted, coarse_inv, picker, *stiff_parts[:4], *came)
    rows = jnp.transpose(rows.reshape(own_rows, total, 2, half), (2, 0, 3, 1)).reshape(2 * own_rows, half * total)

    def solve_own(part, weight, weighted, high, low, fhigh, flow):
        scaled = part * weight
        return [times(scaled, high, low), times(scaled, fhigh, flow, NT), times(weighted, *split(part), NT)]

    solve_outs = [vec, ((cases, slots), F32), lines]

    def solve_rest(scale, inner, inner_faces, lines, sums, weight, basis_slots, fhigh, flow, block_high, block_low, *came):
        came = scale * jnp.concatenate(came, axis=1)
        lines = lines + times(basis_slots, *split(came), NT)
        came = 0.5 * came
        inner = weight * (inner + times(came, fhigh, flow))
        inner_faces = 0.5 * (inner_faces + times(came, block_high, block_low))
        return [payload_of(lines, sums), inner] + cut(inner_faces)

    rest_outs = [((total, (primal + 2) * cases), F32), vec] + face

    def apply_own(inner, high, low, fhigh, flow):
        return [times(inner, high, low), times(inner, fhigh, flow, NT)]

    def apply_rest(inner, image, image_faces, picker, fhigh, flow, block_high, block_low, *came):
        came = jnp.concatenate(came, axis=1)
        inner = inner + pick(came, picker)
        image = image + times(came, fhigh, flow)
        image_faces = image_faces + times(came, block_high, block_low)
        return [inner, image, image_faces]

    def correct(everyone, inner, image, image_faces, rows, high, low):
        gathered = jnp.concatenate([everyone[:, i * 2 * cases:(i + 1) * 2 * cases] for i in range(half)], axis=0)
        product = times(rows, *split(gathered))
        factors = (product[:own_rows, :cases] + product[own_rows:, cases:]).T
        extra = times(factors, high, low)
        return [
            inner + extra[:, :ndof],
            image + extra[:, ndof:2 * ndof],
            *both_sums(everyone),
        ] + cut(image_faces + extra[:, 2 * ndof:])

    def precondition(part, scale, sums, exchanged):
        inner, inner_faces, lines = stage("solve_own", solve_own, solve_outs, part, weight, weighted, *inv_parts[:4])
        payload, inner, *sent = stage(
            "solve_rest", solve_rest, rest_outs,
            scale, inner, inner_faces, lines, sums, weight, basis_slots, *inv_parts[2:], *exchanged)
        everyone = spread(payload)
        came = exchange(sent)
        image, image_faces = stage("apply_own", apply_own, [vec, ((cases, slots), F32)], inner, *stiff_parts[:4])
        inner, image, image_faces = stage(
            "apply_rest", apply_rest, [vec, vec, ((cases, slots), F32)],
            inner, image, image_faces, picker, *stiff_parts[2:], *came)
        inner, image, gamma, delta, *sent = stage(
            "correct", correct, [vec, vec, column, column] + face, everyone, inner, image, image_faces, rows, *function_parts)
        return inner, image, gamma, delta, sent

    def scatter(picker, *came):
        return pick(jnp.concatenate(came, axis=1), picker)

    one = jnp.ones((cases, 1), F32)
    load_in = [part[:cases] for part in came]
    none = jnp.zeros((1, 2 * cases), F32)
    u, image, _, _, sent = precondition(load, one, none, load_in)
    came = exchange(sent)

    def begin(load, u, image, weight, picker, *load_in):
        residual = load + scatter(picker, *load_in)
        gamma = dot(residual * weight, u)
        delta = dot(image, u)
        return [residual, jnp.concatenate([to_row(gamma), to_row(delta)], axis=1)]

    pair = ((1, 2 * cases), F32)
    residual, sums = stage("begin", begin, [vec, pair], load, u, image, weight, picker, *load_in)
    part, scale = image, one

    def assembled(part, scale, picker, *came):
        return [part + scale * scatter(picker, *came)]

    for step in range(ITERS - 1):
        m, image, gamma, delta, sent = precondition(part, scale, sums, came)
        (w,) = stage("assembled", assembled, [vec], part, scale, picker, *came)
        if step > 0:
            (z,) = stage("assembled", assembled, [vec], z_part, one, picker, *came)
        came_next = exchange(sent)
        if step == 0:
            def update(gamma, delta, u, w, m, image, residual, weight):
                alpha = gamma / delta
                q, s, p = m, w, u
                x = alpha * p
                residual = residual - alpha * s
                u = u - alpha * q
                part = w - alpha * image
                sums = jnp.concatenate([to_row(dot(weight * residual, u)), to_row(dot(weight * w - alpha * image, u))], axis=1)
                return [alpha, -alpha, q, s, p, x, residual, u, image, part, sums]

            alpha, scale, q, s, p, x, residual, u, z_part, part, sums = stage(
                "update", update, [column] * 2 + [vec] * 8 + [pair], gamma, delta, u, w, m, image, residual, weight)
        else:
            def update(gamma, delta, gamma_old, alpha_old, u, w, m, image, residual, x, p, s, q, z, weight):
                beta = gamma / gamma_old
                alpha = gamma / (delta - beta * gamma / alpha_old)
                q = m + beta * q
                s = w + beta * s
                p = u + beta * p
                x = x + alpha * p
                residual = residual - alpha * s
                u = u - alpha * q
                before = w - (alpha * beta) * z
                part = before - alpha * image
                sums = jnp.concatenate([to_row(dot(weight * residual, u)), to_row(dot(weight * before - alpha * image, u))], axis=1)
                return [alpha, -alpha, q, s, p, x, residual, u, image + beta * z, part, sums]

            alpha, scale, q, s, p, x, residual, u, z_part, part, sums = stage(
                "update", update, [column] * 2 + [vec] * 8 + [pair],
                gamma, delta, gamma_old, alpha_old, u, w, m, image, residual, x, p, s, q, z, weight)
        gamma_old, alpha_old = gamma, alpha
        came = came_next

    everyone = spread(jnp.broadcast_to(sums, (total, 2 * cases)))

    def finish(everyone, gamma_old, alpha_old, part, scale, u, residual, x, p, s, picker, *came):
        w = part + scale * scatter(picker, *came)
        gamma, delta = both_sums(everyone)
        beta = gamma / gamma_old
        alpha = gamma / (delta - beta * gamma / alpha_old)
        return [x + alpha * (u + beta * p), residual - alpha * (w + beta * s)]

    x, residual = stage(
        "finish", finish, [vec, vec],
        everyone, gamma_old, alpha_old, part, scale, u, residual, x, p, s, picker, *came)
    return (x[None], residual[None])


def solution(mesh):
    placed = (
        P("sub", None, None),
        P("sub", None, None),
        P("sub", None, None),
        P("sub", None),
        P("sub", None, None),
        P("sub", None, None),
        P("sub", None),
    )
    return jax.shard_map(
        local,
        mesh=mesh,
        in_specs=placed,
        out_specs=(P("sub", None, None), P("sub", None, None)),
        check_vma=False,
    )
```

```python
from types import SimpleNamespace

import jax
import jax.numpy as jnp
import numpy as np
from jax import lax
from jax.experimental import pallas as pl
from jax.experimental.pallas import tpu as pltpu
from jax.sharding import PartitionSpec as P

CYCLE = 16
ITERS = 4

BF = jnp.bfloat16
F32 = jnp.float32
NN = ((1,), (0,))
NT = ((1,), (1,))
STAGE_BYTES = 12 * 1024 * 1024
TILES = 8
AXIS = "sub"


def contract(left, right, dims=NN):
    return lax.dot_general(left, right, (dims, ((), ())), preferred_element_type=F32)


def split(value):
    high = value.astype(BF)
    return high, (value - high.astype(F32)).astype(BF)


def times(value, high, low, dims=NN):
    rows = value.shape[0]
    top, rest = split(value)
    both = contract(jnp.concatenate([top, rest], axis=0), high, dims)
    return both[:rows] + both[rows:] + contract(top, low, dims)


def pick(value, onehot, dims=NN):
    rows = value.shape[0]
    top, rest = split(value)
    last = (value - top.astype(F32) - rest.astype(F32)).astype(BF)
    parts = contract(jnp.concatenate([top, rest, last], axis=0), onehot, dims)
    return parts[:rows] + (parts[rows:2 * rows] + parts[2 * rows:])


def diagonal(count):
    first = lax.broadcasted_iota(jnp.int32, (count, count), 0)
    return first == lax.broadcasted_iota(jnp.int32, (count, count), 1)


def to_column(row):
    count = row.shape[1]
    return jnp.sum(jnp.where(diagonal(count), jnp.broadcast_to(row, (count, count)), 0), axis=1, keepdims=True)


def to_row(column):
    count = column.shape[0]
    return jnp.sum(jnp.where(diagonal(count), jnp.broadcast_to(column, (count, count)), 0), axis=0, keepdims=True)


def dot(left, right):
    return jnp.sum(left * right, axis=1, keepdims=True)


def flat(tree):
    names = [(name, len(held) if isinstance(held, list) else 0) for name, held in tree.items()]
    entries = []
    for held in tree.values():
        entries += held if isinstance(held, list) else [held]
    return names, entries


def named(names, entries):
    space, at = SimpleNamespace(), 0
    for name, count in names:
        setattr(space, name, list(entries[at:at + count]) if count else entries[at])
        at += max(count, 1)
    return space


def stage(name, body, ins, outs):
    in_names, arrays = flat(ins)
    out_names, kinds = flat(outs)

    def kernel(*refs):
        body(named(in_names, refs[:len(arrays)]), named(out_names, refs[len(arrays):]))

    whole = pl.BlockSpec(memory_space=pltpu.VMEM)
    made = pl.pallas_call(
        kernel,
        name=name,
        out_shape=[jax.ShapeDtypeStruct(*kind) for kind in kinds],
        in_specs=[whole] * len(arrays),
        out_specs=[whole] * len(kinds),
        compiler_params=pltpu.CompilerParams(vmem_limit_bytes=STAGE_BYTES),
    )(*arrays)
    return named(out_names, made)


def swaps(total):
    sets = []
    for by in (1, CYCLE):
        for parity in (0, 1):
            ahead = [i for i in range(total - by) if (i // by) % 2 == parity]
            sets.append((by, parity, [(i, i + by) for i in ahead] + [(i + by, i) for i in ahead]))
    return sets


def rounds_of(total):
    bits = total.bit_length() - 1
    assert total == 1 << bits
    rounds = []
    while bits:
        take = 1 if bits % 2 else 2
        low = 1 << (bits - take)
        rounds.append([low * i for i in range(1, 1 << take)])
        bits -= take
    places = [0]
    for distances in rounds:
        places = [place ^ far for far in [0] + distances for place in places]
    return rounds, places


def local(stiffness, neumann_inv, coarse_basis, coarse_inv, loads, face_index, face_len):
    total = lax.axis_size(AXIS)
    _, cases, ndof = loads.shape
    primal = coarse_basis.shape[1]
    width = face_index.shape[2]
    known = coarse_inv.shape[1]
    half = primal // 2
    lines_a_block = half + 1
    reps = known // width
    rounds, places = rounds_of(total)

    chosen = []
    for by, parity, pairs in swaps(total):
        if pairs:
            behind, ahead = (0, 1) if by == 1 else (2, 3)
            chosen.append((pairs, behind, ahead, by, parity))
    blocks = len(chosen)
    slots = blocks * width
    own_rows = (blocks + 1) * primal

    vec = ((cases, ndof), F32)
    faces = ((cases, slots), F32)
    pair = ((1, 2 * cases), F32)
    block_kind = ((lines_a_block, 2 * cases), F32)
    face_kinds = [((cases, width), F32)] * blocks
    blocked = [slice(i * width, (i + 1) * width) for i in range(blocks)]
    strips = [slice(i * ndof // TILES, (i + 1) * ndof // TILES) for i in range(TILES)]

    def joined(refs, rows=slice(None)):
        return jnp.concatenate([ref[rows] for ref in refs], axis=1)

    def put_faces(refs, value):
        for i, ref in enumerate(refs):
            ref[...] = value[:, blocked[i]]

    def exchange(arrays):
        return [lax.ppermute(array, AXIS, chosen[i][0]) for i, array in enumerate(arrays)]

    def gather(block):
        for at, distances in enumerate(rounds):
            pieces = [block] + [lax.ppermute(block, AXIS, [(i, i ^ far) for i in range(total)]) for far in distances]
            if at + 1 == len(rounds):
                return pieces

            def join(i, o):
                o.block[...] = jnp.concatenate([ref[...] for ref in i.pieces], axis=0)

            rows, lanes = block.shape
            block = stage("join", join, dict(pieces=pieces), dict(block=((rows * len(pieces), lanes), F32))).block

    def both_sums(pieces, stride):
        rows = []
        for piece in pieces:
            count = piece.shape[0] // stride
            rows += [piece[i * stride + stride - 1:(i + 1) * stride] for i in range(count)]
        while len(rows) > 1:
            rows = [rows[i] + rows[i + 1] for i in range(0, len(rows), 2)]
        return rows[0]

    def as_columns(row):
        return to_column(row[:, :cases]), to_column(row[:, cases:])

    def first(i, o):
        me = lax.axis_index(AXIS)
        index, lengths = i.index[0], i.lengths[...]
        lane = lax.broadcasted_iota(jnp.int32, (1, width), 1)
        rows = []
        for _, behind, ahead, by, parity in chosen:
            forward = (me // by) % 2 == parity
            row = jnp.where(forward, index[ahead:ahead + 1], index[behind:behind + 1])
            length = jnp.where(forward, lengths[:, ahead:ahead + 1], lengths[:, behind:behind + 1])
            rows.append(jnp.where(lane < length, row, -1))
        row = jnp.concatenate(rows, axis=1)
        unpicker = (lax.broadcasted_iota(jnp.int32, (ndof, slots), 0) == row).astype(F32).astype(BF)
        picker = (lax.broadcasted_iota(jnp.int32, (slots, ndof), 1) == to_column(row)).astype(F32)
        weight = 1.0 / (1.0 + jnp.sum(picker, axis=0, keepdims=True))
        weighted = i.basis[0] * weight
        at_slots = pick(jnp.concatenate([i.load[0], weighted], axis=0), unpicker)
        inv = i.inv[...]
        inv_packed = jnp.concatenate([inv[:, j * width:(j + 1) * width] for j in range(reps)], axis=0)
        put_faces(o.face, jnp.concatenate([at_slots, jnp.concatenate([inv_packed] * blocks, axis=1)], axis=0))
        o.picker[...] = picker.astype(BF)
        o.unpicker[...] = unpicker
        o.weight[...] = weight
        o.weighted[...] = weighted
        o.basis_slots[...] = at_slots[cases:]

    packed = ((cases + primal + reps * primal, width), F32)
    start = stage(
        "first", first,
        dict(lengths=face_len, index=face_index, basis=coarse_basis, load=loads, inv=coarse_inv),
        dict(face=[packed] * blocks, picker=((slots, ndof), BF), unpicker=((ndof, slots), BF), weight=((1, ndof), F32),
             weighted=((primal, ndof), F32), basis_slots=((primal, slots), F32)))
    weight, picker, unpicker = start.weight, start.picker, start.unpicker
    came = exchange(start.face)

    part_kinds = [((ndof, ndof), BF)] * 2 + [((slots, ndof), BF)] * 2 + [((slots, slots), BF)] * 2

    def prepare(name, matrix):
        def body(i, o):
            for strip in strips:
                o.parts[0][strip], o.parts[1][strip] = split(i.matrix[0, strip])
            for at in range(2):
                face = contract(i.picker[...], o.parts[at][...]).astype(BF)
                o.parts[2 + at][...] = face
                o.parts[4 + at][...] = contract(face, i.unpicker[...]).astype(BF)

        return stage(name, body, dict(matrix=matrix, picker=picker, unpicker=unpicker), dict(parts=part_kinds)).parts

    inv = prepare("prepare_inv", neumann_inv)
    stiff = prepare("prepare_stiff", stiffness)

    own_kinds = dict(lines=((primal, cases), F32), inner_faces=faces, inner=vec)

    def solve_own(part, i, o):
        scaled = part * i.weight[...]
        o.lines[...] = times(i.weighted[...], *split(part), NT)
        o.inner_faces[...] = times(scaled, i.inv[2][...], i.inv[3][...], NT)
        o.inner[...] = times(scaled, i.inv[0][...], i.inv[1][...])

    def solve_loads(i, o):
        solve_own(i.load[0], i, o)

    own = stage("solve_loads", solve_loads, dict(load=loads, weight=weight, weighted=start.weighted, inv=inv[:4]), own_kinds)

    def reach(i, o):
        functions, rows = [i.weighted[...]], [i.inv[...]]
        for j in range(blocks):
            part = i.came[j][...]
            functions.append(pick(part[cases:cases + primal], i.picker[blocked[j]]))
            rest = part[cases + primal:]
            rows.append(jnp.concatenate([rest[k * primal:(k + 1) * primal] for k in range(reps)], axis=1))
        functions = jnp.concatenate(functions, axis=0)
        rows = jnp.concatenate(rows, axis=0)
        image = times(functions, i.stiff[0][...], i.stiff[1][...])
        image_faces = times(functions, i.stiff[2][...], i.stiff[3][...], NT)
        o.reach[0][...], o.reach[1][...] = split(jnp.concatenate([functions, image, image_faces], axis=1))
        me = lax.axis_index(AXIS)
        count = i.place.shape[1]
        for upper in range(2):
            for at in range(0, count, 256):
                lanes = slice(at, min(at + 256, count))
                device, line = i.place[:, lanes] ^ me, i.line[:, lanes]
                source = jnp.where(line < half, device * primal + upper * half + line, -1)
                move = lax.broadcasted_iota(jnp.int32, (known, lanes.stop - at), 0) == source
                o.rows[upper * own_rows:(upper + 1) * own_rows, lanes] = pick(rows, move.astype(F32).astype(BF))

    place = jnp.asarray(np.repeat(np.array(places, np.int32), lines_a_block)[None])
    line = jnp.asarray(np.tile(np.arange(lines_a_block, dtype=np.int32), total)[None])
    wide = 2 * ndof + slots
    reached = stage(
        "reach", reach,
        dict(weighted=start.weighted, inv=coarse_inv, came=came, picker=picker, stiff=stiff[:4], place=place, line=line),
        dict(reach=[((own_rows, wide), BF)] * 2, rows=((2 * own_rows, total * lines_a_block), F32)))

    def to_solve(came, own, coef=None, sums=None):
        def body(i, o):
            arrived = joined(i.came, slice(0, cases))
            if coef is not None:
                arrived = to_column(i.coef[:, cases:]) * -arrived
            lines = i.lines[...] + times(i.basis_slots[...], *split(arrived), NT)
            o.block[:half] = jnp.concatenate([lines[:half], lines[half:]], axis=1)
            o.block[half:] = i.sums[...] if sums is not None else jnp.zeros((1, 2 * cases), F32)
            put_faces(o.face, 0.5 * (i.inner_faces[...] + times(0.5 * arrived, i.inv[0][...], i.inv[1][...])))

        ins = dict(came=came, basis_slots=start.basis_slots, lines=own.lines, inner_faces=own.inner_faces, inv=inv[4:])
        if coef is not None:
            ins.update(coef=coef)
        if sums is not None:
            ins.update(sums=sums)
        made = stage("solve_rest", body, ins, dict(block=block_kind, face=face_kinds))
        return gather(made.block), exchange(made.face)

    def to_apply(step, came, own, state, coef):
        def body(i, o):
            arrived = joined(i.came, slice(0, cases))
            if step == 0:
                o.residual[...] = i.load[0] + pick(arrived, i.picker[...])
            else:
                if step > 1:
                    o.z[...] = i.z_part[...] + pick(arrived, i.picker[...])
                    arrived = to_column(i.coef[:, cases:]) * -arrived
                o.w[...] = i.w_part[...] + pick(arrived, i.picker[...])
            inner = i.weight[...] * (i.inner[...] + times(0.5 * arrived, i.inv[0][...], i.inv[1][...]))
            o.v[...] = inner
            o.image_faces[...] = times(inner, i.stiff[2][...], i.stiff[3][...], NT)
            o.image[...] = times(inner, i.stiff[0][...], i.stiff[1][...])

        ins = dict(came=came, picker=picker, weight=weight, inner=own.inner, inv=inv[2:4], stiff=stiff[:4])
        outs = dict(v=vec, image_faces=faces, image=vec)
        if step == 0:
            ins.update(load=loads)
            outs.update(residual=vec)
        else:
            ins.update(w_part=state.w_part)
            outs.update(w=vec)
        if step > 1:
            ins.update(z_part=state.z_part, coef=coef)
            outs.update(z=vec)
        return stage("apply_own", body, ins, outs)

    def apply_rest(i, o):
        rows = jnp.concatenate([ref[...] for ref in i.everyone], axis=0)
        product = times(i.rows[...], *split(rows))
        factors = (product[:own_rows, :cases] + product[own_rows:, cases:]).T
        extra = times(factors, i.reach[0][...], i.reach[1][...])
        arrived = joined(i.came)
        put_faces(o.face, i.image_faces[...] + times(arrived, i.stiff[2][...], i.stiff[3][...]) + extra[:, 2 * ndof:])
        o.inner[...] = i.v[...] + extra[:, :ndof]
        o.image[...] = i.image[...] + extra[:, ndof:2 * ndof]
        o.sums[...] = both_sums([ref[...] for ref in i.everyone], lines_a_block)

    state = SimpleNamespace()
    came_image, coef, sums = came, None, None
    for step in range(ITERS):
        final = step + 1 == ITERS
        everyone, came_solve = to_solve(came_image, own, coef, sums)
        applied = to_apply(step, came_image, own, state, coef)
        vars(state).update(vars(applied))
        made = stage(
            "apply_rest", apply_rest,
            dict(everyone=everyone, rows=reached.rows, reach=reached.reach, came=came_solve, stiff=stiff[2:],
                 image_faces=state.image_faces, v=state.v, image=state.image),
            dict(face=face_kinds, inner=vec, image=vec, sums=pair))
        came_image = exchange(made.face)

        def update(i, o, step=step, final=final):
            arrived = joined(i.came)
            inner = i.inner[...] + pick(arrived, i.picker[...])
            image = i.image[...] + times(arrived, i.stiff[0][...], i.stiff[1][...])
            weight = i.weight[...]
            if step == 0:
                part, u, residual = image, inner, i.residual[...]
                delta = dot(image, u)
            else:
                both = i.both[...]
                gamma, delta = as_columns(both)
                w = i.w[...]
                if step == 1:
                    alpha = gamma / delta
                    q, s, p = inner, w, i.u[...]
                    x = alpha * p
                    before = w
                else:
                    gamma_old, alpha_old = as_columns(i.coef[...])
                    beta = gamma / gamma_old
                    alpha = gamma / (delta - beta * gamma / alpha_old)
                    q = inner + beta * i.q[...]
                    s = w + beta * i.s[...]
                    p = i.u[...] + beta * i.p[...]
                    x = i.x[...] + alpha * p
                    before = w - (alpha * beta) * i.z[...]
                residual = i.residual[...] - alpha * s
                u = i.u[...] - alpha * q
                part = before - alpha * image
                delta = dot(weight * before - alpha * image, u)
                o.coef[...] = jnp.concatenate([both[:, :cases], to_row(alpha)], axis=1)
                o.s[...], o.p[...], o.x[...], o.residual[...], o.q[...] = s, p, x, residual, q
                o.z_part[...] = image if step == 1 else image + beta * i.z[...]
            o.u[...] = u
            o.w_part[...] = part
            o.sums[...] = jnp.concatenate([to_row(dot(weight * residual, u)), to_row(delta)], axis=1)
            if not final:
                solve_own(part, i, o)

        ins = dict(came=came_solve, picker=picker, inner=made.inner, image=made.image, stiff=stiff[2:4], weight=weight, residual=state.residual)
        outs = dict(u=vec, w_part=vec, sums=pair)
        if step > 0:
            ins.update(both=made.sums, w=state.w, u=state.u)
            outs.update(coef=pair, s=vec, p=vec, x=vec, residual=vec, q=vec, z_part=vec)
        if step > 1:
            ins.update(coef=coef, q=state.q, s=state.s, p=state.p, x=state.x, z=state.z)
        if not final:
            ins.update(weighted=start.weighted, inv=inv[:4])
            outs.update(own_kinds)
        own = stage("update", update, ins, outs)
        vars(state).update(vars(own))
        sums = own.sums
        if step > 0:
            coef = own.coef

    def finish(i, o):
        gamma_old, alpha_old = as_columns(i.coef[...])
        w = i.w_part[...] - alpha_old * pick(joined(i.came), i.picker[...])
        gamma, delta = as_columns(both_sums([ref[...] for ref in i.everyone], 1))
        beta = gamma / gamma_old
        alpha = gamma / (delta - beta * gamma / alpha_old)
        o.solution[0] = i.x[...] + alpha * (i.u[...] + beta * i.p[...])
        o.remainder[0] = i.residual[...] - alpha * (w + beta * i.s[...])

    whole = ((1, cases, ndof), F32)
    made = stage(
        "finish", finish,
        dict(everyone=gather(sums), came=came_image, picker=picker, coef=coef, w_part=state.w_part, x=state.x, u=state.u, p=state.p,
             residual=state.residual, s=state.s),
        dict(solution=whole, remainder=whole))
    return made.solution, made.remainder


def solution(mesh):
    placed = (
        P(AXIS, None, None),
        P(AXIS, None, None),
        P(AXIS, None, None),
        P(AXIS, None),
        P(AXIS, None, None),
        P(AXIS, None, None),
        P(AXIS, None),
    )
    return jax.shard_map(
        local,
        mesh=mesh,
        in_specs=placed,
        out_specs=(P(AXIS, None, None), P(AXIS, None, None)),
        check_vma=False,
    )
```

```python
from types import SimpleNamespace

import jax
import jax.numpy as jnp
import numpy as np
from jax import lax
from jax.experimental import pallas as pl
from jax.experimental.pallas import tpu as pltpu
from jax.sharding import PartitionSpec as P

CYCLE = 16
ITERS = 4

BF = jnp.bfloat16
F32 = jnp.float32
NN = ((1,), (0,))
NT = ((1,), (1,))
STAGE_BYTES = 12 * 1024 * 1024
TILES = 8
AXIS = "sub"
LONGER = 64


def contract(left, right, dims=NN):
    return lax.dot_general(left, right, (dims, ((), ())), preferred_element_type=F32)


def split(value):
    high = value.astype(BF)
    return high, (value - high.astype(F32)).astype(BF)


def times(value, high, low, dims=NN):
    rows = value.shape[0]
    top, rest = split(value)
    both = contract(jnp.concatenate([top, rest], axis=0), high, dims)
    return both[:rows] + both[rows:] + contract(top, low, dims)


def pick(value, onehot, dims=NN):
    rows = value.shape[0]
    top, rest = split(value)
    last = (value - top.astype(F32) - rest.astype(F32)).astype(BF)
    parts = contract(jnp.concatenate([top, rest, last], axis=0), onehot, dims)
    return parts[:rows] + (parts[rows:2 * rows] + parts[2 * rows:])


def diagonal(count):
    first = lax.broadcasted_iota(jnp.int32, (count, count), 0)
    return first == lax.broadcasted_iota(jnp.int32, (count, count), 1)


def to_column(row):
    count = row.shape[1]
    return jnp.sum(jnp.where(diagonal(count), jnp.broadcast_to(row, (count, count)), 0), axis=1, keepdims=True)


def to_row(column):
    count = column.shape[0]
    return jnp.sum(jnp.where(diagonal(count), jnp.broadcast_to(column, (count, count)), 0), axis=0, keepdims=True)


def dot(left, right):
    return jnp.sum(left * right, axis=1, keepdims=True)


def flat(tree):
    tree = {name: held for name, held in tree.items() if not isinstance(held, list) or held}
    names = [(name, len(held) if isinstance(held, list) else 0) for name, held in tree.items()]
    entries = []
    for held in tree.values():
        entries += held if isinstance(held, list) else [held]
    return names, entries


def named(names, entries):
    space, at = SimpleNamespace(), 0
    for name, count in names:
        setattr(space, name, list(entries[at:at + count]) if count else entries[at])
        at += max(count, 1)
    return space


def stage(name, body, ins, outs):
    in_names, arrays = flat(ins)
    out_names, kinds = flat(outs)

    def kernel(*refs):
        body(named(in_names, refs[:len(arrays)]), named(out_names, refs[len(arrays):]))

    whole = pl.BlockSpec(memory_space=pltpu.VMEM)
    made = pl.pallas_call(
        kernel,
        name=name,
        out_shape=[jax.ShapeDtypeStruct(*kind) for kind in kinds],
        in_specs=[whole] * len(arrays),
        out_specs=[whole] * len(kinds),
        compiler_params=pltpu.CompilerParams(vmem_limit_bytes=STAGE_BYTES),
    )(*arrays)
    return named(out_names, made)


def swaps(total):
    sets = []
    for by in (1, CYCLE):
        for parity in (0, 1):
            ahead = [i for i in range(total - by) if (i // by) % 2 == parity]
            sets.append((by, parity, [(i, i + by) for i in ahead] + [(i + by, i) for i in ahead]))
    return sets


def rounds_of(total):
    bits = [1 << i for i in reversed(range(total.bit_length() - 1)) if 1 << i != CYCLE]
    assert total == 1 << (len(bits) + 1)
    rounds = [[CYCLE]]
    if len(bits) % 2:
        rounds.append([bits.pop(0)])
    while bits:
        far, near = bits.pop(0), bits.pop(0)
        rounds.append([near, far, near + far])
    places = [0]
    for distances in rounds:
        places = [place ^ far for far in [0] + distances for place in places]
    return rounds, places


def local(stiffness, neumann_inv, coarse_basis, coarse_inv, loads, face_index, face_len):
    total = lax.axis_size(AXIS)
    _, cases, ndof = loads.shape
    primal = coarse_basis.shape[1]
    width = face_index.shape[2]
    known = coarse_inv.shape[1]
    half = primal // 2
    lines_a_block = half + 1
    reps = known // width
    rounds, places = rounds_of(total)

    chosen = []
    for by, parity, pairs in swaps(total):
        if pairs:
            behind, ahead = (0, 1) if by == 1 else (2, 3)
            chosen.append((pairs, behind, ahead, by, parity))
    blocks = len(chosen)
    paired = [at for at, block in enumerate(chosen) if block[3:] == (CYCLE, 0)][0]
    slots = blocks * width
    own_rows = (blocks + 1) * primal

    vec = ((cases, ndof), F32)
    faces = ((cases, slots), F32)
    pair = ((1, 2 * cases), F32)
    face_kinds = [((cases, width), F32)] * blocks
    extra_rows = [lines_a_block if at == paired else LONGER if block[3:] == (1, 1) else 0 for at, block in enumerate(chosen)]
    solve_kinds = [((cases + extra, width), F32) for extra in extra_rows]
    last_kinds = [((cases + (8 if at == paired else 0), width), F32) for at in range(blocks)]
    blocked = [slice(i * width, (i + 1) * width) for i in range(blocks)]
    strips = [slice(i * ndof // TILES, (i + 1) * ndof // TILES) for i in range(TILES)]

    def joined(refs):
        return jnp.concatenate([ref[:cases] for ref in refs], axis=1)

    def put_faces(refs, value):
        for i, ref in enumerate(refs):
            ref[:value.shape[0]] = value[:, blocked[i]]

    def exchange(arrays):
        return [lax.ppermute(array, AXIS, chosen[i][0]) for i, array in enumerate(arrays)]

    def gather(own, got, lines, after):
        pieces, start = [own, got], cases
        for distances in rounds[1:]:
            def join(i, o):
                o.block[...] = jnp.concatenate([ref[start:start + lines] for ref in i.pieces], axis=0)

            block = stage("join", join, dict(pieces=pieces, after=after), dict(block=((lines * len(pieces), 2 * cases), F32))).block
            pieces = [block] + [lax.ppermute(block, AXIS, [(i, i ^ far) for i in range(total)]) for far in distances]
            start, lines, after = 0, block.shape[0], []
        return pieces

    def both_sums(pieces, stride):
        rows = []
        for piece in pieces:
            count = piece.shape[0] // stride
            rows += [piece[i * stride + stride - 1:(i + 1) * stride] for i in range(count)]
        while len(rows) > 1:
            rows = [rows[i] + rows[i + 1] for i in range(0, len(rows), 2)]
        return rows[0]

    def as_columns(row):
        return to_column(row[:, :cases]), to_column(row[:, cases:])

    def first(i, o):
        me = lax.axis_index(AXIS)
        index, lengths = i.index[0], i.lengths[...]
        lane = lax.broadcasted_iota(jnp.int32, (1, width), 1)
        rows = []
        for _, behind, ahead, by, parity in chosen:
            forward = (me // by) % 2 == parity
            row = jnp.where(forward, index[ahead:ahead + 1], index[behind:behind + 1])
            length = jnp.where(forward, lengths[:, ahead:ahead + 1], lengths[:, behind:behind + 1])
            rows.append(jnp.where(lane < length, row, -1))
        row = jnp.concatenate(rows, axis=1)
        unpicker = (lax.broadcasted_iota(jnp.int32, (ndof, slots), 0) == row).astype(F32).astype(BF)
        picker = (lax.broadcasted_iota(jnp.int32, (slots, ndof), 1) == to_column(row)).astype(F32)
        weight = 1.0 / (1.0 + jnp.sum(picker, axis=0, keepdims=True))
        weighted = i.basis[0] * weight
        at_slots = pick(jnp.concatenate([i.load[0], weighted], axis=0), unpicker)
        inv = i.inv[...]
        inv_packed = jnp.concatenate([inv[:, j * width:(j + 1) * width] for j in range(reps)], axis=0)
        put_faces(o.face, jnp.concatenate([at_slots, jnp.concatenate([inv_packed] * blocks, axis=1)], axis=0))
        o.picker[...] = picker.astype(BF)
        o.unpicker[...] = unpicker
        o.weight[...] = weight
        o.weighted[...] = weighted
        o.basis_slots[...] = at_slots[cases:]

    packed = ((cases + primal + reps * primal, width), F32)
    start = stage(
        "first", first,
        dict(lengths=face_len, index=face_index, basis=coarse_basis, load=loads, inv=coarse_inv),
        dict(face=[packed] * blocks, picker=((slots, ndof), BF), unpicker=((ndof, slots), BF), weight=((1, ndof), F32),
             weighted=((primal, ndof), F32), basis_slots=((primal, slots), F32)))
    weight, picker, unpicker = start.weight, start.picker, start.unpicker
    came = exchange(start.face)

    part_kinds = [((ndof, ndof), BF)] * 2 + [((slots, ndof), BF)] * 2 + [((slots, slots), BF)] * 2

    def prepare(name, matrix):
        def body(i, o):
            for strip in strips:
                o.parts[0][strip], o.parts[1][strip] = split(i.matrix[0, strip])
            for at in range(2):
                face = contract(i.picker[...], o.parts[at][...]).astype(BF)
                o.parts[2 + at][...] = face
                o.parts[4 + at][...] = contract(face, i.unpicker[...]).astype(BF)

        return stage(name, body, dict(matrix=matrix, picker=picker, unpicker=unpicker), dict(parts=part_kinds)).parts

    inv = prepare("prepare_inv", neumann_inv)
    stiff = prepare("prepare_stiff", stiffness)

    own_kinds = dict(lines=((primal, cases), F32), inner_faces=faces, inner=vec)

    def solve_own(part, i, o):
        scaled = part * i.weight[...]
        o.lines[...] = times(i.weighted[...], *split(part), NT)
        o.inner_faces[...] = times(scaled, i.inv[2][...], i.inv[3][...], NT)
        o.inner[...] = times(scaled, i.inv[0][...], i.inv[1][...])

    def solve_loads(i, o):
        solve_own(i.load[0], i, o)

    own = stage("solve_loads", solve_loads, dict(load=loads, weight=weight, weighted=start.weighted, inv=inv[:4]), own_kinds)

    def reach(i, o):
        functions, rows = [i.weighted[...]], [i.inv[...]]
        for j in range(blocks):
            part = i.came[j][...]
            functions.append(pick(part[cases:cases + primal], i.picker[blocked[j]]))
            rest = part[cases + primal:]
            rows.append(jnp.concatenate([rest[k * primal:(k + 1) * primal] for k in range(reps)], axis=1))
        functions = jnp.concatenate(functions, axis=0)
        rows = jnp.concatenate(rows, axis=0)
        image = times(functions, i.stiff[0][...], i.stiff[1][...])
        image_faces = times(functions, i.stiff[2][...], i.stiff[3][...], NT)
        o.reach[0][...], o.reach[1][...] = split(jnp.concatenate([functions, image, image_faces], axis=1))
        me = lax.axis_index(AXIS)
        count = i.place.shape[1]
        for upper in range(2):
            for at in range(0, count, 256):
                lanes = slice(at, min(at + 256, count))
                device, line = i.place[:, lanes] ^ me, i.line[:, lanes]
                source = jnp.where(line < half, device * primal + upper * half + line, -1)
                move = lax.broadcasted_iota(jnp.int32, (known, lanes.stop - at), 0) == source
                o.rows[upper * own_rows:(upper + 1) * own_rows, lanes] = pick(rows, move.astype(F32).astype(BF))

    place = jnp.asarray(np.repeat(np.array(places, np.int32), lines_a_block)[None])
    line = jnp.asarray(np.tile(np.arange(lines_a_block, dtype=np.int32), total)[None])
    wide = 2 * ndof + slots
    reached = stage(
        "reach", reach,
        dict(weighted=start.weighted, inv=coarse_inv, came=came, picker=picker, stiff=stiff[:4], place=place, line=line),
        dict(reach=[((own_rows, wide), BF)] * 2, rows=((2 * own_rows, total * lines_a_block), F32)))

    def to_solve(came, own, coef=None, sums=None):
        def body(i, o):
            arrived = joined(i.came)
            if coef is not None:
                arrived = to_column(i.coef[:, cases:]) * -arrived
            lines = i.lines[...] + times(i.basis_slots[...], *split(arrived), NT)
            put_faces(o.face, 0.5 * (i.inner_faces[...] + times(0.5 * arrived, i.inv[0][...], i.inv[1][...])))
            o.face[paired][cases:cases + half] = jnp.concatenate([lines[:half], lines[half:]], axis=1)
            o.face[paired][cases + half:] = i.sums[...] if sums is not None else jnp.zeros((1, 2 * cases), F32)
            for at, extra in enumerate(extra_rows):
                if extra and at != paired:
                    o.face[at][cases:] = jnp.zeros((extra, width), F32)

        ins = dict(came=came, basis_slots=start.basis_slots, lines=own.lines, inner_faces=own.inner_faces, inv=inv[4:])
        if coef is not None:
            ins.update(coef=coef)
        if sums is not None:
            ins.update(sums=sums)
        made = stage("solve_rest", body, ins, dict(face=solve_kinds))
        return made.face[paired], exchange(made.face)

    def to_apply(step, came, own, state, coef):
        def body(i, o):
            arrived = joined(i.came)
            if step == 0:
                o.residual[...] = i.load[0] + pick(arrived, i.picker[...])
            else:
                if step > 1:
                    o.z[...] = i.z_part[...] + pick(arrived, i.picker[...])
                    arrived = to_column(i.coef[:, cases:]) * -arrived
                o.w[...] = i.w_part[...] + pick(arrived, i.picker[...])
            inner = i.weight[...] * (i.inner[...] + times(0.5 * arrived, i.inv[0][...], i.inv[1][...]))
            o.v[...] = inner
            o.image_faces[...] = times(inner, i.stiff[2][...], i.stiff[3][...], NT)
            o.image[...] = times(inner, i.stiff[0][...], i.stiff[1][...])

        ins = dict(came=came, picker=picker, weight=weight, inner=own.inner, inv=inv[2:4], stiff=stiff[:4])
        outs = dict(v=vec, image_faces=faces, image=vec)
        if step == 0:
            ins.update(load=loads)
            outs.update(residual=vec)
        else:
            ins.update(w_part=state.w_part)
            outs.update(w=vec)
        if step > 1:
            ins.update(z_part=state.z_part, coef=coef)
            outs.update(z=vec)
        return stage("apply_own", body, ins, outs)

    def corrected(i):
        rows = jnp.concatenate([ref[...] for ref in i.everyone], axis=0)
        product = times(i.rows[...], *split(rows))
        factors = (product[:own_rows, :cases] + product[own_rows:, cases:]).T
        extra = times(factors, i.reach[0][...], i.reach[1][...])
        at_slots = i.image_faces[...] + times(joined(i.came), i.stiff_block[0][...], i.stiff_block[1][...]) + extra[:, 2 * ndof:]
        both = both_sums([ref[...] for ref in i.everyone], lines_a_block)
        return at_slots, i.v[...] + extra[:, :ndof], i.image[...] + extra[:, ndof:2 * ndof], both

    def recur(i, o, step, inner, image, both):
        arrived = joined(i.came)
        inner = inner + pick(arrived, i.picker[...])
        image = image + times(arrived, i.stiff[0][...], i.stiff[1][...])
        weight = i.weight[...]
        if step == 0:
            part, u, residual = image, inner, i.residual[...]
            delta = dot(image, u)
        else:
            gamma, delta = as_columns(both)
            w = i.w[...]
            if step == 1:
                alpha = gamma / delta
                q, s, p = inner, w, i.u[...]
                x = alpha * p
                before = w
            else:
                gamma_old, alpha_old = as_columns(i.coef[...])
                beta = gamma / gamma_old
                alpha = gamma / (delta - beta * gamma / alpha_old)
                q = inner + beta * i.q[...]
                s = w + beta * i.s[...]
                p = i.u[...] + beta * i.p[...]
                x = i.x[...] + alpha * p
                before = w - (alpha * beta) * i.z[...]
            residual = i.residual[...] - alpha * s
            u = i.u[...] - alpha * q
            part = before - alpha * image
            delta = dot(weight * before - alpha * image, u)
            o.coef[...] = jnp.concatenate([both[:, :cases], to_row(alpha)], axis=1)
            o.s[...], o.p[...], o.x[...], o.residual[...] = s, p, x, residual
            if step + 1 < ITERS:
                o.q[...] = q
                o.z_part[...] = image if step == 1 else image + beta * i.z[...]
        o.u[...] = u
        o.w_part[...] = part
        return part, jnp.concatenate([to_row(dot(weight * residual, u)), to_row(delta)], axis=1)

    state = SimpleNamespace()
    came_image, coef, sums = came, None, None
    for step in range(ITERS):
        final = step + 1 == ITERS
        sent, came_solve = to_solve(came_image, own, coef, sums)
        applied = to_apply(step, came_image, own, state, coef)
        vars(state).update(vars(applied))
        everyone = gather(sent, came_solve[paired], lines_a_block, [applied.v])
        rest_ins = dict(everyone=everyone, rows=reached.rows, reach=reached.reach, came=came_solve, stiff_block=stiff[4:],
                        image_faces=state.image_faces, v=state.v, image=state.image)
        ins = dict(came=came_solve, picker=picker, stiff=stiff[2:4], weight=weight, residual=state.residual)
        outs = dict(u=vec, w_part=vec)
        if step > 0:
            ins.update(w=state.w, u=state.u)
            outs.update(coef=pair, s=vec, p=vec, x=vec, residual=vec)
            if not final:
                outs.update(q=vec, z_part=vec)
        if step > 1:
            ins.update(coef=coef, q=state.q, s=state.s, p=state.p, x=state.x, z=state.z)
        if final:
            def last(i, o):
                at_slots, inner, image, both = corrected(i)
                put_faces(o.face, at_slots)
                o.face[paired][cases:] = jnp.broadcast_to(recur(i, o, step, inner, image, both)[1], (8, 2 * cases))

            ins.update(rest_ins)
            outs.update(face=last_kinds)
            made = stage("last", last, ins, outs)
            vars(state).update(vars(made))
            came_image = exchange(made.face)
            break

        def apply_rest(i, o):
            at_slots, o.inner[...], o.image[...], o.sums[...] = corrected(i)
            put_faces(o.face, at_slots)

        made = stage("apply_rest", apply_rest, rest_ins, dict(face=face_kinds, inner=vec, image=vec, sums=pair))
        came_image = exchange(made.face)

        def update(i, o, step=step):
            part, o.sums[...] = recur(i, o, step, i.inner[...], i.image[...], i.both[...])
            solve_own(part, i, o)

        ins.update(inner=made.inner, image=made.image, both=made.sums, weighted=start.weighted, inv=inv[:4])
        outs.update(own_kinds, sums=pair)
        own = stage("update", update, ins, outs)
        vars(state).update(vars(own))
        sums = own.sums
        if step > 0:
            coef = own.coef

    def finish(i, o):
        gamma_old, alpha_old = as_columns(i.coef[...])
        w = i.w_part[...] - alpha_old * pick(joined(i.came), i.picker[...])
        gamma, delta = as_columns(both_sums([ref[...] for ref in i.everyone], 1))
        beta = gamma / gamma_old
        alpha = gamma / (delta - beta * gamma / alpha_old)
        o.solution[0] = i.x[...] + alpha * (i.u[...] + beta * i.p[...])
        o.remainder[0] = i.residual[...] - alpha * (w + beta * i.s[...])

    whole = ((1, cases, ndof), F32)
    everyone = gather(state.face[paired], came_image[paired], 1, [])
    done = stage(
        "finish", finish,
        dict(everyone=everyone, came=came_image, picker=picker, coef=state.coef, w_part=state.w_part, x=state.x, u=state.u, p=state.p,
             residual=state.residual, s=state.s),
        dict(solution=whole, remainder=whole))
    return done.solution, done.remainder


def solution(mesh):
    placed = (
        P(AXIS, None, None),
        P(AXIS, None, None),
        P(AXIS, None, None),
        P(AXIS, None),
        P(AXIS, None, None),
        P(AXIS, None, None),
        P(AXIS, None),
    )
    return jax.shard_map(
        local,
        mesh=mesh,
        in_specs=placed,
        out_specs=(P(AXIS, None, None), P(AXIS, None, None)),
        check_vma=False,
    )
```

```python
from types import SimpleNamespace

import jax
import jax.numpy as jnp
import numpy as np
from jax import lax
from jax.experimental import pallas as pl
from jax.experimental.pallas import tpu as pltpu
from jax.sharding import PartitionSpec as P

CYCLE = 16
ITERS = 4

BF = jnp.bfloat16
F32 = jnp.float32
NN = ((1,), (0,))
NT = ((1,), (1,))
STAGE_BYTES = 12 * 1024 * 1024
TILES = 8
AXIS = "sub"
LONGER = 64


def contract(left, right, dims=NN):
    return lax.dot_general(left, right, (dims, ((), ())), preferred_element_type=F32)


def split(value):
    high = value.astype(BF)
    return high, (value - high.astype(F32)).astype(BF)


def times(value, high, low, dims=NN):
    rows = value.shape[0]
    top, rest = split(value)
    both = contract(jnp.concatenate([top, rest], axis=0), high, dims)
    return both[:rows] + both[rows:] + contract(top, low, dims)


def pick(value, onehot, dims=NN):
    rows = value.shape[0]
    top, rest = split(value)
    last = (value - top.astype(F32) - rest.astype(F32)).astype(BF)
    parts = contract(jnp.concatenate([top, rest, last], axis=0), onehot, dims)
    return parts[:rows] + (parts[rows:2 * rows] + parts[2 * rows:])


def diagonal(count):
    first = lax.broadcasted_iota(jnp.int32, (count, count), 0)
    return first == lax.broadcasted_iota(jnp.int32, (count, count), 1)


def to_column(row):
    count = row.shape[1]
    return jnp.sum(jnp.where(diagonal(count), jnp.broadcast_to(row, (count, count)), 0), axis=1, keepdims=True)


def to_row(column):
    count = column.shape[0]
    return jnp.sum(jnp.where(diagonal(count), jnp.broadcast_to(column, (count, count)), 0), axis=0, keepdims=True)


def dot(left, right):
    return jnp.sum(left * right, axis=1, keepdims=True)


def flat(tree):
    tree = {name: held for name, held in tree.items() if not isinstance(held, list) or held}
    names = [(name, len(held) if isinstance(held, list) else 0) for name, held in tree.items()]
    entries = []
    for held in tree.values():
        entries += held if isinstance(held, list) else [held]
    return names, entries


def named(names, entries):
    space, at = SimpleNamespace(), 0
    for name, count in names:
        setattr(space, name, list(entries[at:at + count]) if count else entries[at])
        at += max(count, 1)
    return space


def stage(name, body, ins, outs):
    in_names, arrays = flat(ins)
    out_names, kinds = flat(outs)

    def kernel(*refs):
        body(named(in_names, refs[:len(arrays)]), named(out_names, refs[len(arrays):]))

    whole = pl.BlockSpec(memory_space=pltpu.VMEM)
    made = pl.pallas_call(
        kernel,
        name=name,
        out_shape=[jax.ShapeDtypeStruct(*kind) for kind in kinds],
        in_specs=[whole] * len(arrays),
        out_specs=[whole] * len(kinds),
        compiler_params=pltpu.CompilerParams(vmem_limit_bytes=STAGE_BYTES),
    )(*arrays)
    return named(out_names, made)


def swaps(total):
    sets = []
    for by in (1, CYCLE):
        for parity in (0, 1):
            ahead = [i for i in range(total - by) if (i // by) % 2 == parity]
            sets.append((by, parity, [(i, i + by) for i in ahead] + [(i + by, i) for i in ahead]))
    return sets


def rounds_of(total):
    bits = [1 << i for i in reversed(range(total.bit_length() - 1)) if 1 << i != CYCLE]
    assert total == 1 << (len(bits) + 1)
    rounds = [[CYCLE]]
    if len(bits) % 2:
        rounds.append([bits.pop(0)])
    while bits:
        far, near = bits.pop(0), bits.pop(0)
        rounds.append([near, far, near + far])
    places = [0]
    for distances in rounds:
        places = [place ^ far for far in [0] + distances for place in places]
    return rounds, places


def local(stiffness, neumann_inv, coarse_basis, coarse_inv, loads, face_index, face_len):
    total = lax.axis_size(AXIS)
    _, cases, ndof = loads.shape
    primal = coarse_basis.shape[1]
    width = face_index.shape[2]
    known = coarse_inv.shape[1]
    half = primal // 2
    lines_a_block = half + 1
    reps = known // width
    rounds, places = rounds_of(total)

    chosen = []
    for by, parity, pairs in swaps(total):
        if pairs:
            behind, ahead = (0, 1) if by == 1 else (2, 3)
            chosen.append((pairs, behind, ahead, by, parity))
    blocks = len(chosen)
    paired = [at for at, block in enumerate(chosen) if block[3:] == (CYCLE, 0)][0]
    slots = blocks * width
    own_rows = (blocks + 1) * primal

    vec = ((cases, ndof), F32)
    faces = ((cases, slots), F32)
    pair = ((1, 2 * cases), F32)
    face_kinds = [((cases, width), F32)] * blocks
    extra_rows = [lines_a_block if at == paired else LONGER if block[3:] == (1, 1) else 0 for at, block in enumerate(chosen)]
    solve_kinds = [((cases + extra, width), F32) for extra in extra_rows]
    last_kinds = [((cases + (8 if at == paired else 0), width), F32) for at in range(blocks)]
    blocked = [slice(i * width, (i + 1) * width) for i in range(blocks)]
    strips = [slice(i * ndof // TILES, (i + 1) * ndof // TILES) for i in range(TILES)]

    def joined(refs):
        return jnp.concatenate([ref[:cases] for ref in refs], axis=1)

    def put_faces(refs, value):
        for i, ref in enumerate(refs):
            ref[:value.shape[0]] = value[:, blocked[i]]

    def exchange(arrays):
        return [lax.ppermute(array, AXIS, chosen[i][0]) for i, array in enumerate(arrays)]

    def gather(own, got, lines, after=()):
        pieces, start = [own, got], cases
        for distances in rounds[1:]:
            def join(i, o):
                o.block[...] = jnp.concatenate([ref[start:start + lines] for ref in i.pieces], axis=0)

            block = stage("join", join, dict(pieces=pieces, after=list(after)), dict(block=((lines * len(pieces), 2 * cases), F32))).block
            pieces = [block] + [lax.ppermute(block, AXIS, [(i, i ^ far) for i in range(total)]) for far in distances]
            start, lines, after = 0, block.shape[0], ()
        return pieces

    def both_sums(pieces, stride):
        rows = []
        for piece in pieces:
            count = piece.shape[0] // stride
            rows += [piece[i * stride + stride - 1:(i + 1) * stride] for i in range(count)]
        while len(rows) > 1:
            rows = [rows[i] + rows[i + 1] for i in range(0, len(rows), 2)]
        return rows[0]

    def as_columns(row):
        return to_column(row[:, :cases]), to_column(row[:, cases:])

    def first(i, o):
        me = lax.axis_index(AXIS)
        index, lengths = i.index[0], i.lengths[...]
        lane = lax.broadcasted_iota(jnp.int32, (1, width), 1)
        rows = []
        for _, behind, ahead, by, parity in chosen:
            forward = (me // by) % 2 == parity
            row = jnp.where(forward, index[ahead:ahead + 1], index[behind:behind + 1])
            length = jnp.where(forward, lengths[:, ahead:ahead + 1], lengths[:, behind:behind + 1])
            rows.append(jnp.where(lane < length, row, -1))
        row = jnp.concatenate(rows, axis=1)
        unpicker = (lax.broadcasted_iota(jnp.int32, (ndof, slots), 0) == row).astype(F32).astype(BF)
        picker = (lax.broadcasted_iota(jnp.int32, (slots, ndof), 1) == to_column(row)).astype(F32)
        weight = 1.0 / (1.0 + jnp.sum(picker, axis=0, keepdims=True))
        weighted = i.basis[0] * weight
        at_slots = pick(jnp.concatenate([i.load[0], weighted], axis=0), unpicker)
        inv = i.inv[...]
        inv_packed = jnp.concatenate([inv[:, j * width:(j + 1) * width] for j in range(reps)], axis=0)
        put_faces(o.face, jnp.concatenate([at_slots, jnp.concatenate([inv_packed] * blocks, axis=1)], axis=0))
        o.picker[...] = picker.astype(BF)
        o.unpicker[...] = unpicker
        o.weight[...] = weight
        o.weighted[...] = weighted
        o.basis_slots[...] = at_slots[cases:]

    packed = ((cases + primal + reps * primal, width), F32)
    start = stage(
        "first", first,
        dict(lengths=face_len, index=face_index, basis=coarse_basis, load=loads, inv=coarse_inv),
        dict(face=[packed] * blocks, picker=((slots, ndof), BF), unpicker=((ndof, slots), BF), weight=((1, ndof), F32),
             weighted=((primal, ndof), F32), basis_slots=((primal, slots), F32)))
    weight, picker, unpicker = start.weight, start.picker, start.unpicker
    came = exchange(start.face)

    part_kinds = [((ndof, ndof), BF)] * 2 + [((slots, ndof), BF)] * 2 + [((slots, slots), BF)] * 2

    def prepare(name, matrix):
        def body(i, o):
            for strip in strips:
                o.parts[0][strip], o.parts[1][strip] = split(i.matrix[0, strip])
            for at in range(2):
                face = contract(i.picker[...], o.parts[at][...]).astype(BF)
                o.parts[2 + at][...] = face
                o.parts[4 + at][...] = contract(face, i.unpicker[...]).astype(BF)

        return stage(name, body, dict(matrix=matrix, picker=picker, unpicker=unpicker), dict(parts=part_kinds)).parts

    inv = prepare("prepare_inv", neumann_inv)
    stiff = prepare("prepare_stiff", stiffness)

    own_kinds = dict(lines=((primal, cases), F32), inner_faces=faces, inner=vec)

    def solve_own(part, i, o):
        scaled = part * i.weight[...]
        o.lines[...] = times(i.weighted[...], *split(part), NT)
        o.inner_faces[...] = times(scaled, i.inv[2][...], i.inv[3][...], NT)
        o.inner[...] = times(scaled, i.inv[0][...], i.inv[1][...])

    def solve_loads(i, o):
        solve_own(i.load[0], i, o)

    own = stage("solve_loads", solve_loads, dict(load=loads, weight=weight, weighted=start.weighted, inv=inv[:4]), own_kinds)

    def reach(i, o):
        functions, rows = [i.weighted[...]], [i.inv[...]]
        for j in range(blocks):
            part = i.came[j][...]
            functions.append(pick(part[cases:cases + primal], i.picker[blocked[j]]))
            rest = part[cases + primal:]
            rows.append(jnp.concatenate([rest[k * primal:(k + 1) * primal] for k in range(reps)], axis=1))
        functions = jnp.concatenate(functions, axis=0)
        rows = jnp.concatenate(rows, axis=0)
        image = times(functions, i.stiff[0][...], i.stiff[1][...])
        image_faces = times(functions, i.stiff[2][...], i.stiff[3][...], NT)
        o.reach[0][...], o.reach[1][...] = split(jnp.concatenate([functions, image], axis=1))
        o.reach_faces[0][...], o.reach_faces[1][...] = split(image_faces)
        me = lax.axis_index(AXIS)
        count = i.place.shape[1]
        for upper in range(2):
            for at in range(0, count, 256):
                lanes = slice(at, min(at + 256, count))
                device, line = i.place[:, lanes] ^ me, i.line[:, lanes]
                source = jnp.where(line < half, device * primal + upper * half + line, -1)
                move = lax.broadcasted_iota(jnp.int32, (known, lanes.stop - at), 0) == source
                o.rows[upper * own_rows:(upper + 1) * own_rows, lanes] = pick(rows, move.astype(F32).astype(BF))

    place = jnp.asarray(np.repeat(np.array(places, np.int32), lines_a_block)[None])
    line = jnp.asarray(np.tile(np.arange(lines_a_block, dtype=np.int32), total)[None])
    reached = stage(
        "reach", reach,
        dict(weighted=start.weighted, inv=coarse_inv, came=came, picker=picker, stiff=stiff[:4], place=place, line=line),
        dict(reach=[((own_rows, 2 * ndof), BF)] * 2, reach_faces=[((own_rows, slots), BF)] * 2, rows=((2 * own_rows, total * lines_a_block), F32)))

    def to_solve(came, own, coef=None, sums=None):
        def body(i, o):
            arrived = joined(i.came)
            if coef is not None:
                arrived = to_column(i.coef[:, cases:]) * -arrived
            lines = i.lines[...] + times(i.basis_slots[...], *split(arrived), NT)
            put_faces(o.face, 0.5 * (i.inner_faces[...] + times(0.5 * arrived, i.inv[0][...], i.inv[1][...])))
            o.face[paired][cases:cases + half] = jnp.concatenate([lines[:half], lines[half:]], axis=1)
            o.face[paired][cases + half:] = i.sums[...] if sums is not None else jnp.zeros((1, 2 * cases), F32)
            for at, extra in enumerate(extra_rows):
                if extra and at != paired:
                    o.face[at][cases:] = jnp.zeros((extra, width), F32)

        ins = dict(came=came, basis_slots=start.basis_slots, lines=own.lines, inner_faces=own.inner_faces, inv=inv[4:])
        if coef is not None:
            ins.update(coef=coef)
        if sums is not None:
            ins.update(sums=sums)
        made = stage("solve_rest", body, ins, dict(face=solve_kinds))
        return made.face[paired], exchange(made.face)

    def to_apply(step, came, own, state, coef):
        def body(i, o):
            arrived = joined(i.came)
            if step == 0:
                o.residual[...] = i.load[0] + pick(arrived, i.picker[...])
            else:
                if step > 1:
                    o.z[...] = i.z_part[...] + pick(arrived, i.picker[...])
                    arrived = to_column(i.coef[:, cases:]) * -arrived
                o.w[...] = i.w_part[...] + pick(arrived, i.picker[...])
            inner = i.weight[...] * (i.inner[...] + times(0.5 * arrived, i.inv[0][...], i.inv[1][...]))
            o.v[...] = inner
            o.image_faces[...] = times(inner, i.stiff[2][...], i.stiff[3][...], NT)
            o.image[...] = times(inner, i.stiff[0][...], i.stiff[1][...])

        ins = dict(came=came, picker=picker, weight=weight, inner=own.inner, inv=inv[2:4], stiff=stiff[:4])
        outs = dict(v=vec, image_faces=faces, image=vec)
        if step == 0:
            ins.update(load=loads)
            outs.update(residual=vec)
        else:
            ins.update(w_part=state.w_part)
            outs.update(w=vec)
        if step > 1:
            ins.update(z_part=state.z_part, coef=coef)
            outs.update(z=vec)
        return stage("apply_own", body, ins, outs)

    def corrected(i):
        rows = jnp.concatenate([ref[...] for ref in i.everyone], axis=0)
        product = times(i.rows[...], *split(rows))
        factors = (product[:own_rows, :cases] + product[own_rows:, cases:]).T
        at_slots = i.image_faces[...] + times(joined(i.came), i.stiff_block[0][...], i.stiff_block[1][...])
        both = both_sums([ref[...] for ref in i.everyone], lines_a_block)
        return at_slots + times(factors, i.reach_faces[0][...], i.reach_faces[1][...]), factors, both

    def recur(i, o, step, factors, both):
        arrived = joined(i.came)
        extra = times(factors, i.reach[0][...], i.reach[1][...])
        inner = i.v[...] + pick(arrived, i.picker[...]) + extra[:, :ndof]
        image = i.image[...] + times(arrived, i.stiff[0][...], i.stiff[1][...]) + extra[:, ndof:]
        weight = i.weight[...]
        if step == 0:
            part, u, residual = image, inner, i.residual[...]
            delta = dot(image, u)
        else:
            gamma, delta = as_columns(both)
            w = i.w[...]
            if step == 1:
                alpha = gamma / delta
                q, s, p = inner, w, i.u[...]
                x = alpha * p
                before = w
            else:
                gamma_old, alpha_old = as_columns(i.coef[...])
                beta = gamma / gamma_old
                alpha = gamma / (delta - beta * gamma / alpha_old)
                q = inner + beta * i.q[...]
                s = w + beta * i.s[...]
                p = i.u[...] + beta * i.p[...]
                x = i.x[...] + alpha * p
                before = w - (alpha * beta) * i.z[...]
            residual = i.residual[...] - alpha * s
            u = i.u[...] - alpha * q
            part = before - alpha * image
            delta = dot(weight * before - alpha * image, u)
            o.coef[...] = jnp.concatenate([both[:, :cases], to_row(alpha)], axis=1)
            o.s[...], o.p[...], o.x[...], o.residual[...] = s, p, x, residual
            if step + 1 < ITERS:
                o.q[...] = q
                o.z_part[...] = image if step == 1 else image + beta * i.z[...]
        o.u[...] = u
        o.w_part[...] = part
        return part, jnp.concatenate([to_row(dot(weight * residual, u)), to_row(delta)], axis=1)

    state = SimpleNamespace()
    came_image, coef, sums = came, None, None
    for step in range(ITERS):
        final = step + 1 == ITERS
        sent, came_solve = to_solve(came_image, own, coef, sums)
        applied = to_apply(step, came_image, own, state, coef)
        vars(state).update(vars(applied))
        everyone = gather(sent, came_solve[paired], lines_a_block)
        rest_ins = dict(everyone=everyone, rows=reached.rows, reach_faces=reached.reach_faces, came=came_solve, stiff_block=stiff[4:],
                        image_faces=state.image_faces)
        ins = dict(came=came_solve, picker=picker, stiff=stiff[2:4], weight=weight, residual=state.residual, reach=reached.reach,
                   v=state.v, image=state.image)
        outs = dict(u=vec, w_part=vec)
        if step > 0:
            ins.update(w=state.w, u=state.u)
            outs.update(coef=pair, s=vec, p=vec, x=vec, residual=vec)
            if not final:
                outs.update(q=vec, z_part=vec)
        if step > 1:
            ins.update(coef=coef, q=state.q, s=state.s, p=state.p, x=state.x, z=state.z)
        if final:
            def last(i, o):
                at_slots, factors, both = corrected(i)
                put_faces(o.face, at_slots)
                o.face[paired][cases:] = jnp.broadcast_to(recur(i, o, step, factors, both)[1], (8, 2 * cases))

            ins.update(rest_ins)
            outs.update(face=last_kinds)
            made = stage("last", last, ins, outs)
            vars(state).update(vars(made))
            came_image = exchange(made.face)
            break

        def apply_rest(i, o):
            at_slots, o.factors[...], o.sums[...] = corrected(i)
            put_faces(o.face, at_slots)

        made = stage("apply_rest", apply_rest, rest_ins, dict(face=face_kinds, factors=((cases, own_rows), F32), sums=pair))
        came_image = exchange(made.face)

        def update(i, o, step=step):
            part, o.sums[...] = recur(i, o, step, i.factors[...], i.both[...])
            solve_own(part, i, o)

        ins.update(factors=made.factors, both=made.sums, weighted=start.weighted, inv=inv[:4])
        outs.update(own_kinds, sums=pair)
        own = stage("update", update, ins, outs)
        vars(state).update(vars(own))
        sums = own.sums
        if step > 0:
            coef = own.coef

    def finish(i, o):
        gamma_old, alpha_old = as_columns(i.coef[...])
        w = i.w_part[...] - alpha_old * pick(joined(i.came), i.picker[...])
        gamma, delta = as_columns(both_sums([ref[...] for ref in i.everyone], 1))
        beta = gamma / gamma_old
        alpha = gamma / (delta - beta * gamma / alpha_old)
        o.solution[0] = i.x[...] + alpha * (i.u[...] + beta * i.p[...])
        o.remainder[0] = i.residual[...] - alpha * (w + beta * i.s[...])

    whole = ((1, cases, ndof), F32)
    everyone = gather(state.face[paired], came_image[paired], 1)
    done = stage(
        "finish", finish,
        dict(everyone=everyone, came=came_image, picker=picker, coef=state.coef, w_part=state.w_part, x=state.x, u=state.u, p=state.p,
             residual=state.residual, s=state.s),
        dict(solution=whole, remainder=whole))
    return done.solution, done.remainder


def solution(mesh):
    placed = (
        P(AXIS, None, None),
        P(AXIS, None, None),
        P(AXIS, None, None),
        P(AXIS, None),
        P(AXIS, None, None),
        P(AXIS, None, None),
        P(AXIS, None),
    )
    return jax.shard_map(
        local,
        mesh=mesh,
        in_specs=placed,
        out_specs=(P(AXIS, None, None), P(AXIS, None, None)),
        check_vma=False,
    )
```

```python
from types import SimpleNamespace

import jax
import jax.numpy as jnp
import numpy as np
from jax import lax
from jax.experimental import pallas as pl
from jax.experimental.pallas import tpu as pltpu
from jax.sharding import PartitionSpec as P

CYCLE = 16
ITERS = 4

BF = jnp.bfloat16
F32 = jnp.float32
NN = ((1,), (0,))
NT = ((1,), (1,))
STAGE_BYTES = 12 * 1024 * 1024
TILES = 8
AXIS = "sub"
LONGER = 64


def contract(left, right, dims=NN):
    return lax.dot_general(left, right, (dims, ((), ())), preferred_element_type=F32)


def split(value):
    high = value.astype(BF)
    return high, (value - high.astype(F32)).astype(BF)


def times(value, high, low, dims=NN):
    rows = value.shape[0]
    top, rest = split(value)
    both = contract(jnp.concatenate([top, rest], axis=0), high, dims)
    return both[:rows] + both[rows:] + contract(top, low, dims)


def pick(value, onehot, dims=NN):
    rows = value.shape[0]
    top, rest = split(value)
    last = (value - top.astype(F32) - rest.astype(F32)).astype(BF)
    parts = contract(jnp.concatenate([top, rest, last], axis=0), onehot, dims)
    return parts[:rows] + (parts[rows:2 * rows] + parts[2 * rows:])


def diagonal(count):
    first = lax.broadcasted_iota(jnp.int32, (count, count), 0)
    return first == lax.broadcasted_iota(jnp.int32, (count, count), 1)


def to_column(row):
    count = row.shape[1]
    return jnp.sum(jnp.where(diagonal(count), jnp.broadcast_to(row, (count, count)), 0), axis=1, keepdims=True)


def to_row(column):
    count = column.shape[0]
    return jnp.sum(jnp.where(diagonal(count), jnp.broadcast_to(column, (count, count)), 0), axis=0, keepdims=True)


def dot(left, right):
    return jnp.sum(left * right, axis=1, keepdims=True)


def flat(tree):
    tree = {name: held for name, held in tree.items() if not isinstance(held, list) or held}
    names = [(name, len(held) if isinstance(held, list) else 0) for name, held in tree.items()]
    entries = []
    for held in tree.values():
        entries += held if isinstance(held, list) else [held]
    return names, entries


def named(names, entries):
    space, at = SimpleNamespace(), 0
    for name, count in names:
        setattr(space, name, list(entries[at:at + count]) if count else entries[at])
        at += max(count, 1)
    return space


def stage(name, body, ins, outs):
    in_names, arrays = flat(ins)
    out_names, kinds = flat(outs)

    def kernel(*refs):
        body(named(in_names, refs[:len(arrays)]), named(out_names, refs[len(arrays):]))

    whole = pl.BlockSpec(memory_space=pltpu.VMEM)
    made = pl.pallas_call(
        kernel,
        name=name,
        out_shape=[jax.ShapeDtypeStruct(*kind) for kind in kinds],
        in_specs=[whole] * len(arrays),
        out_specs=[whole] * len(kinds),
        compiler_params=pltpu.CompilerParams(vmem_limit_bytes=STAGE_BYTES),
    )(*arrays)
    return named(out_names, made)


def swaps(total):
    sets = []
    for by in (1, CYCLE):
        for parity in (0, 1):
            ahead = [i for i in range(total - by) if (i // by) % 2 == parity]
            sets.append((by, parity, [(i, i + by) for i in ahead] + [(i + by, i) for i in ahead]))
    return sets


def rounds_of(total):
    bits = [1 << i for i in reversed(range(total.bit_length() - 1)) if 1 << i != CYCLE]
    assert total == 1 << (len(bits) + 1)
    rounds = [[CYCLE]]
    if len(bits) % 2:
        rounds.append([bits.pop(0)])
    while bits:
        far, near = bits.pop(0), bits.pop(0)
        rounds.append([near + far, far, near])
    places = [0]
    for distances in rounds:
        places = [place ^ far for far in [0] + distances for place in places]
    return rounds, places


def local(stiffness, neumann_inv, coarse_basis, coarse_inv, loads, face_index, face_len):
    total = lax.axis_size(AXIS)
    _, cases, ndof = loads.shape
    primal = coarse_basis.shape[1]
    width = face_index.shape[2]
    known = coarse_inv.shape[1]
    half = primal // 2
    lines_a_block = half + 1
    reps = known // width
    rounds, places = rounds_of(total)

    chosen = []
    for by, parity, pairs in swaps(total):
        if pairs:
            behind, ahead = (0, 1) if by == 1 else (2, 3)
            chosen.append((pairs, behind, ahead, by, parity))
    blocks = len(chosen)
    paired = [at for at, block in enumerate(chosen) if block[3:] == (CYCLE, 0)][0]
    slots = blocks * width
    own_rows = (blocks + 1) * primal

    vec = ((cases, ndof), F32)
    faces = ((cases, slots), F32)
    pair = ((1, 2 * cases), F32)
    face_kinds = [((cases, width), F32)] * blocks
    extra_rows = [lines_a_block if at == paired else LONGER if block[3:] == (1, 1) else 0 for at, block in enumerate(chosen)]
    solve_kinds = [((cases + extra, width), F32) for extra in extra_rows]
    last_kinds = [((cases + (8 if at == paired else 0), width), F32) for at in range(blocks)]
    blocked = [slice(i * width, (i + 1) * width) for i in range(blocks)]
    strips = [slice(i * ndof // TILES, (i + 1) * ndof // TILES) for i in range(TILES)]

    def joined(refs):
        return jnp.concatenate([ref[:cases] for ref in refs], axis=1)

    def put_faces(refs, value):
        for i, ref in enumerate(refs):
            ref[:value.shape[0]] = value[:, blocked[i]]

    def exchange(arrays):
        return [lax.ppermute(array, AXIS, chosen[i][0]) for i, array in enumerate(arrays)]

    def gather(own, got, lines, beside=()):
        pieces, start = [own, got], cases
        for at, distances in enumerate(rounds[1:]):
            def join(i, o):
                o.block[...] = jnp.concatenate([ref[start:start + lines] for ref in i.pieces], axis=0)

            block = stage("join", join, dict(pieces=pieces, beside=list(beside[at:at + 1])), dict(block=((lines * len(pieces), 2 * cases), F32))).block
            pieces = [block] + [lax.ppermute(block, AXIS, [(i, i ^ far) for i in range(total)]) for far in distances]
            start, lines = 0, block.shape[0]
        return pieces

    def both_sums(pieces, stride):
        rows = []
        for piece in pieces:
            count = piece.shape[0] // stride
            rows += [piece[i * stride + stride - 1:(i + 1) * stride] for i in range(count)]
        while len(rows) > 1:
            rows = [rows[i] + rows[i + 1] for i in range(0, len(rows), 2)]
        return rows[0]

    def as_columns(row):
        return to_column(row[:, :cases]), to_column(row[:, cases:])

    def first(i, o):
        me = lax.axis_index(AXIS)
        index, lengths = i.index[0], i.lengths[...]
        lane = lax.broadcasted_iota(jnp.int32, (1, width), 1)
        rows = []
        for _, behind, ahead, by, parity in chosen:
            forward = (me // by) % 2 == parity
            row = jnp.where(forward, index[ahead:ahead + 1], index[behind:behind + 1])
            length = jnp.where(forward, lengths[:, ahead:ahead + 1], lengths[:, behind:behind + 1])
            rows.append(jnp.where(lane < length, row, -1))
        row = jnp.concatenate(rows, axis=1)
        unpicker = (lax.broadcasted_iota(jnp.int32, (ndof, slots), 0) == row).astype(F32).astype(BF)
        picker = (lax.broadcasted_iota(jnp.int32, (slots, ndof), 1) == to_column(row)).astype(F32)
        weight = 1.0 / (1.0 + jnp.sum(picker, axis=0, keepdims=True))
        weighted = i.basis[0] * weight
        at_slots = pick(jnp.concatenate([i.load[0], weighted], axis=0), unpicker)
        inv = i.inv[...]
        inv_packed = jnp.concatenate([inv[:, j * width:(j + 1) * width] for j in range(reps)], axis=0)
        put_faces(o.face, jnp.concatenate([at_slots, jnp.concatenate([inv_packed] * blocks, axis=1)], axis=0))
        o.picker[...] = picker.astype(BF)
        o.unpicker[...] = unpicker
        o.weight[...] = weight
        o.weighted[...] = weighted
        o.basis_slots[...] = at_slots[cases:]

    packed = ((cases + primal + reps * primal, width), F32)
    start = stage(
        "first", first,
        dict(lengths=face_len, index=face_index, basis=coarse_basis, load=loads, inv=coarse_inv),
        dict(face=[packed] * blocks, picker=((slots, ndof), BF), unpicker=((ndof, slots), BF), weight=((1, ndof), F32),
             weighted=((primal, ndof), F32), basis_slots=((primal, slots), F32)))
    weight, picker, unpicker = start.weight, start.picker, start.unpicker
    came = exchange(start.face)

    part_kinds = [((ndof, ndof), BF)] * 2 + [((slots, ndof), BF)] * 2 + [((slots, slots), BF)] * 2

    def prepare(name, matrix):
        def body(i, o):
            for strip in strips:
                o.parts[0][strip], o.parts[1][strip] = split(i.matrix[0, strip])
            for at in range(2):
                face = contract(i.picker[...], o.parts[at][...]).astype(BF)
                o.parts[2 + at][...] = face
                o.parts[4 + at][...] = contract(face, i.unpicker[...]).astype(BF)

        return stage(name, body, dict(matrix=matrix, picker=picker, unpicker=unpicker), dict(parts=part_kinds)).parts

    inv = prepare("prepare_inv", neumann_inv)
    stiff = prepare("prepare_stiff", stiffness)

    own_kinds = dict(lines=((primal, cases), F32), inner_faces=faces, inner=vec)

    def solve_own(part, i, o):
        scaled = part * i.weight[...]
        o.lines[...] = times(i.weighted[...], *split(part), NT)
        o.inner_faces[...] = times(scaled, i.inv[2][...], i.inv[3][...], NT)
        o.inner[...] = times(scaled, i.inv[0][...], i.inv[1][...])

    def loads_faces(i, o):
        o.lines[...] = times(i.weighted[...], *split(i.load[0]), NT)
        o.inner_faces[...] = times(i.load[0] * i.weight[...], i.inv[0][...], i.inv[1][...], NT)

    def loads_inner(i, o):
        o.inner[...] = times(i.load[0] * i.weight[...], i.inv[0][...], i.inv[1][...])

    own = stage("loads_faces", loads_faces, dict(load=loads, weight=weight, weighted=start.weighted, inv=inv[2:4]),
                dict(lines=own_kinds["lines"], inner_faces=faces))
    own.inner = stage("loads_inner", loads_inner, dict(load=loads, weight=weight, inv=inv[:2]), dict(inner=vec)).inner

    def reach(i, o):
        functions, rows = [i.weighted[...]], [i.inv[...]]
        for j in range(blocks):
            part = i.came[j][...]
            functions.append(pick(part[cases:cases + primal], i.picker[blocked[j]]))
            rest = part[cases + primal:]
            rows.append(jnp.concatenate([rest[k * primal:(k + 1) * primal] for k in range(reps)], axis=1))
        functions = jnp.concatenate(functions, axis=0)
        rows = jnp.concatenate(rows, axis=0)
        image = times(functions, i.stiff[0][...], i.stiff[1][...])
        image_faces = times(functions, i.stiff[2][...], i.stiff[3][...], NT)
        o.reach[0][...], o.reach[1][...] = split(jnp.concatenate([functions, image], axis=1))
        o.reach_faces[0][...], o.reach_faces[1][...] = split(image_faces)
        me = lax.axis_index(AXIS)
        count = i.place.shape[1]
        for upper in range(2):
            for at in range(0, count, 256):
                lanes = slice(at, min(at + 256, count))
                device, line = i.place[:, lanes] ^ me, i.line[:, lanes]
                source = jnp.where(line < half, device * primal + upper * half + line, -1)
                move = lax.broadcasted_iota(jnp.int32, (known, lanes.stop - at), 0) == source
                o.rows[upper * own_rows:(upper + 1) * own_rows, lanes] = pick(rows, move.astype(F32).astype(BF))

    place = jnp.asarray(np.repeat(np.array(places, np.int32), lines_a_block)[None])
    line = jnp.asarray(np.tile(np.arange(lines_a_block, dtype=np.int32), total)[None])
    reached = stage(
        "reach", reach,
        dict(weighted=start.weighted, inv=coarse_inv, came=came, picker=picker, stiff=stiff[:4], place=place, line=line),
        dict(reach=[((own_rows, 2 * ndof), BF)] * 2, reach_faces=[((own_rows, slots), BF)] * 2, rows=((2 * own_rows, total * lines_a_block), F32)))

    def to_solve(came, own, coef=None, sums=None):
        def body(i, o):
            arrived = joined(i.came)
            if coef is not None:
                arrived = to_column(i.coef[:, cases:]) * -arrived
            lines = i.lines[...] + times(i.basis_slots[...], *split(arrived), NT)
            put_faces(o.face, 0.5 * (i.inner_faces[...] + times(0.5 * arrived, i.inv[0][...], i.inv[1][...])))
            o.face[paired][cases:cases + half] = jnp.concatenate([lines[:half], lines[half:]], axis=1)
            o.face[paired][cases + half:] = i.sums[...] if sums is not None else jnp.zeros((1, 2 * cases), F32)
            for at, extra in enumerate(extra_rows):
                if extra and at != paired:
                    o.face[at][cases:] = jnp.zeros((extra, width), F32)

        ins = dict(came=came, basis_slots=start.basis_slots, lines=own.lines, inner_faces=own.inner_faces, inv=inv[4:])
        if coef is not None:
            ins.update(coef=coef)
        if sums is not None:
            ins.update(sums=sums)
        made = stage("solve_rest", body, ins, dict(face=solve_kinds))
        return made.face[paired], exchange(made.face)

    def to_apply(step, came, own, state, coef):
        def body(i, o):
            arrived = joined(i.came)
            if step == 0:
                o.residual[...] = i.load[0] + pick(arrived, i.picker[...])
            else:
                if step > 1:
                    o.z[...] = i.z_part[...] + pick(arrived, i.picker[...])
                    arrived = to_column(i.coef[:, cases:]) * -arrived
                o.w[...] = i.w_part[...] + pick(arrived, i.picker[...])
            inner = i.weight[...] * (i.inner[...] + times(0.5 * arrived, i.inv[0][...], i.inv[1][...]))
            o.v[...] = inner
            o.image_faces[...] = times(inner, i.stiff[2][...], i.stiff[3][...], NT)
            o.image[...] = times(inner, i.stiff[0][...], i.stiff[1][...])

        ins = dict(came=came, picker=picker, weight=weight, inner=own.inner, inv=inv[2:4], stiff=stiff[:4])
        outs = dict(v=vec, image_faces=faces, image=vec)
        if step == 0:
            ins.update(load=loads)
            outs.update(residual=vec)
        else:
            ins.update(w_part=state.w_part)
            outs.update(w=vec)
        if step > 1:
            ins.update(z_part=state.z_part, coef=coef)
            outs.update(z=vec)
        return stage("apply_own", body, ins, outs)

    def corrected(i):
        rows = jnp.concatenate([ref[...] for ref in i.everyone], axis=0)
        product = times(i.rows[...], *split(rows))
        factors = (product[:own_rows, :cases] + product[own_rows:, cases:]).T
        at_slots = i.image_faces[...] + times(joined(i.came), i.stiff_block[0][...], i.stiff_block[1][...])
        both = both_sums([ref[...] for ref in i.everyone], lines_a_block)
        return at_slots + times(factors, i.reach_faces[0][...], i.reach_faces[1][...]), factors, both

    def recur(i, o, step, factors, both):
        arrived = joined(i.came)
        extra = times(factors, i.reach[0][...], i.reach[1][...])
        inner = i.v[...] + pick(arrived, i.picker[...]) + extra[:, :ndof]
        image = i.image[...] + times(arrived, i.stiff[0][...], i.stiff[1][...]) + extra[:, ndof:]
        weight = i.weight[...]
        if step == 0:
            part, u, residual = image, inner, i.residual[...]
            delta = dot(image, u)
        else:
            gamma, delta = as_columns(both)
            w = i.w[...]
            if step == 1:
                alpha = gamma / delta
                q, s, p = inner, w, i.u[...]
                x = alpha * p
                before = w
            else:
                gamma_old, alpha_old = as_columns(i.coef[...])
                beta = gamma / gamma_old
                alpha = gamma / (delta - beta * gamma / alpha_old)
                q = inner + beta * i.q[...]
                s = w + beta * i.s[...]
                p = i.u[...] + beta * i.p[...]
                x = i.x[...] + alpha * p
                before = w - (alpha * beta) * i.z[...]
            residual = i.residual[...] - alpha * s
            u = i.u[...] - alpha * q
            part = before - alpha * image
            delta = dot(weight * before - alpha * image, u)
            o.coef[...] = jnp.concatenate([both[:, :cases], to_row(alpha)], axis=1)
            o.s[...], o.p[...], o.x[...], o.residual[...] = s, p, x, residual
            if step + 1 < ITERS:
                o.q[...] = q
                o.z_part[...] = image if step == 1 else image + beta * i.z[...]
        o.u[...] = u
        o.w_part[...] = part
        return part, jnp.concatenate([to_row(dot(weight * residual, u)), to_row(delta)], axis=1)

    state = SimpleNamespace()
    came_image, coef, sums = came, None, None
    for step in range(ITERS):
        final = step + 1 == ITERS
        sent, came_solve = to_solve(came_image, own, coef, sums)
        applied = to_apply(step, came_image, own, state, coef)
        vars(state).update(vars(applied))
        everyone = gather(sent, came_solve[paired], lines_a_block, (stiff[4], reached.rows) if step == 0 else ())
        rest_ins = dict(everyone=everyone, rows=reached.rows, reach_faces=reached.reach_faces, came=came_solve, stiff_block=stiff[4:],
                        image_faces=state.image_faces)
        ins = dict(came=came_solve, picker=picker, stiff=stiff[2:4], weight=weight, residual=state.residual, reach=reached.reach,
                   v=state.v, image=state.image)
        outs = dict(u=vec, w_part=vec)
        if step > 0:
            ins.update(w=state.w, u=state.u)
            outs.update(coef=pair, s=vec, p=vec, x=vec, residual=vec)
            if not final:
                outs.update(q=vec, z_part=vec)
        if step > 1:
            ins.update(coef=coef, q=state.q, s=state.s, p=state.p, x=state.x, z=state.z)
        if final:
            def last(i, o):
                at_slots, factors, both = corrected(i)
                put_faces(o.face, at_slots)
                o.face[paired][cases:] = jnp.broadcast_to(recur(i, o, step, factors, both)[1], (8, 2 * cases))

            ins.update(rest_ins)
            outs.update(face=last_kinds)
            made = stage("last", last, ins, outs)
            vars(state).update(vars(made))
            came_image = exchange(made.face)
            break

        def apply_rest(i, o):
            at_slots, o.factors[...], o.sums[...] = corrected(i)
            put_faces(o.face, at_slots)

        made = stage("apply_rest", apply_rest, rest_ins, dict(face=face_kinds, factors=((cases, own_rows), F32), sums=pair))
        came_image = exchange(made.face)

        def update(i, o, step=step):
            part, o.sums[...] = recur(i, o, step, i.factors[...], i.both[...])
            solve_own(part, i, o)

        ins.update(factors=made.factors, both=made.sums, weighted=start.weighted, inv=inv[:4])
        outs.update(own_kinds, sums=pair)
        own = stage("update", update, ins, outs)
        vars(state).update(vars(own))
        sums = own.sums
        if step > 0:
            coef = own.coef

    def finish(i, o):
        gamma_old, alpha_old = as_columns(i.coef[...])
        w = i.w_part[...] - alpha_old * pick(joined(i.came), i.picker[...])
        gamma, delta = as_columns(both_sums([ref[...] for ref in i.everyone], 1))
        beta = gamma / gamma_old
        alpha = gamma / (delta - beta * gamma / alpha_old)
        o.solution[0] = i.x[...] + alpha * (i.u[...] + beta * i.p[...])
        o.remainder[0] = i.residual[...] - alpha * (w + beta * i.s[...])

    whole = ((1, cases, ndof), F32)
    everyone = gather(state.face[paired], came_image[paired], 1)
    done = stage(
        "finish", finish,
        dict(everyone=everyone, came=came_image, picker=picker, coef=state.coef, w_part=state.w_part, x=state.x, u=state.u, p=state.p,
             residual=state.residual, s=state.s),
        dict(solution=whole, remainder=whole))
    return done.solution, done.remainder


def solution(mesh):
    placed = (
        P(AXIS, None, None),
        P(AXIS, None, None),
        P(AXIS, None, None),
        P(AXIS, None),
        P(AXIS, None, None),
        P(AXIS, None, None),
        P(AXIS, None),
    )
    return jax.shard_map(
        local,
        mesh=mesh,
        in_specs=placed,
        out_specs=(P(AXIS, None, None), P(AXIS, None, None)),
        check_vma=False,
    )
```

```python
from types import SimpleNamespace

import jax
import jax.numpy as jnp
import numpy as np
from jax import lax
from jax.experimental import pallas as pl
from jax.experimental.pallas import tpu as pltpu
from jax.sharding import PartitionSpec as P

CYCLE = 16
ITERS = 4

BF = jnp.bfloat16
F32 = jnp.float32
NN = ((1,), (0,))
NT = ((1,), (1,))
STAGE_BYTES = 12 * 1024 * 1024
TILES = 8
AXIS = "sub"
LONGER = 64
ROOM_FOR_COPIES = pl.CostEstimate(flops=4 * 10**9, bytes_accessed=16 * 10**6, transcendentals=0)


def contract(left, right, dims=NN):
    return lax.dot_general(left, right, (dims, ((), ())), preferred_element_type=F32)


def split(value):
    high = value.astype(BF)
    return high, (value - high.astype(F32)).astype(BF)


def times(value, high, low, dims=NN):
    rows = value.shape[0]
    top, rest = split(value)
    both = contract(jnp.concatenate([top, rest], axis=0), high, dims)
    return both[:rows] + both[rows:] + contract(top, low, dims)


def pick(value, onehot, dims=NN):
    rows = value.shape[0]
    top, rest = split(value)
    last = (value - top.astype(F32) - rest.astype(F32)).astype(BF)
    parts = contract(jnp.concatenate([top, rest, last], axis=0), onehot, dims)
    return parts[:rows] + (parts[rows:2 * rows] + parts[2 * rows:])


def diagonal(count):
    first = lax.broadcasted_iota(jnp.int32, (count, count), 0)
    return first == lax.broadcasted_iota(jnp.int32, (count, count), 1)


def to_column(row):
    count = row.shape[1]
    return jnp.sum(jnp.where(diagonal(count), jnp.broadcast_to(row, (count, count)), 0), axis=1, keepdims=True)


def to_row(column):
    count = column.shape[0]
    return jnp.sum(jnp.where(diagonal(count), jnp.broadcast_to(column, (count, count)), 0), axis=0, keepdims=True)


def dot(left, right):
    return jnp.sum(left * right, axis=1, keepdims=True)


def flat(tree):
    tree = {name: held for name, held in tree.items() if not isinstance(held, list) or held}
    names = [(name, len(held) if isinstance(held, list) else 0) for name, held in tree.items()]
    entries = []
    for held in tree.values():
        entries += held if isinstance(held, list) else [held]
    return names, entries


def named(names, entries):
    space, at = SimpleNamespace(), 0
    for name, count in names:
        setattr(space, name, list(entries[at:at + count]) if count else entries[at])
        at += max(count, 1)
    return space


def stage(name, body, ins, outs, cost=None):
    in_names, arrays = flat(ins)
    out_names, kinds = flat(outs)

    def kernel(*refs):
        body(named(in_names, refs[:len(arrays)]), named(out_names, refs[len(arrays):]))

    whole = pl.BlockSpec(memory_space=pltpu.VMEM)
    made = pl.pallas_call(
        kernel,
        name=name,
        out_shape=[jax.ShapeDtypeStruct(*kind) for kind in kinds],
        in_specs=[whole] * len(arrays),
        out_specs=[whole] * len(kinds),
        compiler_params=pltpu.CompilerParams(vmem_limit_bytes=STAGE_BYTES),
        cost_estimate=cost,
    )(*arrays)
    return named(out_names, made)


def swaps(total):
    sets = []
    for by in (1, CYCLE):
        for parity in (0, 1):
            ahead = [i for i in range(total - by) if (i // by) % 2 == parity]
            sets.append((by, parity, [(i, i + by) for i in ahead] + [(i + by, i) for i in ahead]))
    return sets


def rounds_of(total):
    bits = [1 << i for i in reversed(range(total.bit_length() - 1)) if 1 << i != CYCLE]
    assert total == 1 << (len(bits) + 1)
    rounds = [[CYCLE]]
    if len(bits) % 2:
        rounds.append([bits.pop(0)])
    while bits:
        far, near = bits.pop(0), bits.pop(0)
        rounds.append([near + far, far, near])
    places = [0]
    for distances in rounds:
        places = [place ^ far for far in [0] + distances for place in places]
    return rounds, places


def local(stiffness, neumann_inv, coarse_basis, coarse_inv, loads, face_index, face_len):
    total = lax.axis_size(AXIS)
    _, cases, ndof = loads.shape
    primal = coarse_basis.shape[1]
    width = face_index.shape[2]
    known = coarse_inv.shape[1]
    half = primal // 2
    lines_a_block = half + 1
    reps = known // width
    rounds, places = rounds_of(total)

    chosen = []
    for by, parity, pairs in swaps(total):
        if pairs:
            behind, ahead = (0, 1) if by == 1 else (2, 3)
            chosen.append((pairs, behind, ahead, by, parity))
    blocks = len(chosen)
    paired = [at for at, block in enumerate(chosen) if block[3:] == (CYCLE, 0)][0]
    slots = blocks * width
    own_rows = (blocks + 1) * primal

    vec = ((cases, ndof), F32)
    faces = ((cases, slots), F32)
    pair = ((1, 2 * cases), F32)
    faces_kind = ((cases, width), F32)
    extra_rows = [lines_a_block if at == paired else LONGER if block[3:] == (1, 1) else 0 for at, block in enumerate(chosen)]
    solve_kinds = [((cases + extra, width), F32) for extra in extra_rows]

    def longer(kind):
        rows, lanes = kind[0]
        return [((rows + (8 if at == paired else 0), lanes), F32) for at in range(blocks)]

    blocked = [slice(i * width, (i + 1) * width) for i in range(blocks)]
    strips = [slice(i * ndof // TILES, (i + 1) * ndof // TILES) for i in range(TILES)]

    def joined(refs):
        return jnp.concatenate([ref[:cases] for ref in refs], axis=1)

    def put_faces(refs, value):
        rows = value.shape[0]
        for i, ref in enumerate(refs):
            ref[:rows] = value[:, blocked[i]]
            if ref.shape[0] > rows:
                ref[rows:] = jnp.zeros((ref.shape[0] - rows, width), F32)

    def exchange(arrays):
        return [lax.ppermute(array, AXIS, chosen[i][0]) for i, array in enumerate(arrays)]

    def gather(own, got, lines, beside=()):
        pieces, start = [own, got], cases
        for at, distances in enumerate(rounds[1:]):
            def join(i, o):
                o.block[...] = jnp.concatenate([ref[start:start + lines] for ref in i.pieces], axis=0)

            block = stage("join", join, dict(pieces=pieces, beside=list(beside[at:at + 1])), dict(block=((lines * len(pieces), 2 * cases), F32))).block
            pieces = [block] + [lax.ppermute(block, AXIS, [(i, i ^ far) for i in range(total)]) for far in distances]
            start, lines = 0, block.shape[0]
        return pieces

    def both_sums(pieces, stride):
        rows = []
        for piece in pieces:
            count = piece.shape[0] // stride
            rows += [piece[i * stride + stride - 1:(i + 1) * stride] for i in range(count)]
        while len(rows) > 1:
            rows = [rows[i] + rows[i + 1] for i in range(0, len(rows), 2)]
        return rows[0]

    def as_columns(row):
        return to_column(row[:, :cases]), to_column(row[:, cases:])

    def first(i, o):
        me = lax.axis_index(AXIS)
        index, lengths = i.index[0], i.lengths[...]
        lane = lax.broadcasted_iota(jnp.int32, (1, width), 1)
        rows = []
        for _, behind, ahead, by, parity in chosen:
            forward = (me // by) % 2 == parity
            row = jnp.where(forward, index[ahead:ahead + 1], index[behind:behind + 1])
            length = jnp.where(forward, lengths[:, ahead:ahead + 1], lengths[:, behind:behind + 1])
            rows.append(jnp.where(lane < length, row, -1))
        row = jnp.concatenate(rows, axis=1)
        unpicker = (lax.broadcasted_iota(jnp.int32, (ndof, slots), 0) == row).astype(F32).astype(BF)
        picker = (lax.broadcasted_iota(jnp.int32, (slots, ndof), 1) == to_column(row)).astype(F32)
        weight = 1.0 / (1.0 + jnp.sum(picker, axis=0, keepdims=True))
        weighted = i.basis[0] * weight
        at_slots = pick(jnp.concatenate([i.load[0], weighted], axis=0), unpicker)
        inv = i.inv[...]
        inv_packed = jnp.concatenate([inv[:, j * width:(j + 1) * width] for j in range(reps)], axis=0)
        put_faces(o.face, jnp.concatenate([at_slots, jnp.concatenate([inv_packed] * blocks, axis=1)], axis=0))
        o.picker[...] = picker.astype(BF)
        o.unpicker[...] = unpicker
        o.weight[...] = weight
        o.weighted[...] = weighted
        o.basis_slots[...] = at_slots[cases:]

    def lead(i, o):
        o.ready[...] = jnp.zeros((8, width), F32)

    packed = ((cases + primal + reps * primal, width), F32)
    ready = stage("lead", lead, dict(), dict(ready=((8, width), F32)), cost=ROOM_FOR_COPIES).ready
    start = stage(
        "first", first,
        dict(ready=ready, lengths=face_len, index=face_index, basis=coarse_basis, load=loads, inv=coarse_inv),
        dict(face=longer(packed), picker=((slots, ndof), BF), unpicker=((ndof, slots), BF), weight=((1, ndof), F32),
             weighted=((primal, ndof), F32), basis_slots=((primal, slots), F32)),
        cost=ROOM_FOR_COPIES)
    weight, picker, unpicker = start.weight, start.picker, start.unpicker
    came = exchange(start.face)

    part_kinds = [((ndof, ndof), BF)] * 2 + [((slots, ndof), BF)] * 2 + [((slots, slots), BF)] * 2

    def prepare(name, matrix):
        def body(i, o):
            for strip in strips:
                o.parts[0][strip], o.parts[1][strip] = split(i.matrix[0, strip])
            for at in range(2):
                face = contract(i.picker[...], o.parts[at][...]).astype(BF)
                o.parts[2 + at][...] = face
                o.parts[4 + at][...] = contract(face, i.unpicker[...]).astype(BF)

        return stage(name, body, dict(matrix=matrix, picker=picker, unpicker=unpicker), dict(parts=part_kinds)).parts

    inv = prepare("prepare_inv", neumann_inv)
    stiff = prepare("prepare_stiff", stiffness)

    own_kinds = dict(lines=((primal, cases), F32), inner_faces=faces, inner=vec)

    def solve_own(part, i, o):
        scaled = part * i.weight[...]
        o.lines[...] = times(i.weighted[...], *split(part), NT)
        o.inner_faces[...] = times(scaled, i.inv[2][...], i.inv[3][...], NT)
        o.inner[...] = times(scaled, i.inv[0][...], i.inv[1][...])

    def loads_faces(i, o):
        o.lines[...] = times(i.weighted[...], *split(i.load[0]), NT)
        o.inner_faces[...] = times(i.load[0] * i.weight[...], i.inv[0][...], i.inv[1][...], NT)

    def loads_inner(i, o):
        o.inner[...] = times(i.load[0] * i.weight[...], i.inv[0][...], i.inv[1][...])

    own = stage("loads_faces", loads_faces, dict(load=loads, weight=weight, weighted=start.weighted, inv=inv[2:4]),
                dict(lines=own_kinds["lines"], inner_faces=faces))
    own.inner = stage("loads_inner", loads_inner, dict(load=loads, weight=weight, inv=inv[:2]), dict(inner=vec)).inner

    def reach(i, o):
        functions, rows = [i.weighted[...]], [i.inv[...]]
        for j in range(blocks):
            part = i.came[j][...]
            functions.append(pick(part[cases:cases + primal], i.picker[blocked[j]]))
            rest = part[cases + primal:]
            rows.append(jnp.concatenate([rest[k * primal:(k + 1) * primal] for k in range(reps)], axis=1))
        functions = jnp.concatenate(functions, axis=0)
        rows = jnp.concatenate(rows, axis=0)
        image = times(functions, i.stiff[0][...], i.stiff[1][...])
        image_faces = times(functions, i.stiff[2][...], i.stiff[3][...], NT)
        o.reach[0][...], o.reach[1][...] = split(jnp.concatenate([functions, image], axis=1))
        o.reach_faces[0][...], o.reach_faces[1][...] = split(image_faces)
        me = lax.axis_index(AXIS)
        count = i.place.shape[1]
        for upper in range(2):
            for at in range(0, count, 256):
                lanes = slice(at, min(at + 256, count))
                device, line = i.place[:, lanes] ^ me, i.line[:, lanes]
                source = jnp.where(line < half, device * primal + upper * half + line, -1)
                move = lax.broadcasted_iota(jnp.int32, (known, lanes.stop - at), 0) == source
                o.rows[upper * own_rows:(upper + 1) * own_rows, lanes] = pick(rows, move.astype(F32).astype(BF))

    place = jnp.asarray(np.repeat(np.array(places, np.int32), lines_a_block)[None])
    line = jnp.asarray(np.tile(np.arange(lines_a_block, dtype=np.int32), total)[None])
    reached = stage(
        "reach", reach,
        dict(weighted=start.weighted, inv=coarse_inv, came=came, picker=picker, stiff=stiff[:4], place=place, line=line),
        dict(reach=[((own_rows, 2 * ndof), BF)] * 2, reach_faces=[((own_rows, slots), BF)] * 2, rows=((2 * own_rows, total * lines_a_block), F32)))

    def to_solve(came, own, coef=None, sums=None):
        def body(i, o):
            arrived = joined(i.came)
            if coef is not None:
                arrived = to_column(i.coef[:, cases:]) * -arrived
            lines = i.lines[...] + times(i.basis_slots[...], *split(arrived), NT)
            put_faces(o.face, 0.5 * (i.inner_faces[...] + times(0.5 * arrived, i.inv[0][...], i.inv[1][...])))
            o.face[paired][cases:cases + half] = jnp.concatenate([lines[:half], lines[half:]], axis=1)
            o.face[paired][cases + half:] = i.sums[...] if sums is not None else jnp.zeros((1, 2 * cases), F32)

        ins = dict(came=came, basis_slots=start.basis_slots, lines=own.lines, inner_faces=own.inner_faces, inv=inv[4:])
        if coef is not None:
            ins.update(coef=coef)
        if sums is not None:
            ins.update(sums=sums)
        made = stage("solve_rest", body, ins, dict(face=solve_kinds))
        return made.face[paired], exchange(made.face)

    def to_apply(step, came, own, state, coef):
        def body(i, o):
            arrived = joined(i.came)
            if step == 0:
                o.residual[...] = i.load[0] + pick(arrived, i.picker[...])
            else:
                if step > 1:
                    o.z[...] = i.z_part[...] + pick(arrived, i.picker[...])
                    arrived = to_column(i.coef[:, cases:]) * -arrived
                o.w[...] = i.w_part[...] + pick(arrived, i.picker[...])
            inner = i.weight[...] * (i.inner[...] + times(0.5 * arrived, i.inv[0][...], i.inv[1][...]))
            o.v[...] = inner
            o.image_faces[...] = times(inner, i.stiff[2][...], i.stiff[3][...], NT)
            o.image[...] = times(inner, i.stiff[0][...], i.stiff[1][...])

        ins = dict(came=came, picker=picker, weight=weight, inner=own.inner, inv=inv[2:4], stiff=stiff[:4])
        outs = dict(v=vec, image_faces=faces, image=vec)
        if step == 0:
            ins.update(load=loads)
            outs.update(residual=vec)
        else:
            ins.update(w_part=state.w_part)
            outs.update(w=vec)
        if step > 1:
            ins.update(z_part=state.z_part, coef=coef)
            outs.update(z=vec)
        return stage("apply_own", body, ins, outs)

    def corrected(i):
        rows = jnp.concatenate([ref[...] for ref in i.everyone], axis=0)
        product = times(i.rows[...], *split(rows))
        factors = (product[:own_rows, :cases] + product[own_rows:, cases:]).T
        at_slots = i.image_faces[...] + times(joined(i.came), i.stiff_block[0][...], i.stiff_block[1][...])
        both = both_sums([ref[...] for ref in i.everyone], lines_a_block)
        return at_slots + times(factors, i.reach_faces[0][...], i.reach_faces[1][...]), factors, both

    def recur(i, o, step, factors, both):
        arrived = joined(i.came)
        extra = times(factors, i.reach[0][...], i.reach[1][...])
        inner = i.v[...] + pick(arrived, i.picker[...]) + extra[:, :ndof]
        image = i.image[...] + times(arrived, i.stiff[0][...], i.stiff[1][...]) + extra[:, ndof:]
        weight = i.weight[...]
        if step == 0:
            part, u, residual = image, inner, i.residual[...]
            delta = dot(image, u)
        else:
            gamma, delta = as_columns(both)
            w = i.w[...]
            if step == 1:
                alpha = gamma / delta
                q, s, p = inner, w, i.u[...]
                x = alpha * p
                before = w
            else:
                gamma_old, alpha_old = as_columns(i.coef[...])
                beta = gamma / gamma_old
                alpha = gamma / (delta - beta * gamma / alpha_old)
                q = inner + beta * i.q[...]
                s = w + beta * i.s[...]
                p = i.u[...] + beta * i.p[...]
                x = i.x[...] + alpha * p
                before = w - (alpha * beta) * i.z[...]
            residual = i.residual[...] - alpha * s
            u = i.u[...] - alpha * q
            part = before - alpha * image
            delta = dot(weight * before - alpha * image, u)
            o.coef[...] = jnp.concatenate([both[:, :cases], to_row(alpha)], axis=1)
            o.s[...], o.p[...], o.x[...], o.residual[...] = s, p, x, residual
            if step + 1 < ITERS:
                o.q[...] = q
                o.z_part[...] = image if step == 1 else image + beta * i.z[...]
        o.u[...] = u
        o.w_part[...] = part
        return part, jnp.concatenate([to_row(dot(weight * residual, u)), to_row(delta)], axis=1)

    state = SimpleNamespace()
    came_image, coef, sums = came, None, None
    for step in range(ITERS):
        final = step + 1 == ITERS
        sent, came_solve = to_solve(came_image, own, coef, sums)
        applied = to_apply(step, came_image, own, state, coef)
        vars(state).update(vars(applied))
        everyone = gather(sent, came_solve[paired], lines_a_block, (stiff[4], reached.rows) if step == 0 else ())
        rest_ins = dict(everyone=everyone, rows=reached.rows, reach_faces=reached.reach_faces, came=came_solve, stiff_block=stiff[4:],
                        image_faces=state.image_faces)
        ins = dict(came=came_solve, picker=picker, stiff=stiff[2:4], weight=weight, residual=state.residual, reach=reached.reach,
                   v=state.v, image=state.image)
        outs = dict(u=vec, w_part=vec)
        if step > 0:
            ins.update(w=state.w, u=state.u)
            outs.update(coef=pair, s=vec, p=vec, x=vec, residual=vec)
            if not final:
                outs.update(q=vec, z_part=vec)
        if step > 1:
            ins.update(coef=coef, q=state.q, s=state.s, p=state.p, x=state.x, z=state.z)
        if final:
            def last(i, o):
                at_slots, factors, both = corrected(i)
                put_faces(o.face, at_slots)
                o.face[paired][cases:] = jnp.broadcast_to(recur(i, o, step, factors, both)[1], (8, 2 * cases))

            ins.update(rest_ins)
            outs.update(face=longer(faces_kind))
            made = stage("last", last, ins, outs)
            vars(state).update(vars(made))
            came_image = exchange(made.face)
            break

        def apply_rest(i, o):
            at_slots, o.factors[...], o.sums[...] = corrected(i)
            put_faces(o.face, at_slots)

        made = stage("apply_rest", apply_rest, rest_ins, dict(face=longer(faces_kind), factors=((cases, own_rows), F32), sums=pair))
        came_image = exchange(made.face)

        def update(i, o, step=step):
            part, o.sums[...] = recur(i, o, step, i.factors[...], i.both[...])
            solve_own(part, i, o)

        ins.update(factors=made.factors, both=made.sums, weighted=start.weighted, inv=inv[:4])
        outs.update(own_kinds, sums=pair)
        own = stage("update", update, ins, outs)
        vars(state).update(vars(own))
        sums = own.sums
        if step > 0:
            coef = own.coef

    def finish(i, o):
        gamma_old, alpha_old = as_columns(i.coef[...])
        w = i.w_part[...] - alpha_old * pick(joined(i.came), i.picker[...])
        gamma, delta = as_columns(both_sums([ref[...] for ref in i.everyone], 1))
        beta = gamma / gamma_old
        alpha = gamma / (delta - beta * gamma / alpha_old)
        o.solution[0] = i.x[...] + alpha * (i.u[...] + beta * i.p[...])
        o.remainder[0] = i.residual[...] - alpha * (w + beta * i.s[...])

    whole = ((1, cases, ndof), F32)
    everyone = gather(state.face[paired], came_image[paired], 1)
    done = stage(
        "finish", finish,
        dict(everyone=everyone, came=came_image, picker=picker, coef=state.coef, w_part=state.w_part, x=state.x, u=state.u, p=state.p,
             residual=state.residual, s=state.s),
        dict(solution=whole, remainder=whole))
    return done.solution, done.remainder


def solution(mesh):
    placed = (
        P(AXIS, None, None),
        P(AXIS, None, None),
        P(AXIS, None, None),
        P(AXIS, None),
        P(AXIS, None, None),
        P(AXIS, None, None),
        P(AXIS, None),
    )
    return jax.shard_map(
        local,
        mesh=mesh,
        in_specs=placed,
        out_specs=(P(AXIS, None, None), P(AXIS, None, None)),
        check_vma=False,
    )
```

```python
from types import SimpleNamespace

import jax
import jax.numpy as jnp
import numpy as np
from jax import lax
from jax.experimental import pallas as pl
from jax.experimental.pallas import tpu as pltpu
from jax.sharding import PartitionSpec as P

CYCLE = 16
ITERS = 4

BF = jnp.bfloat16
F32 = jnp.float32
NN = ((1,), (0,))
NT = ((1,), (1,))
STAGE_BYTES = 12 * 1024 * 1024
TILES = 8
AXIS = "sub"
LONGER = 64
ROOM_FOR_COPIES = pl.CostEstimate(flops=4 * 10**9, bytes_accessed=16 * 10**6, transcendentals=0)


def contract(left, right, dims=NN):
    return lax.dot_general(left, right, (dims, ((), ())), preferred_element_type=F32)


def split(value):
    high = value.astype(BF)
    return high, (value - high.astype(F32)).astype(BF)


def in_three(value):
    top, rest = split(value)
    return top, rest, (value - top.astype(F32) - rest.astype(F32)).astype(BF)


def times(value, high, low, dims=NN, lowest=None):
    rows = value.shape[0]
    top, rest, last = in_three(value)
    first = contract(jnp.concatenate([top, rest, last], axis=0), high, dims)
    second = contract(jnp.concatenate([top, rest], axis=0), low, dims)
    small = first[2 * rows:] + second[rows:]
    if lowest is not None:
        small += contract(top, lowest, dims)
    return first[:rows] + (first[rows:2 * rows] + second[:rows] + small)


def product(left, right, dims=NN):
    high, low, lowest = in_three(right)
    return times(left, high, low, dims, lowest)


def pick(value, onehot, dims=NN):
    rows = value.shape[0]
    parts = contract(jnp.concatenate(in_three(value), axis=0), onehot, dims)
    return parts[:rows] + (parts[rows:2 * rows] + parts[2 * rows:])


def diagonal(count):
    first = lax.broadcasted_iota(jnp.int32, (count, count), 0)
    return first == lax.broadcasted_iota(jnp.int32, (count, count), 1)


def to_column(row):
    count = row.shape[1]
    return jnp.sum(jnp.where(diagonal(count), jnp.broadcast_to(row, (count, count)), 0), axis=1, keepdims=True)


def to_row(column):
    count = column.shape[0]
    return jnp.sum(jnp.where(diagonal(count), jnp.broadcast_to(column, (count, count)), 0), axis=0, keepdims=True)


def dot(left, right):
    return jnp.sum(left * right, axis=1, keepdims=True)


def flat(tree):
    tree = {name: held for name, held in tree.items() if not isinstance(held, list) or held}
    names = [(name, len(held) if isinstance(held, list) else 0) for name, held in tree.items()]
    entries = []
    for held in tree.values():
        entries += held if isinstance(held, list) else [held]
    return names, entries


def named(names, entries):
    space, at = SimpleNamespace(), 0
    for name, count in names:
        setattr(space, name, list(entries[at:at + count]) if count else entries[at])
        at += max(count, 1)
    return space


def stage(name, body, ins, outs, cost=None):
    in_names, arrays = flat(ins)
    out_names, kinds = flat(outs)

    def kernel(*refs):
        body(named(in_names, refs[:len(arrays)]), named(out_names, refs[len(arrays):]))

    whole = pl.BlockSpec(memory_space=pltpu.VMEM)
    made = pl.pallas_call(
        kernel,
        name=name,
        out_shape=[jax.ShapeDtypeStruct(*kind) for kind in kinds],
        in_specs=[whole] * len(arrays),
        out_specs=[whole] * len(kinds),
        compiler_params=pltpu.CompilerParams(vmem_limit_bytes=STAGE_BYTES),
        cost_estimate=cost,
    )(*arrays)
    return named(out_names, made)


def swaps(total):
    sets = []
    for by in (1, CYCLE):
        for parity in (0, 1):
            ahead = [i for i in range(total - by) if (i // by) % 2 == parity]
            sets.append((by, parity, [(i, i + by) for i in ahead] + [(i + by, i) for i in ahead]))
    return sets


def rounds_of(total):
    bits = [1 << i for i in reversed(range(total.bit_length() - 1)) if 1 << i != CYCLE]
    assert total == 1 << (len(bits) + 1)
    rounds = [[CYCLE]]
    if len(bits) % 2:
        rounds.append([bits.pop(0)])
    middle = len(bits) // 2
    for far, near in zip(bits[:middle], bits[middle:]):
        rounds.append([near + far, far, near])
    places = [0]
    for distances in rounds:
        places = [place ^ far for far in [0] + distances for place in places]
    return rounds, places


def local(stiffness, neumann_inv, coarse_basis, coarse_inv, loads, face_index, face_len):
    total = lax.axis_size(AXIS)
    _, cases, ndof = loads.shape
    primal = coarse_basis.shape[1]
    width = face_index.shape[2]
    known = coarse_inv.shape[1]
    half = primal // 2
    lines_a_block = half + 1
    reps = known // width
    rounds, places = rounds_of(total)

    chosen = []
    for by, parity, pairs in swaps(total):
        if pairs:
            behind, ahead = (0, 1) if by == 1 else (2, 3)
            chosen.append((pairs, behind, ahead, by, parity))
    blocks = len(chosen)
    paired = [at for at, block in enumerate(chosen) if block[3:] == (CYCLE, 0)][0]
    slots = blocks * width
    own_rows = (blocks + 1) * primal

    vec = ((cases, ndof), F32)
    faces = ((cases, slots), F32)
    pair = ((1, 2 * cases), F32)
    faces_kind = ((cases, width), F32)
    extra_rows = [lines_a_block if at == paired else LONGER if block[3:] == (1, 1) else 0 for at, block in enumerate(chosen)]
    solve_kinds = [((cases + extra, width), F32) for extra in extra_rows]

    def longer(kind):
        rows, lanes = kind[0]
        return [((rows + (8 if at == paired else 0), lanes), F32) for at in range(blocks)]

    blocked = [slice(i * width, (i + 1) * width) for i in range(blocks)]
    strips = [slice(i * ndof // TILES, (i + 1) * ndof // TILES) for i in range(TILES)]

    def joined(refs):
        return jnp.concatenate([ref[:cases] for ref in refs], axis=1)

    def put_faces(refs, value):
        rows = value.shape[0]
        for i, ref in enumerate(refs):
            ref[:rows] = value[:, blocked[i]]
            if ref.shape[0] > rows:
                ref[rows:] = jnp.zeros((ref.shape[0] - rows, width), F32)

    def exchange(arrays):
        return [lax.ppermute(array, AXIS, chosen[i][0]) for i, array in enumerate(arrays)]

    def gather(own, got, lines, beside=()):
        pieces, start = [own, got], cases
        for at, distances in enumerate(rounds[1:]):
            def join(i, o):
                o.block[...] = jnp.concatenate([ref[start:start + lines] for ref in i.pieces], axis=0)

            block = stage("join", join, dict(pieces=pieces, beside=beside[at] if at < len(beside) else []), dict(block=((lines * len(pieces), 2 * cases), F32))).block
            pieces = [block] + [lax.ppermute(block, AXIS, [(i, i ^ far) for i in range(total)]) for far in distances]
            start, lines = 0, block.shape[0]
        return pieces

    def both_sums(pieces, stride):
        rows = []
        for piece in pieces:
            count = piece.shape[0] // stride
            rows += [piece[i * stride + stride - 1:(i + 1) * stride] for i in range(count)]
        while len(rows) > 1:
            rows = [rows[i] + rows[i + 1] for i in range(0, len(rows), 2)]
        return rows[0]

    def as_columns(row):
        return to_column(row[:, :cases]), to_column(row[:, cases:])

    def first(i, o):
        me = lax.axis_index(AXIS)
        index, lengths = i.index[0], i.lengths[...]
        lane = lax.broadcasted_iota(jnp.int32, (1, width), 1)
        rows = []
        for _, behind, ahead, by, parity in chosen:
            forward = (me // by) % 2 == parity
            row = jnp.where(forward, index[ahead:ahead + 1], index[behind:behind + 1])
            length = jnp.where(forward, lengths[:, ahead:ahead + 1], lengths[:, behind:behind + 1])
            rows.append(jnp.where(lane < length, row, -1))
        row = jnp.concatenate(rows, axis=1)
        unpicker = (lax.broadcasted_iota(jnp.int32, (ndof, slots), 0) == row).astype(F32).astype(BF)
        picker = (lax.broadcasted_iota(jnp.int32, (slots, ndof), 1) == to_column(row)).astype(F32)
        weight = 1.0 / (1.0 + jnp.sum(picker, axis=0, keepdims=True))
        weighted = i.basis[0] * weight
        at_slots = pick(jnp.concatenate([i.load[0], weighted], axis=0), unpicker)
        inv = i.inv[...]
        inv_packed = jnp.concatenate([inv[:, j * width:(j + 1) * width] for j in range(reps)], axis=0)
        put_faces(o.face, jnp.concatenate([at_slots, jnp.concatenate([inv_packed] * blocks, axis=1)], axis=0))
        o.picker[...] = picker.astype(BF)
        o.unpicker[...] = unpicker
        o.weight[...] = weight
        o.weighted[...] = weighted
        o.basis_slots[...] = at_slots[cases:]

    def lead(i, o):
        o.ready[...] = jnp.zeros((8, width), F32)

    packed = ((cases + primal + reps * primal, width), F32)
    ready = stage("lead", lead, dict(), dict(ready=((8, width), F32)), cost=ROOM_FOR_COPIES).ready
    start = stage(
        "first", first,
        dict(ready=ready, lengths=face_len, index=face_index, basis=coarse_basis, load=loads, inv=coarse_inv),
        dict(face=longer(packed), picker=((slots, ndof), BF), unpicker=((ndof, slots), BF), weight=((1, ndof), F32),
             weighted=((primal, ndof), F32), basis_slots=((primal, slots), F32)),
        cost=ROOM_FOR_COPIES)
    weight, picker, unpicker = start.weight, start.picker, start.unpicker
    came = exchange(start.face)

    part_kinds = [((ndof, ndof), BF)] * 2 + [((slots, ndof), BF)] * 2 + [((slots, slots), BF)] * 2

    def prepare(name, matrix):
        def body(i, o):
            for strip in strips:
                o.parts[0][strip], o.parts[1][strip] = split(i.matrix[0, strip])
            for at in range(2):
                face = contract(i.picker[...], o.parts[at][...]).astype(BF)
                o.parts[2 + at][...] = face
                o.parts[4 + at][...] = contract(face, i.unpicker[...]).astype(BF)

        return stage(name, body, dict(matrix=matrix, picker=picker, unpicker=unpicker), dict(parts=part_kinds)).parts

    inv = prepare("prepare_inv", neumann_inv)
    stiff = prepare("prepare_stiff", stiffness)

    own_kinds = dict(lines=((primal, cases), F32), inner_faces=faces, inner=vec)

    def solve_own(part, i, o):
        scaled = part * i.weight[...]
        o.lines[...] = product(i.weighted[...], part, NT)
        o.inner_faces[...] = times(scaled, i.inv[2][...], i.inv[3][...], NT)
        o.inner[...] = times(scaled, i.inv[0][...], i.inv[1][...])

    def loads_faces(i, o):
        o.lines[...] = product(i.weighted[...], i.load[0], NT)
        o.inner_faces[...] = times(i.load[0] * i.weight[...], i.inv[0][...], i.inv[1][...], NT)

    def loads_inner(i, o):
        o.inner[...] = times(i.load[0] * i.weight[...], i.inv[0][...], i.inv[1][...])

    own = stage("loads_faces", loads_faces, dict(load=loads, weight=weight, weighted=start.weighted, inv=inv[2:4]),
                dict(lines=own_kinds["lines"], inner_faces=faces))
    own.inner = stage("loads_inner", loads_inner, dict(load=loads, weight=weight, inv=inv[:2]), dict(inner=vec)).inner

    def reach(i, o):
        functions, rows = [i.weighted[...]], [i.inv[...]]
        for j in range(blocks):
            part = i.came[j][...]
            functions.append(pick(part[cases:cases + primal], i.picker[blocked[j]]))
            rest = part[cases + primal:]
            rows.append(jnp.concatenate([rest[k * primal:(k + 1) * primal] for k in range(reps)], axis=1))
        functions = jnp.concatenate(functions, axis=0)
        rows = jnp.concatenate(rows, axis=0)
        image = times(functions, i.stiff[0][...], i.stiff[1][...])
        image_faces = times(functions, i.stiff[2][...], i.stiff[3][...], NT)
        o.reach[0][...], o.reach[1][...] = split(jnp.concatenate([functions, image], axis=1))
        o.reach_faces[0][...], o.reach_faces[1][...] = split(image_faces)
        me = lax.axis_index(AXIS)
        count = i.place.shape[1]
        for upper in range(2):
            for at in range(0, count, 256):
                lanes = slice(at, min(at + 256, count))
                device, line = i.place[:, lanes] ^ me, i.line[:, lanes]
                source = jnp.where(line < half, device * primal + upper * half + line, -1)
                move = lax.broadcasted_iota(jnp.int32, (known, lanes.stop - at), 0) == source
                o.rows[upper * own_rows:(upper + 1) * own_rows, lanes] = pick(rows, move.astype(F32).astype(BF))

    place = jnp.asarray(np.repeat(np.array(places, np.int32), lines_a_block)[None])
    line = jnp.asarray(np.tile(np.arange(lines_a_block, dtype=np.int32), total)[None])
    reached = stage(
        "reach", reach,
        dict(weighted=start.weighted, inv=coarse_inv, came=came, picker=picker, stiff=stiff[:4], place=place, line=line),
        dict(reach=[((own_rows, 2 * ndof), BF)] * 2, reach_faces=[((own_rows, slots), BF)] * 2, rows=((2 * own_rows, total * lines_a_block), F32)))

    def to_solve(came, own, coef=None, sums=None):
        def body(i, o):
            arrived = joined(i.came)
            if coef is not None:
                arrived = to_column(i.coef[:, cases:]) * -arrived
            lines = i.lines[...] + product(i.basis_slots[...], arrived, NT)
            put_faces(o.face, 0.5 * (i.inner_faces[...] + times(0.5 * arrived, i.inv[0][...], i.inv[1][...])))
            o.face[paired][cases:cases + half] = jnp.concatenate([lines[:half], lines[half:]], axis=1)
            o.face[paired][cases + half:] = i.sums[...] if sums is not None else jnp.zeros((1, 2 * cases), F32)

        ins = dict(came=came, basis_slots=start.basis_slots, lines=own.lines, inner_faces=own.inner_faces, inv=inv[4:])
        if coef is not None:
            ins.update(coef=coef)
        if sums is not None:
            ins.update(sums=sums)
        made = stage("solve_rest", body, ins, dict(face=solve_kinds))
        return made.face[paired], exchange(made.face)

    def to_apply(step, came, own, state, coef):
        def body(i, o):
            arrived = joined(i.came)
            if step == 0:
                o.residual[...] = i.load[0] + pick(arrived, i.picker[...])
            else:
                if step > 1:
                    o.z[...] = i.z_part[...] + pick(arrived, i.picker[...])
                    arrived = to_column(i.coef[:, cases:]) * -arrived
                o.w[...] = i.w_part[...] + pick(arrived, i.picker[...])
            inner = i.weight[...] * (i.inner[...] + times(0.5 * arrived, i.inv[0][...], i.inv[1][...]))
            o.v[...] = inner
            o.image_faces[...] = times(inner, i.stiff[2][...], i.stiff[3][...], NT)
            o.image[...] = times(inner, i.stiff[0][...], i.stiff[1][...])

        ins = dict(came=came, picker=picker, weight=weight, inner=own.inner, inv=inv[2:4], stiff=stiff[:4])
        outs = dict(v=vec, image_faces=faces, image=vec)
        if step == 0:
            ins.update(load=loads)
            outs.update(residual=vec)
        else:
            ins.update(w_part=state.w_part)
            outs.update(w=vec)
        if step > 1:
            ins.update(z_part=state.z_part, coef=coef)
            outs.update(z=vec)
        return stage("apply_own", body, ins, outs)

    def corrected(i):
        rows = jnp.concatenate([ref[...] for ref in i.everyone], axis=0)
        halves = product(i.rows[...], rows)
        factors = (halves[:own_rows, :cases] + halves[own_rows:, cases:]).T
        at_slots = i.image_faces[...] + times(joined(i.came), i.stiff_block[0][...], i.stiff_block[1][...])
        both = both_sums([ref[...] for ref in i.everyone], lines_a_block)
        return at_slots + times(factors, i.reach_faces[0][...], i.reach_faces[1][...]), factors, both

    def recur(i, o, step, factors, both):
        arrived = joined(i.came)
        extra = times(factors, i.reach[0][...], i.reach[1][...])
        inner = i.v[...] + pick(arrived, i.picker[...]) + extra[:, :ndof]
        image = i.image[...] + times(arrived, i.stiff[0][...], i.stiff[1][...]) + extra[:, ndof:]
        weight = i.weight[...]
        if step == 0:
            part, u, residual = image, inner, i.residual[...]
            delta = dot(image, u)
        else:
            gamma, delta = as_columns(both)
            w = i.w[...]
            if step == 1:
                alpha = gamma / delta
                q, s, p = inner, w, i.u[...]
                x = alpha * p
                before = w
            else:
                gamma_old, alpha_old = as_columns(i.coef[...])
                beta = gamma / gamma_old
                alpha = gamma / (delta - beta * gamma / alpha_old)
                q = inner + beta * i.q[...]
                s = w + beta * i.s[...]
                p = i.u[...] + beta * i.p[...]
                x = i.x[...] + alpha * p
                before = w - (alpha * beta) * i.z[...]
            residual = i.residual[...] - alpha * s
            u = i.u[...] - alpha * q
            part = before - alpha * image
            delta = dot(weight * before - alpha * image, u)
            o.coef[...] = jnp.concatenate([both[:, :cases], to_row(alpha)], axis=1)
            o.s[...], o.p[...], o.x[...], o.residual[...] = s, p, x, residual
            if step + 1 < ITERS:
                o.q[...] = q
                o.z_part[...] = image if step == 1 else image + beta * i.z[...]
        o.u[...] = u
        o.w_part[...] = part
        return part, jnp.concatenate([to_row(dot(weight * residual, u)), to_row(delta)], axis=1)

    state = SimpleNamespace()
    came_image, coef, sums = came, None, None
    for step in range(ITERS):
        final = step + 1 == ITERS
        sent, came_solve = to_solve(came_image, own, coef, sums)
        applied = to_apply(step, came_image, own, state, coef)
        vars(state).update(vars(applied))
        everyone = gather(sent, came_solve[paired], lines_a_block, ([stiff[4]], [reached.rows, own.inner]) if step == 0 else ())
        rest_ins = dict(everyone=everyone, rows=reached.rows, reach_faces=reached.reach_faces, came=came_solve, stiff_block=stiff[4:],
                        image_faces=state.image_faces)
        ins = dict(came=came_solve, picker=picker, stiff=stiff[2:4], weight=weight, residual=state.residual, reach=reached.reach,
                   v=state.v, image=state.image)
        outs = dict(u=vec, w_part=vec)
        if step > 0:
            ins.update(w=state.w, u=state.u)
            outs.update(coef=pair, s=vec, p=vec, x=vec, residual=vec)
            if not final:
                outs.update(q=vec, z_part=vec)
        if step > 1:
            ins.update(coef=coef, q=state.q, s=state.s, p=state.p, x=state.x, z=state.z)
        if final:
            def last(i, o):
                at_slots, factors, both = corrected(i)
                put_faces(o.face, at_slots)
                o.face[paired][cases:] = jnp.broadcast_to(recur(i, o, step, factors, both)[1], (8, 2 * cases))

            ins.update(rest_ins)
            outs.update(face=longer(faces_kind))
            made = stage("last", last, ins, outs)
            vars(state).update(vars(made))
            came_image = exchange(made.face)
            break

        def apply_rest(i, o):
            at_slots, o.factors[...], o.sums[...] = corrected(i)
            put_faces(o.face, at_slots)

        made = stage("apply_rest", apply_rest, rest_ins, dict(face=longer(faces_kind), factors=((cases, own_rows), F32), sums=pair))
        came_image = exchange(made.face)

        def update(i, o, step=step):
            part, o.sums[...] = recur(i, o, step, i.factors[...], i.both[...])
            solve_own(part, i, o)

        ins.update(factors=made.factors, both=made.sums, weighted=start.weighted, inv=inv[:4])
        outs.update(own_kinds, sums=pair)
        own = stage("update", update, ins, outs)
        vars(state).update(vars(own))
        sums = own.sums
        if step > 0:
            coef = own.coef

    def settle(i, o):
        alpha_old = as_columns(i.coef[...])[1]
        o.w[...] = i.w_part[...] - alpha_old * pick(joined(i.came), i.picker[...])

    def finish(i, o):
        gamma_old, alpha_old = as_columns(i.coef[...])
        gamma, delta = as_columns(both_sums([ref[...] for ref in i.everyone], 1))
        beta = gamma / gamma_old
        alpha = gamma / (delta - beta * gamma / alpha_old)
        o.solution[0] = i.x[...] + alpha * (i.u[...] + beta * i.p[...])
        o.remainder[0] = i.residual[...] - alpha * (i.w[...] + beta * i.s[...])

    whole = ((1, cases, ndof), F32)
    everyone = gather(state.face[paired], came_image[paired], 1)
    w = stage("settle", settle, dict(came=came_image, picker=picker, coef=state.coef, w_part=state.w_part), dict(w=vec)).w
    done = stage(
        "finish", finish,
        dict(everyone=everyone, coef=state.coef, w=w, x=state.x, u=state.u, p=state.p, residual=state.residual, s=state.s),
        dict(solution=whole, remainder=whole))
    return done.solution, done.remainder


def solution(mesh):
    placed = (
        P(AXIS, None, None),
        P(AXIS, None, None),
        P(AXIS, None, None),
        P(AXIS, None),
        P(AXIS, None, None),
        P(AXIS, None, None),
        P(AXIS, None),
    )
    return jax.shard_map(
        local,
        mesh=mesh,
        in_specs=placed,
        out_specs=(P(AXIS, None, None), P(AXIS, None, None)),
        check_vma=False,
    )
```

```python
from types import SimpleNamespace

import jax
import jax.numpy as jnp
import numpy as np
from jax import lax
from jax.experimental import pallas as pl
from jax.experimental.pallas import tpu as pltpu
from jax.sharding import PartitionSpec as P

CYCLE = 16
ITERS = 4

BF = jnp.bfloat16
F32 = jnp.float32
NN = ((1,), (0,))
NT = ((1,), (1,))
STAGE_BYTES = 12 * 1024 * 1024
TILES = 8
AXIS = "sub"
LONGER = 32
ROOM_FOR_COPIES = pl.CostEstimate(flops=4 * 10**9, bytes_accessed=16 * 10**6, transcendentals=0)


def contract(left, right, dims=NN):
    return lax.dot_general(left, right, (dims, ((), ())), preferred_element_type=F32)


def split(value):
    high = value.astype(BF)
    return high, (value - high.astype(F32)).astype(BF)


def in_three(value):
    top, rest = split(value)
    return top, rest, (value - top.astype(F32) - rest.astype(F32)).astype(BF)


def times(value, high, low, dims=NN, lowest=None):
    rows = value.shape[0]
    top, rest, last = in_three(value)
    first = contract(jnp.concatenate([top, rest, last], axis=0), high, dims)
    second = contract(jnp.concatenate([top, rest], axis=0), low, dims)
    small = first[2 * rows:] + second[rows:]
    if lowest is not None:
        small += contract(top, lowest, dims)
    return first[:rows] + (first[rows:2 * rows] + second[:rows] + small)


def product(left, right, dims=NN):
    high, low, lowest = in_three(right)
    return times(left, high, low, dims, lowest)


def pick(value, onehot, dims=NN):
    rows = value.shape[0]
    parts = contract(jnp.concatenate(in_three(value), axis=0), onehot, dims)
    return parts[:rows] + (parts[rows:2 * rows] + parts[2 * rows:])


def diagonal(count):
    first = lax.broadcasted_iota(jnp.int32, (count, count), 0)
    return first == lax.broadcasted_iota(jnp.int32, (count, count), 1)


def to_column(row):
    count = row.shape[1]
    return jnp.sum(jnp.where(diagonal(count), jnp.broadcast_to(row, (count, count)), 0), axis=1, keepdims=True)


def to_row(column):
    count = column.shape[0]
    return jnp.sum(jnp.where(diagonal(count), jnp.broadcast_to(column, (count, count)), 0), axis=0, keepdims=True)


def dot(left, right):
    return jnp.sum(left * right, axis=1, keepdims=True)


def flat(tree):
    tree = {name: held for name, held in tree.items() if not isinstance(held, list) or held}
    names = [(name, len(held) if isinstance(held, list) else 0) for name, held in tree.items()]
    entries = []
    for held in tree.values():
        entries += held if isinstance(held, list) else [held]
    return names, entries


def named(names, entries):
    space, at = SimpleNamespace(), 0
    for name, count in names:
        setattr(space, name, list(entries[at:at + count]) if count else entries[at])
        at += max(count, 1)
    return space


def stage(name, body, ins, outs, cost=None):
    in_names, arrays = flat(ins)
    out_names, kinds = flat(outs)

    def kernel(*refs):
        body(named(in_names, refs[:len(arrays)]), named(out_names, refs[len(arrays):]))

    whole = pl.BlockSpec(memory_space=pltpu.VMEM)
    made = pl.pallas_call(
        kernel,
        name=name,
        out_shape=[jax.ShapeDtypeStruct(*kind) for kind in kinds],
        in_specs=[whole] * len(arrays),
        out_specs=[whole] * len(kinds),
        compiler_params=pltpu.CompilerParams(vmem_limit_bytes=STAGE_BYTES),
        cost_estimate=cost,
    )(*arrays)
    return named(out_names, made)


def swaps(total):
    sets = []
    for by in (1, CYCLE):
        for parity in (0, 1):
            ahead = [i for i in range(total - by) if (i // by) % 2 == parity]
            sets.append((by, parity, [(i, i + by) for i in ahead] + [(i + by, i) for i in ahead]))
    return sets


def rounds_of(total):
    bits = [1 << i for i in reversed(range(total.bit_length() - 1)) if 1 << i != CYCLE]
    assert total == 1 << (len(bits) + 1)
    rounds = [[CYCLE]]
    if len(bits) % 2:
        rounds.append([bits.pop(0)])
    middle = len(bits) // 2
    for far, near in zip(bits[:middle], bits[middle:]):
        rounds.append([near + far, far, near])
    places = [0]
    for distances in rounds:
        places = [place ^ far for far in [0] + distances for place in places]
    return rounds, places


def local(stiffness, neumann_inv, coarse_basis, coarse_inv, loads, face_index, face_len):
    total = lax.axis_size(AXIS)
    _, cases, ndof = loads.shape
    primal = coarse_basis.shape[1]
    width = face_index.shape[2]
    known = coarse_inv.shape[1]
    half = primal // 2
    lines_a_block = half + 1
    reps = known // width
    rounds, places = rounds_of(total)

    chosen = []
    for by, parity, pairs in swaps(total):
        if pairs:
            behind, ahead = (0, 1) if by == 1 else (2, 3)
            chosen.append((pairs, behind, ahead, by, parity))
    blocks = len(chosen)
    paired = [at for at, block in enumerate(chosen) if block[3:] == (CYCLE, 0)][0]
    slots = blocks * width
    own_rows = (blocks + 1) * primal

    vec = ((cases, ndof), F32)
    faces = ((cases, slots), F32)
    pair = ((1, 2 * cases), F32)
    faces_kind = ((cases, width), F32)
    extra_rows = [lines_a_block if at == paired else LONGER if block[3:] == (1, 1) else 0 for at, block in enumerate(chosen)]
    solve_kinds = [((cases + extra, width), F32) for extra in extra_rows]

    def longer(kind):
        rows, lanes = kind[0]
        return [((rows + (8 if at == paired else 0), lanes), F32) for at in range(blocks)]

    blocked = [slice(i * width, (i + 1) * width) for i in range(blocks)]
    strips = [slice(i * ndof // TILES, (i + 1) * ndof // TILES) for i in range(TILES)]

    def joined(refs):
        return jnp.concatenate([ref[:cases] for ref in refs], axis=1)

    def put_faces(refs, value):
        rows = value.shape[0]
        for i, ref in enumerate(refs):
            ref[:rows] = value[:, blocked[i]]
            if ref.shape[0] > rows:
                ref[rows:] = jnp.zeros((ref.shape[0] - rows, width), F32)

    def exchange(arrays):
        return [lax.ppermute(array, AXIS, chosen[i][0]) for i, array in enumerate(arrays)]

    def gather(own, got, lines, beside=()):
        pieces, start = [own, got], cases
        for at, distances in enumerate(rounds[1:]):
            def join(i, o):
                o.block[...] = jnp.concatenate([ref[start:start + lines] for ref in i.pieces], axis=0)

            block = stage("join", join, dict(pieces=pieces, beside=beside[at] if at < len(beside) else []), dict(block=((lines * len(pieces), 2 * cases), F32))).block
            pieces = [block] + [lax.ppermute(block, AXIS, [(i, i ^ far) for i in range(total)]) for far in distances]
            start, lines = 0, block.shape[0]
        return pieces

    def both_sums(pieces, stride):
        rows = []
        for piece in pieces:
            count = piece.shape[0] // stride
            rows += [piece[i * stride + stride - 1:(i + 1) * stride] for i in range(count)]
        while len(rows) > 1:
            rows = [rows[i] + rows[i + 1] for i in range(0, len(rows), 2)]
        return rows[0]

    def as_columns(row):
        return to_column(row[:, :cases]), to_column(row[:, cases:])

    def first(i, o):
        me = lax.axis_index(AXIS)
        index, lengths = i.index[0], i.lengths[...]
        lane = lax.broadcasted_iota(jnp.int32, (1, width), 1)
        rows = []
        for _, behind, ahead, by, parity in chosen:
            forward = (me // by) % 2 == parity
            row = jnp.where(forward, index[ahead:ahead + 1], index[behind:behind + 1])
            length = jnp.where(forward, lengths[:, ahead:ahead + 1], lengths[:, behind:behind + 1])
            rows.append(jnp.where(lane < length, row, -1))
        row = jnp.concatenate(rows, axis=1)
        unpicker = (lax.broadcasted_iota(jnp.int32, (ndof, slots), 0) == row).astype(F32).astype(BF)
        picker = (lax.broadcasted_iota(jnp.int32, (slots, ndof), 1) == to_column(row)).astype(F32)
        weight = 1.0 / (1.0 + jnp.sum(picker, axis=0, keepdims=True))
        weighted = i.basis[0] * weight
        at_slots = pick(jnp.concatenate([i.load[0], weighted], axis=0), unpicker)
        inv = i.inv[...]
        inv_packed = jnp.concatenate([inv[:, j * width:(j + 1) * width] for j in range(reps)], axis=0)
        put_faces(o.face, jnp.concatenate([at_slots, jnp.concatenate([inv_packed] * blocks, axis=1)], axis=0))
        o.picker[...] = picker.astype(BF)
        o.unpicker[...] = unpicker
        o.weight[...] = weight
        o.weighted[...] = weighted
        o.basis_slots[...] = at_slots[cases:]

    def lead(i, o):
        o.ready[...] = jnp.zeros((8, width), F32)

    packed = ((cases + primal + reps * primal, width), F32)
    ready = stage("lead", lead, dict(), dict(ready=((8, width), F32)), cost=ROOM_FOR_COPIES).ready
    start = stage(
        "first", first,
        dict(ready=ready, lengths=face_len, index=face_index, basis=coarse_basis, load=loads, inv=coarse_inv),
        dict(face=longer(packed), picker=((slots, ndof), BF), unpicker=((ndof, slots), BF), weight=((1, ndof), F32),
             weighted=((primal, ndof), F32), basis_slots=((primal, slots), F32)),
        cost=ROOM_FOR_COPIES)
    weight, picker, unpicker = start.weight, start.picker, start.unpicker
    came = exchange(start.face)

    part_kinds = [((ndof, ndof), BF)] * 2 + [((slots, ndof), BF)] * 2 + [((slots, slots), BF)] * 2

    def prepare(name, matrix):
        def body(i, o):
            for strip in strips:
                o.parts[0][strip], o.parts[1][strip] = split(i.matrix[0, strip])
            for at in range(2):
                face = contract(i.picker[...], o.parts[at][...]).astype(BF)
                o.parts[2 + at][...] = face
                o.parts[4 + at][...] = contract(face, i.unpicker[...]).astype(BF)

        return stage(name, body, dict(matrix=matrix, picker=picker, unpicker=unpicker), dict(parts=part_kinds)).parts

    inv = prepare("prepare_inv", neumann_inv)
    stiff = prepare("prepare_stiff", stiffness)

    own_kinds = dict(lines=((primal, cases), F32), inner_faces=faces, inner=vec)

    def solve_own(part, i, o):
        scaled = part * i.weight[...]
        o.lines[...] = product(i.weighted[...], part, NT)
        o.inner_faces[...] = times(scaled, i.inv[2][...], i.inv[3][...], NT)
        o.inner[...] = times(scaled, i.inv[0][...], i.inv[1][...])

    def loads_faces(i, o):
        o.lines[...] = product(i.weighted[...], i.load[0], NT)
        o.inner_faces[...] = times(i.load[0] * i.weight[...], i.inv[0][...], i.inv[1][...], NT)

    def loads_inner(i, o):
        o.inner[...] = times(i.load[0] * i.weight[...], i.inv[0][...], i.inv[1][...])

    own = stage("loads_faces", loads_faces, dict(load=loads, weight=weight, weighted=start.weighted, inv=inv[2:4]),
                dict(lines=own_kinds["lines"], inner_faces=faces))
    own.inner = stage("loads_inner", loads_inner, dict(load=loads, weight=weight, inv=inv[:2]), dict(inner=vec)).inner

    def reach(i, o):
        functions, rows = [i.weighted[...]], [i.inv[...]]
        for j in range(blocks):
            part = i.came[j][...]
            functions.append(pick(part[cases:cases + primal], i.picker[blocked[j]]))
            rest = part[cases + primal:]
            rows.append(jnp.concatenate([rest[k * primal:(k + 1) * primal] for k in range(reps)], axis=1))
        functions = jnp.concatenate(functions, axis=0)
        rows = jnp.concatenate(rows, axis=0)
        image = times(functions, i.stiff[0][...], i.stiff[1][...])
        image_faces = times(functions, i.stiff[2][...], i.stiff[3][...], NT)
        o.reach[0][...], o.reach[1][...] = split(jnp.concatenate([functions, image], axis=1))
        o.reach_faces[0][...], o.reach_faces[1][...] = split(image_faces)
        me = lax.axis_index(AXIS)
        count = i.place.shape[1]
        for upper in range(2):
            for at in range(0, count, 256):
                lanes = slice(at, min(at + 256, count))
                device, line = i.place[:, lanes] ^ me, i.line[:, lanes]
                source = jnp.where(line < half, device * primal + upper * half + line, -1)
                move = lax.broadcasted_iota(jnp.int32, (known, lanes.stop - at), 0) == source
                o.rows[upper * own_rows:(upper + 1) * own_rows, lanes] = pick(rows, move.astype(F32).astype(BF))

    place = jnp.asarray(np.repeat(np.array(places, np.int32), lines_a_block)[None])
    line = jnp.asarray(np.tile(np.arange(lines_a_block, dtype=np.int32), total)[None])
    reached = stage(
        "reach", reach,
        dict(weighted=start.weighted, inv=coarse_inv, came=came, picker=picker, stiff=stiff[:4], place=place, line=line),
        dict(reach=[((own_rows, 2 * ndof), BF)] * 2, reach_faces=[((own_rows, slots), BF)] * 2, rows=((2 * own_rows, total * lines_a_block), F32)))

    def to_solve(came, own, coef=None, sums=None):
        def body(i, o):
            arrived = joined(i.came)
            if coef is not None:
                arrived = to_column(i.coef[:, cases:]) * -arrived
            lines = i.lines[...] + product(i.basis_slots[...], arrived, NT)
            put_faces(o.face, 0.5 * (i.inner_faces[...] + times(0.5 * arrived, i.inv[0][...], i.inv[1][...])))
            o.face[paired][cases:cases + half] = jnp.concatenate([lines[:half], lines[half:]], axis=1)
            o.face[paired][cases + half:] = i.sums[...] if sums is not None else jnp.zeros((1, 2 * cases), F32)

        ins = dict(came=came, basis_slots=start.basis_slots, lines=own.lines, inner_faces=own.inner_faces, inv=inv[4:])
        if coef is not None:
            ins.update(coef=coef)
        if sums is not None:
            ins.update(sums=sums)
        made = stage("solve_rest", body, ins, dict(face=solve_kinds))
        return made.face[paired], exchange(made.face)

    def to_apply(step, came, own, state, coef):
        def body(i, o):
            arrived = joined(i.came)
            if step == 0:
                o.residual[...] = i.load[0] + pick(arrived, i.picker[...])
            else:
                if step > 1:
                    o.z[...] = i.z_part[...] + pick(arrived, i.picker[...])
                    arrived = to_column(i.coef[:, cases:]) * -arrived
                o.w[...] = i.w_part[...] + pick(arrived, i.picker[...])
            inner = i.weight[...] * (i.inner[...] + times(0.5 * arrived, i.inv[0][...], i.inv[1][...]))
            o.v[...] = inner
            image = times(inner, i.stiff[0][...], i.stiff[1][...])
            o.image[...] = image
            o.image_faces[...] = pick(image, i.unpicker[...])

        ins = dict(came=came, picker=picker, unpicker=unpicker, weight=weight, inner=own.inner, inv=inv[2:4], stiff=stiff[:2])
        outs = dict(v=vec, image_faces=faces, image=vec)
        if step == 0:
            ins.update(load=loads)
            outs.update(residual=vec)
        else:
            ins.update(w_part=state.w_part)
            outs.update(w=vec)
        if step > 1:
            ins.update(z_part=state.z_part, coef=coef)
            outs.update(z=vec)
        return stage("apply_own", body, ins, outs)

    def corrected(i):
        rows = jnp.concatenate([ref[...] for ref in i.everyone], axis=0)
        halves = product(i.rows[...], rows)
        factors = (halves[:own_rows, :cases] + halves[own_rows:, cases:]).T
        at_slots = i.image_faces[...] + times(joined(i.came), i.stiff_block[0][...], i.stiff_block[1][...])
        both = both_sums([ref[...] for ref in i.everyone], lines_a_block)
        return at_slots + times(factors, i.reach_faces[0][...], i.reach_faces[1][...]), factors, both

    def recur(i, o, step, factors, both):
        arrived = joined(i.came)
        extra = times(factors, i.reach[0][...], i.reach[1][...])
        inner = i.v[...] + pick(arrived, i.picker[...]) + extra[:, :ndof]
        image = i.image[...] + times(arrived, i.stiff[0][...], i.stiff[1][...]) + extra[:, ndof:]
        weight = i.weight[...]
        if step == 0:
            part, u, residual = image, inner, i.residual[...]
            delta = dot(image, u)
        else:
            gamma, delta = as_columns(both)
            w = i.w[...]
            if step == 1:
                alpha = gamma / delta
                q, s, p = inner, w, i.u[...]
                x = alpha * p
                before = w
            else:
                gamma_old, alpha_old = as_columns(i.coef[...])
                beta = gamma / gamma_old
                alpha = gamma / (delta - beta * gamma / alpha_old)
                q = inner + beta * i.q[...]
                s = w + beta * i.s[...]
                p = i.u[...] + beta * i.p[...]
                x = i.x[...] + alpha * p
                before = w - (alpha * beta) * i.z[...]
            residual = i.residual[...] - alpha * s
            u = i.u[...] - alpha * q
            part = before - alpha * image
            delta = dot(weight * before - alpha * image, u)
            o.coef[...] = jnp.concatenate([both[:, :cases], to_row(alpha)], axis=1)
            o.s[...], o.p[...], o.x[...], o.residual[...] = s, p, x, residual
            if step + 1 < ITERS:
                o.q[...] = q
                o.z_part[...] = image if step == 1 else image + beta * i.z[...]
        o.u[...] = u
        o.w_part[...] = part
        return part, jnp.concatenate([to_row(dot(weight * residual, u)), to_row(delta)], axis=1)

    state = SimpleNamespace()
    came_image, coef, sums = came, None, None
    for step in range(ITERS):
        final = step + 1 == ITERS
        sent, came_solve = to_solve(came_image, own, coef, sums)
        applied = to_apply(step, came_image, own, state, coef)
        vars(state).update(vars(applied))
        everyone = gather(sent, came_solve[paired], lines_a_block, ([stiff[4]], [reached.rows, own.inner]) if step == 0 else ())
        rest_ins = dict(everyone=everyone, rows=reached.rows, reach_faces=reached.reach_faces, came=came_solve, stiff_block=stiff[4:],
                        image_faces=state.image_faces)
        ins = dict(came=came_solve, picker=picker, stiff=stiff[2:4], weight=weight, residual=state.residual, reach=reached.reach,
                   v=state.v, image=state.image)
        outs = dict(u=vec, w_part=vec)
        if step > 0:
            ins.update(w=state.w, u=state.u)
            outs.update(coef=pair, s=vec, p=vec, x=vec, residual=vec)
            if not final:
                outs.update(q=vec, z_part=vec)
        if step > 1:
            ins.update(coef=coef, q=state.q, s=state.s, p=state.p, x=state.x, z=state.z)
        if final:
            def last(i, o):
                at_slots, factors, both = corrected(i)
                put_faces(o.face, at_slots)
                o.face[paired][cases:] = jnp.broadcast_to(recur(i, o, step, factors, both)[1], (8, 2 * cases))

            ins.update(rest_ins)
            outs.update(face=longer(faces_kind))
            made = stage("last", last, ins, outs)
            vars(state).update(vars(made))
            came_image = exchange(made.face)
            break

        def apply_rest(i, o):
            at_slots, o.factors[...], o.sums[...] = corrected(i)
            put_faces(o.face, at_slots)

        made = stage("apply_rest", apply_rest, rest_ins, dict(face=longer(faces_kind), factors=((cases, own_rows), F32), sums=pair))
        came_image = exchange(made.face)

        def update(i, o, step=step):
            part, o.sums[...] = recur(i, o, step, i.factors[...], i.both[...])
            solve_own(part, i, o)

        ins.update(factors=made.factors, both=made.sums, weighted=start.weighted, inv=inv[:4])
        outs.update(own_kinds, sums=pair)
        own = stage("update", update, ins, outs)
        vars(state).update(vars(own))
        sums = own.sums
        if step > 0:
            coef = own.coef

    def settle(i, o):
        alpha_old = as_columns(i.coef[...])[1]
        o.w[...] = i.w_part[...] - alpha_old * pick(joined(i.came), i.picker[...])

    def finish(i, o):
        gamma_old, alpha_old = as_columns(i.coef[...])
        gamma, delta = as_columns(both_sums([ref[...] for ref in i.everyone], 1))
        beta = gamma / gamma_old
        alpha = gamma / (delta - beta * gamma / alpha_old)
        o.solution[0] = i.x[...] + alpha * (i.u[...] + beta * i.p[...])
        o.remainder[0] = i.residual[...] - alpha * (i.w[...] + beta * i.s[...])

    whole = ((1, cases, ndof), F32)
    everyone = gather(state.face[paired], came_image[paired], 1)
    w = stage("settle", settle, dict(came=came_image, picker=picker, coef=state.coef, w_part=state.w_part), dict(w=vec)).w
    done = stage(
        "finish", finish,
        dict(everyone=everyone, coef=state.coef, w=w, x=state.x, u=state.u, p=state.p, residual=state.residual, s=state.s),
        dict(solution=whole, remainder=whole))
    return done.solution, done.remainder


def solution(mesh):
    placed = (
        P(AXIS, None, None),
        P(AXIS, None, None),
        P(AXIS, None, None),
        P(AXIS, None),
        P(AXIS, None, None),
        P(AXIS, None, None),
        P(AXIS, None),
    )
    return jax.shard_map(
        local,
        mesh=mesh,
        in_specs=placed,
        out_specs=(P(AXIS, None, None), P(AXIS, None, None)),
        check_vma=False,
    )
```

```python
from types import SimpleNamespace

import jax
import jax.numpy as jnp
import numpy as np
from jax import lax
from jax.experimental import pallas as pl
from jax.experimental.pallas import tpu as pltpu
from jax.sharding import PartitionSpec as P

CYCLE = 16
ITERS = 4

BF = jnp.bfloat16
F32 = jnp.float32
NN = ((1,), (0,))
NT = ((1,), (1,))
STAGE_BYTES = 12 * 1024 * 1024
TILES = 8
AXIS = "sub"
LONGER = 32
ROOM_FOR_COPIES = pl.CostEstimate(flops=4 * 10**9, bytes_accessed=16 * 10**6, transcendentals=0)


def contract(left, right, dims=NN):
    return lax.dot_general(left, right, (dims, ((), ())), preferred_element_type=F32)


def split(value):
    high = value.astype(BF)
    return high, (value - high.astype(F32)).astype(BF)


def in_three(value):
    top, rest = split(value)
    return top, rest, (value - top.astype(F32) - rest.astype(F32)).astype(BF)


def times(value, high, low, dims=NN, lowest=None):
    rows = value.shape[0]
    top, rest, last = in_three(value)
    first = contract(jnp.concatenate([top, rest, last], axis=0), high, dims)
    second = contract(jnp.concatenate([top, rest], axis=0), low, dims)
    small = first[2 * rows:] + second[rows:]
    if lowest is not None:
        small += contract(top, lowest, dims)
    return first[:rows] + (first[rows:2 * rows] + second[:rows] + small)


def product(left, right, dims=NN):
    high, low, lowest = in_three(right)
    return times(left, high, low, dims, lowest)


def pick(value, onehot, dims=NN):
    rows = value.shape[0]
    parts = contract(jnp.concatenate(in_three(value), axis=0), onehot, dims)
    return parts[:rows] + (parts[rows:2 * rows] + parts[2 * rows:])


def diagonal(count):
    first = lax.broadcasted_iota(jnp.int32, (count, count), 0)
    return first == lax.broadcasted_iota(jnp.int32, (count, count), 1)


def to_column(row):
    count = row.shape[1]
    return jnp.sum(jnp.where(diagonal(count), jnp.broadcast_to(row, (count, count)), 0), axis=1, keepdims=True)


def to_row(column):
    count = column.shape[0]
    return jnp.sum(jnp.where(diagonal(count), jnp.broadcast_to(column, (count, count)), 0), axis=0, keepdims=True)


def dot(left, right):
    return jnp.sum(left * right, axis=1, keepdims=True)


def flat(tree):
    tree = {name: held for name, held in tree.items() if not isinstance(held, list) or held}
    names = [(name, len(held) if isinstance(held, list) else 0) for name, held in tree.items()]
    entries = []
    for held in tree.values():
        entries += held if isinstance(held, list) else [held]
    return names, entries


def named(names, entries):
    space, at = SimpleNamespace(), 0
    for name, count in names:
        setattr(space, name, list(entries[at:at + count]) if count else entries[at])
        at += max(count, 1)
    return space


def stage(name, body, ins, outs, cost=None):
    in_names, arrays = flat(ins)
    out_names, kinds = flat(outs)

    def kernel(*refs):
        body(named(in_names, refs[:len(arrays)]), named(out_names, refs[len(arrays):]))

    whole = pl.BlockSpec(memory_space=pltpu.VMEM)
    made = pl.pallas_call(
        kernel,
        name=name,
        out_shape=[jax.ShapeDtypeStruct(*kind) for kind in kinds],
        in_specs=[whole] * len(arrays),
        out_specs=[whole] * len(kinds),
        compiler_params=pltpu.CompilerParams(vmem_limit_bytes=STAGE_BYTES),
        cost_estimate=cost,
    )(*arrays)
    return named(out_names, made)


def swaps(total):
    sets = []
    for by in (1, CYCLE):
        for parity in (0, 1):
            ahead = [i for i in range(total - by) if (i // by) % 2 == parity]
            sets.append((by, parity, [(i, i + by) for i in ahead] + [(i + by, i) for i in ahead]))
    return sets


def rounds_of(total):
    bits = [1 << i for i in reversed(range(total.bit_length() - 1)) if 1 << i != CYCLE]
    assert total == 1 << (len(bits) + 1)
    rounds = [[CYCLE]]
    if len(bits) % 2:
        rounds.append([bits.pop(0)])
    middle = len(bits) // 2
    for far, near in zip(bits[:middle], bits[middle:]):
        rounds.append([near + far, far, near])
    places = [0]
    for distances in rounds:
        places = [place ^ far for far in [0] + distances for place in places]
    return rounds, places


def local(stiffness, neumann_inv, coarse_basis, coarse_inv, loads, face_index, face_len):
    total = lax.axis_size(AXIS)
    _, cases, ndof = loads.shape
    primal = coarse_basis.shape[1]
    width = face_index.shape[2]
    known = coarse_inv.shape[1]
    half = primal // 2
    lines_a_block = half + 1
    reps = known // width
    rounds, places = rounds_of(total)

    chosen = []
    for by, parity, pairs in swaps(total):
        if pairs:
            behind, ahead = (0, 1) if by == 1 else (2, 3)
            chosen.append((pairs, behind, ahead, by, parity))
    blocks = len(chosen)
    paired = [at for at, block in enumerate(chosen) if block[3:] == (CYCLE, 0)][0]
    slots = blocks * width
    own_rows = (blocks + 1) * primal

    vec = ((cases, ndof), F32)
    faces = ((cases, slots), F32)
    pair = ((1, 2 * cases), F32)
    faces_kind = ((cases, width), F32)
    extra_rows = [lines_a_block if at == paired else LONGER if block[3:] == (1, 1) else 0 for at, block in enumerate(chosen)]
    solve_kinds = [((cases + extra, width), F32) for extra in extra_rows]

    def longer(kind):
        rows, lanes = kind[0]
        return [((rows + (8 if at == paired else 0), lanes), F32) for at in range(blocks)]

    blocked = [slice(i * width, (i + 1) * width) for i in range(blocks)]
    strips = [slice(i * ndof // TILES, (i + 1) * ndof // TILES) for i in range(TILES)]

    def joined(refs):
        return jnp.concatenate([ref[:cases] for ref in refs], axis=1)

    def put_faces(refs, value):
        rows = value.shape[0]
        for i, ref in enumerate(refs):
            ref[:rows] = value[:, blocked[i]]
            if ref.shape[0] > rows:
                ref[rows:] = jnp.zeros((ref.shape[0] - rows, width), F32)

    def exchange(arrays):
        return [lax.ppermute(array, AXIS, chosen[i][0]) for i, array in enumerate(arrays)]

    def gather(own, got, lines, beside=()):
        pieces, start = [own, got], cases
        for at, distances in enumerate(rounds[1:]):
            def join(i, o):
                o.block[...] = jnp.concatenate([ref[start:start + lines] for ref in i.pieces], axis=0)

            block = stage("join", join, dict(pieces=pieces, beside=beside[at] if at < len(beside) else []), dict(block=((lines * len(pieces), 2 * cases), F32))).block
            pieces = [block] + [lax.ppermute(block, AXIS, [(i, i ^ far) for i in range(total)]) for far in distances]
            start, lines = 0, block.shape[0]
        return pieces

    def both_sums(pieces, stride):
        rows = []
        for piece in pieces:
            count = piece.shape[0] // stride
            rows += [piece[i * stride + stride - 1:(i + 1) * stride] for i in range(count)]
        while len(rows) > 1:
            rows = [rows[i] + rows[i + 1] for i in range(0, len(rows), 2)]
        return rows[0]

    def as_columns(row):
        return to_column(row[:, :cases]), to_column(row[:, cases:])

    def first(i, o):
        me = lax.axis_index(AXIS)
        index, lengths = i.index[0], i.lengths[...]
        lane = lax.broadcasted_iota(jnp.int32, (1, width), 1)
        rows = []
        for _, behind, ahead, by, parity in chosen:
            forward = (me // by) % 2 == parity
            row = jnp.where(forward, index[ahead:ahead + 1], index[behind:behind + 1])
            length = jnp.where(forward, lengths[:, ahead:ahead + 1], lengths[:, behind:behind + 1])
            rows.append(jnp.where(lane < length, row, -1))
        row = jnp.concatenate(rows, axis=1)
        unpicker = (lax.broadcasted_iota(jnp.int32, (ndof, slots), 0) == row).astype(F32).astype(BF)
        picker = (lax.broadcasted_iota(jnp.int32, (slots, ndof), 1) == to_column(row)).astype(F32)
        weight = 1.0 / (1.0 + jnp.sum(picker, axis=0, keepdims=True))
        weighted = i.basis[0] * weight
        at_slots = pick(jnp.concatenate([i.load[0], weighted], axis=0), unpicker)
        inv = i.inv[...]
        inv_packed = jnp.concatenate([inv[:, j * width:(j + 1) * width] for j in range(reps)], axis=0)
        put_faces(o.face, jnp.concatenate([at_slots, jnp.concatenate([inv_packed] * blocks, axis=1)], axis=0))
        o.picker[...] = picker.astype(BF)
        o.unpicker[...] = unpicker
        o.weight[...] = weight
        o.weighted[...] = weighted
        o.basis_slots[...] = at_slots[cases:]

    def lead(i, o):
        o.ready[...] = jnp.zeros((8, width), F32)

    packed = ((cases + primal + reps * primal, width), F32)
    ready = stage("lead", lead, dict(), dict(ready=((8, width), F32)), cost=ROOM_FOR_COPIES).ready
    start = stage(
        "first", first,
        dict(ready=ready, lengths=face_len, index=face_index, basis=coarse_basis, load=loads, inv=coarse_inv),
        dict(face=longer(packed), picker=((slots, ndof), BF), unpicker=((ndof, slots), BF), weight=((1, ndof), F32),
             weighted=((primal, ndof), F32), basis_slots=((primal, slots), F32)),
        cost=ROOM_FOR_COPIES)
    weight, picker, unpicker = start.weight, start.picker, start.unpicker
    came = exchange(start.face)

    part_kinds = [((ndof, ndof), BF)] * 2 + [((slots, ndof), BF)] * 2 + [((slots, slots), BF)] * 2

    def prepare(name, matrix):
        def body(i, o):
            for strip in strips:
                o.parts[0][strip], o.parts[1][strip] = split(i.matrix[0, strip])
            for at in range(2):
                face = contract(i.picker[...], o.parts[at][...]).astype(BF)
                o.parts[2 + at][...] = face
                o.parts[4 + at][...] = contract(face, i.unpicker[...]).astype(BF)

        return stage(name, body, dict(matrix=matrix, picker=picker, unpicker=unpicker), dict(parts=part_kinds)).parts

    inv = prepare("prepare_inv", neumann_inv)
    stiff = prepare("prepare_stiff", stiffness)

    own_kinds = dict(lines=((primal, cases), F32), inner_faces=faces, inner=vec)

    def solve_own(part, i, o):
        scaled = part * i.weight[...]
        o.lines[...] = product(i.weighted[...], part, NT)
        o.inner_faces[...] = times(scaled, i.inv[2][...], i.inv[3][...], NT)
        o.inner[...] = times(scaled, i.inv[0][...], i.inv[1][...])

    def loads_faces(i, o):
        o.lines[...] = product(i.weighted[...], i.load[0], NT)
        o.inner_faces[...] = times(i.load[0] * i.weight[...], i.inv[0][...], i.inv[1][...], NT)

    def loads_inner(i, o):
        o.inner[...] = times(i.load[0] * i.weight[...], i.inv[0][...], i.inv[1][...])

    own = stage("loads_faces", loads_faces, dict(load=loads, weight=weight, weighted=start.weighted, inv=inv[2:4]),
                dict(lines=own_kinds["lines"], inner_faces=faces))
    own.inner = stage("loads_inner", loads_inner, dict(load=loads, weight=weight, inv=inv[:2]), dict(inner=vec)).inner

    def reach(i, o):
        functions, rows = [i.weighted[...]], [i.inv[...]]
        for j in range(blocks):
            part = i.came[j][...]
            functions.append(pick(part[cases:cases + primal], i.picker[blocked[j]]))
            rest = part[cases + primal:]
            rows.append(jnp.concatenate([rest[k * primal:(k + 1) * primal] for k in range(reps)], axis=1))
        functions = jnp.concatenate(functions, axis=0)
        rows = jnp.concatenate(rows, axis=0)
        image = times(functions, i.stiff[0][...], i.stiff[1][...])
        image_faces = times(functions, i.stiff[2][...], i.stiff[3][...], NT)
        o.reach[0][...], o.reach[1][...] = split(jnp.concatenate([functions, image], axis=1))
        o.reach_faces[0][...], o.reach_faces[1][...] = split(image_faces)
        me = lax.axis_index(AXIS)
        count = i.place.shape[1]
        for upper in range(2):
            for at in range(0, count, 256):
                lanes = slice(at, min(at + 256, count))
                device, line = i.place[:, lanes] ^ me, i.line[:, lanes]
                source = jnp.where(line < half, device * primal + upper * half + line, -1)
                move = lax.broadcasted_iota(jnp.int32, (known, lanes.stop - at), 0) == source
                o.rows[upper * own_rows:(upper + 1) * own_rows, lanes] = pick(rows, move.astype(F32).astype(BF))

    place = jnp.asarray(np.repeat(np.array(places, np.int32), lines_a_block)[None])
    line = jnp.asarray(np.tile(np.arange(lines_a_block, dtype=np.int32), total)[None])
    reached = stage(
        "reach", reach,
        dict(weighted=start.weighted, inv=coarse_inv, came=came, picker=picker, stiff=stiff[:4], place=place, line=line),
        dict(reach=[((own_rows, 2 * ndof), BF)] * 2, reach_faces=[((own_rows, slots), BF)] * 2, rows=((2 * own_rows, total * lines_a_block), F32)))

    def to_solve(came, own, coef=None, sums=None):
        def body(i, o):
            arrived = joined(i.came)
            if coef is not None:
                arrived = to_column(i.coef[:, cases:]) * -arrived
            lines = i.lines[...] + product(i.basis_slots[...], arrived, NT)
            put_faces(o.face, 0.5 * (i.inner_faces[...] + times(0.5 * arrived, i.inv[0][...], i.inv[1][...])))
            o.face[paired][cases:cases + half] = jnp.concatenate([lines[:half], lines[half:]], axis=1)
            o.face[paired][cases + half:] = i.sums[...] if sums is not None else jnp.zeros((1, 2 * cases), F32)

        ins = dict(came=came, basis_slots=start.basis_slots, lines=own.lines, inner_faces=own.inner_faces, inv=inv[4:])
        if coef is not None:
            ins.update(coef=coef)
        if sums is not None:
            ins.update(sums=sums)
        made = stage("solve_rest", body, ins, dict(face=solve_kinds))
        return made.face[paired], exchange(made.face)

    def to_apply(step, came, own, state, coef):
        def body(i, o):
            arrived = joined(i.came)
            if step == 0:
                o.residual[...] = i.load[0] + pick(arrived, i.picker[...])
            else:
                if step > 1:
                    o.z[...] = i.z_part[...] + pick(arrived, i.picker[...])
                    arrived = to_column(i.coef[:, cases:]) * -arrived
                o.w[...] = i.w_part[...] + pick(arrived, i.picker[...])
            inner = i.weight[...] * (i.inner[...] + times(0.5 * arrived, i.inv[0][...], i.inv[1][...]))
            o.v[...] = inner
            image = times(inner, i.stiff[0][...], i.stiff[1][...])
            o.image[...] = image
            o.image_faces[...] = pick(image, i.unpicker[...])

        ins = dict(came=came, picker=picker, unpicker=unpicker, weight=weight, inner=own.inner, inv=inv[2:4], stiff=stiff[:2])
        outs = dict(v=vec, image_faces=faces, image=vec)
        if step == 0:
            ins.update(load=loads)
            outs.update(residual=vec)
        else:
            ins.update(w_part=state.w_part)
            outs.update(w=vec)
        if step > 1:
            ins.update(z_part=state.z_part, coef=coef)
            outs.update(z=vec)
        return stage("apply_own", body, ins, outs)

    def corrected(i):
        rows = jnp.concatenate([ref[...] for ref in i.everyone], axis=0)
        halves = product(i.rows[...], rows)
        factors = (halves[:own_rows, :cases] + halves[own_rows:, cases:]).T
        at_slots = i.image_faces[...] + times(joined(i.came), i.stiff_block[0][...], i.stiff_block[1][...])
        both = both_sums([ref[...] for ref in i.everyone], lines_a_block)
        return at_slots + times(factors, i.reach_faces[0][...], i.reach_faces[1][...]), factors, both

    def recur(i, o, step, factors, both):
        arrived = joined(i.came)
        extra = times(factors, i.reach[0][...], i.reach[1][...])
        inner = i.v[...] + pick(arrived, i.picker[...]) + extra[:, :ndof]
        image = i.image[...] + times(arrived, i.stiff[0][...], i.stiff[1][...]) + extra[:, ndof:]
        weight = i.weight[...]
        if step == 0:
            part, u, residual = image, inner, i.residual[...]
            delta = dot(image, u)
        else:
            gamma, delta = as_columns(both)
            w = i.w[...]
            if step == 1:
                alpha = gamma / delta
                q, s, p = inner, w, i.u[...]
                x = alpha * p
                before = w
            else:
                gamma_old, alpha_old = as_columns(i.coef[...])
                beta = gamma / gamma_old
                alpha = gamma / (delta - beta * gamma / alpha_old)
                q = inner + beta * i.q[...]
                s = w + beta * i.s[...]
                if step + 1 < ITERS:
                    p = i.u[...] + beta * i.p[...]
                    x = i.x[...] + alpha * p
                before = w - (alpha * beta) * i.z[...]
            residual = i.residual[...] - alpha * s
            u = i.u[...] - alpha * q
            part = before - alpha * image
            delta = dot(weight * before - alpha * image, u)
            o.coef[...] = jnp.concatenate([both[:, :cases], to_row(alpha)], axis=1)
            o.s[...], o.residual[...] = s, residual
            if step + 1 < ITERS:
                o.p[...], o.x[...] = p, x
                o.q[...] = q
                o.z_part[...] = image if step == 1 else image + beta * i.z[...]
        o.u[...] = u
        o.w_part[...] = part
        return part, jnp.concatenate([to_row(dot(weight * residual, u)), to_row(delta)], axis=1)

    state = SimpleNamespace()
    came_image, coef, sums = came, None, None
    for step in range(ITERS):
        final = step + 1 == ITERS
        sent, came_solve = to_solve(came_image, own, coef, sums)
        applied = to_apply(step, came_image, own, state, coef)
        vars(state).update(vars(applied))
        everyone = gather(sent, came_solve[paired], lines_a_block, ([stiff[4]], [reached.rows, own.inner]) if step == 0 else ())
        rest_ins = dict(everyone=everyone, rows=reached.rows, reach_faces=reached.reach_faces, came=came_solve, stiff_block=stiff[4:],
                        image_faces=state.image_faces)
        ins = dict(came=came_solve, picker=picker, stiff=stiff[2:4], weight=weight, residual=state.residual, reach=reached.reach,
                   v=state.v, image=state.image)
        outs = dict(u=vec, w_part=vec)
        if step > 0:
            ins.update(w=state.w, u=state.u)
            outs.update(coef=pair, s=vec, residual=vec)
            if not final:
                outs.update(p=vec, x=vec, q=vec, z_part=vec)
        if step > 1:
            ins.update(coef=coef, q=state.q, s=state.s, z=state.z)
            if not final:
                ins.update(p=state.p, x=state.x)
        if final:
            def last(i, o):
                at_slots, factors, both = corrected(i)
                put_faces(o.face, at_slots)
                o.face[paired][cases:] = jnp.broadcast_to(recur(i, o, step, factors, both)[1], (8, 2 * cases))

            ins.update(rest_ins)
            outs.update(face=longer(faces_kind))
            earlier = dict(u=state.u, p=state.p, x=state.x, coef_old=coef)
            made = stage("last", last, ins, outs)
            vars(state).update(vars(made))
            came_image = exchange(made.face)
            break

        def apply_rest(i, o):
            at_slots, o.factors[...], o.sums[...] = corrected(i)
            put_faces(o.face, at_slots)

        made = stage("apply_rest", apply_rest, rest_ins, dict(face=longer(faces_kind), factors=((cases, own_rows), F32), sums=pair))
        came_image = exchange(made.face)

        def update(i, o, step=step):
            part, o.sums[...] = recur(i, o, step, i.factors[...], i.both[...])
            solve_own(part, i, o)

        ins.update(factors=made.factors, both=made.sums, weighted=start.weighted, inv=inv[:4])
        outs.update(own_kinds, sums=pair)
        own = stage("update", update, ins, outs)
        vars(state).update(vars(own))
        sums = own.sums
        if step > 0:
            coef = own.coef

    def settle(i, o):
        gamma, alpha_old = as_columns(i.coef[...])
        p = i.u[...] + gamma / as_columns(i.coef_old[...])[0] * i.p[...]
        o.p[...] = p
        o.x[...] = i.x[...] + alpha_old * p
        o.w[...] = i.w_part[...] - alpha_old * pick(joined(i.came), i.picker[...])

    def finish(i, o):
        gamma_old, alpha_old = as_columns(i.coef[...])
        gamma, delta = as_columns(both_sums([ref[...] for ref in i.everyone], 1))
        beta = gamma / gamma_old
        alpha = gamma / (delta - beta * gamma / alpha_old)
        o.solution[0] = i.x[...] + alpha * (i.u[...] + beta * i.p[...])
        o.remainder[0] = i.residual[...] - alpha * (i.w[...] + beta * i.s[...])

    whole = ((1, cases, ndof), F32)
    everyone = gather(state.face[paired], came_image[paired], 1)
    ins = dict(came=came_image, picker=picker, coef=state.coef, w_part=state.w_part)
    settled = stage("settle", settle, ins | earlier, dict(w=vec, p=vec, x=vec))
    done = stage(
        "finish", finish,
        dict(everyone=everyone, coef=state.coef, w=settled.w, x=settled.x, u=state.u, p=settled.p, residual=state.residual, s=state.s),
        dict(solution=whole, remainder=whole))
    return done.solution, done.remainder


def solution(mesh):
    placed = (
        P(AXIS, None, None),
        P(AXIS, None, None),
        P(AXIS, None, None),
        P(AXIS, None),
        P(AXIS, None, None),
        P(AXIS, None, None),
        P(AXIS, None),
    )
    return jax.shard_map(
        local,
        mesh=mesh,
        in_specs=placed,
        out_specs=(P(AXIS, None, None), P(AXIS, None, None)),
        check_vma=False,
    )
```
